32 devices in a mesh: dp: 4 (over y, core), expert: 8 (over z, x).
Axes of the slice: x: 2, y: 2, z: 4, core: 2. Of those that a mesh axis runs over, the one named last changes fastest.
Arguments:
- tokens: bfloat16 [2, 8, 1024, 768], P(None, 'expert', 'dp'), may hold values from -6 to 6
- doc_lengths: int32 [2, 8, 4], P(None, 'expert'), may hold values from 1 to 1021, as said below
- routes: int32 [2, 8, 1024, 2], P(None, 'expert', 'dp'), may hold values from 0 to 7, as said below
- slots: int32 [2, 8, 1024, 2], P(None, 'expert', 'dp'), may hold values from -1 to 71, as said below
- w_qkv: bfloat16 [768, 2304], P(('dp', 'expert')), may hold values from -0.21875 to 0.21875
- w_out: bfloat16 [768, 768], P(('dp', 'expert')), may hold values from -1.75 to 1.75
- rel_bias: bfloat16 [1024, 12], replicated, may hold values from -4 to 4
- gain_attn: bfloat16 [768], P(('dp', 'expert')), may hold values from 0.5 to 1.5
- gain_ffn: bfloat16 [768], P(('dp', 'expert')), may hold values from 0.5 to 1.5
- w_router: bfloat16 [768, 8], P(('dp', 'expert')), may hold values from -0.15625 to 0.15625
- w_in: bfloat16 [8, 768, 3072], P('expert'), may hold values from -0.21875 to 0.21875
- w_back: bfloat16 [8, 3072, 768], P('expert'), may hold values from -0.109375 to 0.109375
- cotangent: bfloat16 [2, 8, 1024, 768], P(None, 'expert', 'dp'), may hold values from -6 to 6
Outputs:
- output: bfloat16 [2, 8, 1024, 768], P(None, 'expert', 'dp')
- token_grad: bfloat16 [2, 8, 1024, 768], P(None, 'expert', 'dp')
- grad_w_qkv: float32 [768, 2304], P(('dp', 'expert'))
- grad_w_out: float32 [768, 768], P(('dp', 'expert'))
- grad_rel_bias: float32 [1024, 12], replicated
- grad_gain_attn: float32 [768], P(('dp', 'expert'))
- grad_gain_ffn: float32 [768], P(('dp', 'expert'))
- grad_w_router: float32 [768, 8], P(('dp', 'expert'))
- grad_w_in: float32 [8, 768, 3072], P('expert', 'dp')
- grad_w_back: float32 [8, 3072, 768], P('expert', 'dp')
The draws below stay inside these ranges and needn't reach their ends.
Inputs may be any that keep to these rules, and one draw needn't show every extreme that they name: `routes`: the 2 experts of a token differ. Among the pairs of one device and micro-batch that go to one expert, the kept ones hold the slots 0 to their count minus one without repeats, at most 72 of them; -1 marks a dropped pair. In every draw, for each micro-batch and dp index, some expert keeps 72 pairs from every device. `doc_lengths`: the 4 lengths of a sequence are positive and sum to 1024.
All inputs are finite; a program needn't handle non-finite values.
Results may differ from the reference program's by a relative error of at most 0.013.
Values may be sent and summed in bfloat16 or wider, within the bound.
No kernel may reach another device: no remote copies, remote signals or barrier semaphores. Data moves between devices by JAX's collectives and lax.ppermute only.
A program may use at most 256 MiB of HBM per device.

```python
import jax
import jax.numpy as jnp
from jax import lax

D = 768
H = 12
HD = 64
FF = 3072
TOP = 2
WINDOW = 1024
DOCS = 4
MICRO = 2
TOK_MB = 256
SEQS = 8
LENGTH = 1024
EXPERTS = 8
CAP = 72
REACH = 3


def route_table(key):
    shard_count = LENGTH // TOK_MB
    pair_count = TOK_MB * TOP
    key_list = jax.random.split(key, 5)
    lead_shape = (MICRO, SEQS, shard_count, TOK_MB)
    favoured = jax.random.randint(key_list[0], (MICRO, 1, shard_count, 1), 0, EXPERTS)
    token_scores = jax.random.randint(key_list[1], lead_shape, 0, 1 << 16) * TOK_MB + jnp.arange(TOK_MB, dtype=jnp.int32)
    token_ranks = jnp.argsort(jnp.argsort(token_scores, axis=-1), axis=-1)
    others = (favoured + 1 + jax.random.randint(key_list[2], lead_shape, 0, EXPERTS - 1)) % EXPERTS
    first_choice = jnp.where(token_ranks < 2 * CAP, favoured, others)
    second_choice = (first_choice + 1 + jax.random.randint(key_list[3], lead_shape, 0, EXPERTS - 1)) % EXPERTS
    chosen = jnp.stack([first_choice, second_choice], axis=-1).reshape(MICRO, SEQS, shard_count, pair_count)
    pair_scores = jax.random.randint(key_list[4], chosen.shape, 0, 1 << 16) * pair_count + jnp.arange(pair_count, dtype=jnp.int32)
    priority = jnp.argsort(jnp.argsort(pair_scores, axis=-1), axis=-1)
    sort_order = jnp.argsort(chosen * pair_count + priority, axis=-1)
    sorted_experts = jnp.take_along_axis(chosen, sort_order, axis=-1)
    counts = jnp.sum((chosen[..., None] == jnp.arange(EXPERTS, dtype=jnp.int32)).astype(jnp.int32), axis=-2)
    starts = jnp.cumsum(counts, axis=-1) - counts
    sorted_ranks = jnp.arange(pair_count, dtype=jnp.int32) - jnp.take_along_axis(starts, sorted_experts, axis=-1)
    slot_ranks = jnp.take_along_axis(sorted_ranks, jnp.argsort(sort_order, axis=-1), axis=-1)
    slot_values = jnp.where(slot_ranks < CAP, slot_ranks, -1)
    return (chosen.reshape(MICRO, SEQS, LENGTH, TOP), slot_values.reshape(MICRO, SEQS, LENGTH, TOP))


def draw_routes(key, part):
    shared = route_table(key)
    return shared[0].astype(jnp.int32)


def draw_slots(key, part):
    shared = route_table(key)
    return shared[1].astype(jnp.int32)


def draw_doc_lengths(key, part):
    key = jax.random.fold_in(key, 11)
    key_list = jax.random.split(key, 5)
    spread = jax.random.randint(key_list[0], (MICRO, SEQS, DOCS - 1), 0, LENGTH - DOCS + 1)
    drawn_cuts = jnp.sort(spread, axis=-1) + jnp.arange(1, DOCS, dtype=jnp.int32)
    head_cut = jax.random.randint(key_list[1], (MICRO, SEQS, 1), 1, TOK_MB)
    tail_spread = jax.random.randint(key_list[2], (MICRO, SEQS, DOCS - 2), 0, TOK_MB - DOCS + 2)
    tail_cuts = jnp.sort(tail_spread, axis=-1) + jnp.arange(DOCS - 2, dtype=jnp.int32) + (LENGTH - TOK_MB + 1)
    spanning = jax.random.randint(key_list[3], (1, SEQS, 1), 0, MICRO)
    chosen_micro = jnp.arange(MICRO, dtype=jnp.int32)[:, None, None] == spanning
    cuts = jnp.where(chosen_micro, jnp.concatenate([head_cut, tail_cuts], axis=-1), drawn_cuts)
    extreme_seq = jax.random.randint(key_list[4], (1, 1, 1), 0, SEQS)
    extreme_mask = chosen_micro & (jnp.arange(SEQS, dtype=jnp.int32)[None, :, None] == extreme_seq)
    extreme_tail = jnp.arange(DOCS - 2, dtype=jnp.int32) + (LENGTH - DOCS + 2)
    extreme_cuts = jnp.concatenate([jnp.ones((MICRO, SEQS, 1), jnp.int32), jnp.broadcast_to(extreme_tail, (MICRO, SEQS, DOCS - 2))], axis=-1)
    cuts = jnp.where(extreme_mask, extreme_cuts, cuts)
    doc_ends = jnp.concatenate([cuts, jnp.full((MICRO, SEQS, 1), LENGTH, jnp.int32)], axis=-1)
    doc_starts = jnp.concatenate([jnp.zeros((MICRO, SEQS, 1), jnp.int32), cuts], axis=-1)
    return (doc_ends - doc_starts).astype(jnp.int32)


def block_levels(rng, dims, cuts, low, high):
    loudness = 1.0
    for dim, blocks in cuts:
        steps = jax.random.uniform(jax.random.fold_in(jax.random.fold_in(rng, 6), dim), (blocks,), jnp.float32, low / len(cuts), high / len(cuts))
        loudness = loudness * jnp.repeat(jnp.exp(steps), dims[dim] // blocks).reshape((-1,) + (1,) * (len(dims) - 1 - dim))
    return loudness


def centred(stream_key, shape, scale, reach, pieces=(), kind=jnp.bfloat16):
    level = block_levels(stream_key, shape, pieces, -0.22, 0.18) if pieces else 1.0
    entries = jax.random.normal(stream_key, shape, jnp.float32) * scale * level
    return jnp.minimum(jnp.maximum(entries, -reach), reach).astype(kind)


def setup_inputs(seed: int = 0) -> dict:
    keys = jax.random.split(jax.random.key(seed), 14)
    tokens = centred(keys[0], (MICRO, SEQS, LENGTH, D), 1.0, 6.0, ((1, 8), (2, 4)))
    doc_lengths = draw_doc_lengths(jax.random.fold_in(keys[13], 71), 0)
    routes = draw_routes(jax.random.fold_in(keys[13], 71), 0)
    slots = draw_slots(jax.random.fold_in(keys[13], 71), 0)
    w_qkv = centred(keys[4], (D, 3 * D), D ** -0.5, 0.21875, ((0, 32),))
    w_out = centred(keys[5], (D, D), (D // 64) ** -0.5, 1.75, ((0, 32),))
    rel_bias = centred(keys[6], (WINDOW, H), 1.0, 4.0)
    gain_attn = jnp.clip(1.0 + 0.1 * jax.random.normal(keys[7], (D,), jnp.float32), 0.5, 1.5).astype(jnp.bfloat16)
    gain_ffn = jnp.clip(1.0 + 0.1 * jax.random.normal(keys[8], (D,), jnp.float32), 0.5, 1.5).astype(jnp.bfloat16)
    w_router = centred(keys[9], (D, EXPERTS), (2 * D) ** -0.5, 0.15625, ((0, 32),))
    w_in = centred(keys[10], (EXPERTS, D, FF), D ** -0.5, 0.21875, ((0, 8),))
    w_back = centred(keys[11], (EXPERTS, FF, D), FF ** -0.5, 0.109375, ((0, 8),))
    cotangent = centred(keys[12], (MICRO, SEQS, LENGTH, D), 1.0, 6.0, ((1, 8), (2, 4)))
    return {"tokens": tokens, "doc_lengths": doc_lengths, "routes": routes, "slots": slots, "w_qkv": w_qkv, "w_out": w_out, "rel_bias": rel_bias, "gain_attn": gain_attn, "gain_ffn": gain_ffn, "w_router": w_router, "w_in": w_in, "w_back": w_back, "cotangent": cotangent}


EPSILON = 1e-06
HIGHEST = lax.Precision.HIGHEST
MASKED = -1e+30

@jax.custom_vjp
def low(v):
    return lax.optimization_barrier(v.astype(jnp.bfloat16)).astype(jnp.float32)

@jax.custom_vjp
def low_back(v):
    return v

def low_keep(v):
    return (low(v), None)

def low_pass(kept, grad):
    return (grad,)

def back_keep(v):
    return (v, None)

def back_low(kept, grad):
    return (low(grad),)
low.defvjp(low_keep, low_pass)
low_back.defvjp(back_keep, back_low)

def rms_scale(values, gain_vector):
    return values * lax.rsqrt(lax.optimization_barrier(jnp.mean(values * values, axis=-1, keepdims=True)) + EPSILON) * gain_vector

def doc_numbers(lengths_row, places):
    doc_ends = jnp.cumsum(lengths_row)
    return lax.optimization_barrier(jnp.sum((doc_ends[None, :] <= places[:, None]).astype(jnp.int32), axis=1))

def attend_sequence(sequence, lengths_row, w_qkv, w_out, gain_attn, rel_bias):
    normed = low(rms_scale(sequence, gain_attn))
    qkv = low(low_back(jnp.dot(normed, w_qkv, precision=HIGHEST)))
    queries = qkv[:, :D].reshape(LENGTH, H, HD)
    key_rows = qkv[:, D:2 * D].reshape(LENGTH, H, HD)
    value_rows = qkv[:, 2 * D:].reshape(LENGTH, H, HD)
    documents = doc_numbers(lengths_row, jnp.arange(LENGTH, dtype=jnp.int32))
    span = (REACH + 1) * TOK_MB

    def one_block(block_index):
        start = block_index * TOK_MB
        first_key = jnp.maximum(start - REACH * TOK_MB, 0)
        query_block = lax.dynamic_slice_in_dim(queries, start, TOK_MB, 0)
        key_block = lax.dynamic_slice_in_dim(key_rows, first_key, span, 0)
        value_block = lax.dynamic_slice_in_dim(value_rows, first_key, span, 0)
        query_pos = start + jnp.arange(TOK_MB, dtype=jnp.int32)
        key_pos = first_key + jnp.arange(span, dtype=jnp.int32)
        query_doc = lax.dynamic_slice_in_dim(documents, start, TOK_MB, 0)
        key_doc = lax.dynamic_slice_in_dim(documents, first_key, span, 0)
        distance = query_pos[:, None] - key_pos[None, :]
        allowed = (distance >= 0) & (distance < WINDOW) & (query_doc[:, None] == key_doc[None, :])
        bias_tile = jnp.transpose(rel_bias[jnp.clip(distance, 0, WINDOW - 1)], (2, 0, 1))
        scores = jnp.einsum('qhd,khd->hqk', query_block, key_block, precision=HIGHEST) * HD ** (-0.5) + bias_tile
        scores = jnp.where(allowed[None], low_back(scores), MASKED)
        probs = low(jax.nn.softmax(scores, axis=-1))
        return jnp.einsum('hqk,khd->qhd', probs, value_block, precision=HIGHEST).reshape(TOK_MB, D)
    attended = lax.map(jax.checkpoint(one_block), jnp.arange(LENGTH // TOK_MB, dtype=jnp.int32)).reshape(LENGTH, D)
    branch = low_back(jnp.dot(low(low_back(attended)), w_out, precision=HIGHEST))
    return sequence + branch

def run_expert(expert_args):
    rows_in, w_in_one, w_back_one = expert_args
    pre_act = low_back(jnp.einsum('scd,df->scf', rows_in, w_in_one, precision=HIGHEST))
    hidden = low(jax.nn.gelu(pre_act))
    return low(low_back(jnp.einsum('scf,fd->scd', hidden, w_back_one, precision=HIGHEST)))

def fill_owners(place_row):
    empty = jnp.full((EXPERTS * CAP,), TOK_MB * TOP, jnp.int32)
    return empty.at[place_row].set(jnp.arange(TOK_MB * TOP, dtype=jnp.int32), mode='drop')

def take_rows(table_rows, picks):
    return table_rows[picks]

def expert_group(mixed_group, route_group, slot_group, gain_ffn, w_router, w_in, w_back):
    normed = low(rms_scale(mixed_group, gain_ffn))
    logits = jnp.einsum('std,de->ste', normed, w_router, precision=HIGHEST)
    gate_values = jax.nn.softmax(jnp.take_along_axis(logits, route_group, axis=2), axis=-1)
    places = jnp.where(slot_group >= 0, route_group * CAP + slot_group, EXPERTS * CAP).reshape(SEQS, TOK_MB * TOP)
    owners = jax.vmap(fill_owners)(places)
    padded = jnp.concatenate([normed, jnp.zeros((SEQS, 1, D), jnp.float32)], axis=1)
    rows_sent = jax.vmap(take_rows)(padded, owners // TOP)
    rows_sent = low_back(rows_sent).reshape(SEQS, EXPERTS, CAP, D).transpose(1, 0, 2, 3)
    expert_rows = lax.map(jax.checkpoint(run_expert), (rows_sent, w_in, w_back))
    expert_rows = expert_rows.transpose(1, 0, 2, 3).reshape(SEQS, EXPERTS * CAP, D)
    padded_back = jnp.concatenate([expert_rows, jnp.zeros((SEQS, 1, D), jnp.float32)], axis=1)
    picked = jax.vmap(take_rows)(padded_back, places).reshape(SEQS, TOK_MB, TOP, D)
    return lax.optimization_barrier(jnp.sum(gate_values[..., None] * picked, axis=2))

def layer_forward(params, doc_lengths, routes, slots):
    tokens, w_qkv, w_out, rel_bias, gain_attn, gain_ffn, w_router, w_in, w_back = params
    sequences = tokens.reshape(MICRO * SEQS, LENGTH, D)
    lengths_all = doc_lengths.reshape(MICRO * SEQS, DOCS)

    def one_sequence(seq_args):
        return attend_sequence(seq_args[0], seq_args[1], w_qkv, w_out, gain_attn, rel_bias)
    mixed = lax.map(jax.checkpoint(one_sequence), (sequences, lengths_all))
    blocks = LENGTH // TOK_MB

    def regroup(array_in, last_dim):
        shaped = array_in.reshape(MICRO, SEQS, blocks, TOK_MB, last_dim).transpose(0, 2, 1, 3, 4)
        return shaped.reshape(MICRO * blocks, SEQS, TOK_MB, last_dim)
    mixed_groups = regroup(mixed, D)
    route_groups = regroup(routes, TOP)
    slot_groups = regroup(slots, TOP)

    def one_group(group_args):
        return expert_group(group_args[0], group_args[1], group_args[2], gain_ffn, w_router, w_in, w_back)
    moe_groups = lax.map(jax.checkpoint(one_group), (mixed_groups, route_groups, slot_groups))
    final_groups = mixed_groups + moe_groups
    shaped = final_groups.reshape(MICRO, blocks, SEQS, TOK_MB, D).transpose(0, 2, 1, 3, 4)
    return shaped.reshape(MICRO, SEQS, LENGTH, D)

def reference(tokens, doc_lengths, routes, slots, w_qkv, w_out, rel_bias, gain_attn, gain_ffn, w_router, w_in, w_back, cotangent):
    floats = tuple((array_in.astype(jnp.float32) for array_in in (tokens, w_qkv, w_out, rel_bias, gain_attn, gain_ffn, w_router, w_in, w_back)))

    def whole_layer(*params):
        return layer_forward(params, doc_lengths, routes, slots)
    final_sum, pullback = jax.vjp(whole_layer, *floats)
    gradients = pullback(cotangent.astype(jnp.float32))
    return (final_sum.astype(jnp.bfloat16), gradients[0].astype(jnp.bfloat16), gradients[1], gradients[2], gradients[3], gradients[4], gradients[5], gradients[6], gradients[7], gradients[8])
```

```python
import functools

import jax
import jax.numpy as jnp
from jax import lax
from jax.experimental import pallas as pl
from jax.experimental.pallas import tpu as pltpu
from jax.sharding import PartitionSpec as P

H = 12
HD = 64
TOP = 2
WINDOW = 1024
EPSILON = 1e-06
MASKED = -1e30
LANES = 128

bf16 = jnp.bfloat16
f32 = jnp.float32
MIB = 1 << 20

NN = (((1,), (0,)), ((), ()))
NT = (((1,), (1,)), ((), ()))
TN = (((0,), (0,)), ((), ()))


def dot(a, b, dims=NN):
    return lax.dot_general(a, b, dims, preferred_element_type=f32)


def rsq(x):
    return lax.rsqrt(jnp.mean(x * x, axis=-1, keepdims=True) + EPSILON)


def call(kernel, outs, name, flops=0, scratch=(), n_smem=0, n_in=0, limit=48, trans=0, bytes_accessed=4 * MIB):
    smem = pl.BlockSpec(memory_space=pltpu.SMEM)
    vmem = pl.BlockSpec(memory_space=pltpu.VMEM)
    return pl.pallas_call(
        kernel,
        out_shape=[jax.ShapeDtypeStruct(s, d) for s, d in outs],
        in_specs=[smem] * n_smem + [vmem] * n_in,
        out_specs=[vmem] * len(outs),
        scratch_shapes=list(scratch),
        compiler_params=pltpu.CompilerParams(vmem_limit_bytes=limit * MIB),
        cost_estimate=pl.CostEstimate(
            flops=int(flops), transcendentals=int(trans), bytes_accessed=int(bytes_accessed)
        ),
        name=name,
    )


def tiles_kernel(spans, rows, band_ref, out_ref):
    heads = out_ref.shape[0]
    for h in range(heads):
        for s in range(spans):
            ahead = band_ref[h : h + 1, (s + 1) * rows : (s + 2) * rows]
            behind = band_ref[h : h + 1, s * rows : (s + 1) * rows]
            line = jnp.concatenate([ahead, behind], axis=1)
            spread = jnp.broadcast_to(line, (rows, 2 * rows))
            rolled = pltpu.roll(spread, 0, axis=1, stride=1, stride_axis=0)
            out_ref[h, s] = rolled[:, :rows]


def dispatch_cot_kernel(places_ref, other_ref, cot_ref, rows_ref, ids_ref):
    micros, _, tok = places_ref.shape
    total = rows_ref.shape[0]
    width = cot_ref.shape[-1]
    slot = lax.broadcasted_iota(jnp.int32, (total, tok), 0)
    for m in range(micros):
        picks = None
        ids = None
        for k in range(TOP):
            hit = slot == places_ref[m, k : k + 1, :]
            one = jnp.where(hit, 1.0, 0.0)
            other = jnp.sum(
                jnp.where(hit, other_ref[m, k : k + 1, :].astype(f32), 0.0),
                axis=1,
                keepdims=True,
            )
            picks = one if picks is None else picks + one
            ids = other if ids is None else ids + other
        rows_ref[:, m * width : (m + 1) * width] = dot(picks.astype(bf16), cot_ref[m]).astype(bf16)
        ids_ref[:, m : m + 1] = ids.astype(jnp.int32)


def attn_fwd_kernel(m, n, reach, heads, idx_ref, gain_ref, w_ref, tiles_ref, kdoc_ref, qdoc_ref, *rest):
    x_refs = rest[:n]
    att_ref, qkv_ref, lse_ref, vt_scr, ot_scr = rest[n:]
    tok = x_refs[0].shape[1]
    groups = qkv_ref.shape[0] // 3
    me = idx_ref[0]
    gain = gain_ref[...]
    for r in range(n):
        start = pl.multiple_of(jnp.bitwise_xor(me, r) * tok, tok)
        x = x_refs[r][m].astype(f32)
        normed = (x * rsq(x) * gain).astype(bf16)
        qkv = dot(normed, w_ref[...]).astype(bf16)
        for c in range(3 * groups):
            qkv_ref[c, pl.ds(start, tok), :] = qkv[:, c * LANES : (c + 1) * LANES]
    for g in range(groups):
        vt_scr[g * LANES : (g + 1) * LANES, :] = qkv_ref[2 * groups + g].astype(f32).T.astype(bf16)
    lse_ref[...] = jnp.zeros_like(lse_ref)

    def head_body(h, carry):
        g = lax.shift_right_logical(h, 1)
        half = jnp.bitwise_and(h, 1)
        lane = lax.broadcasted_iota(jnp.int32, (tok, LANES), 1)
        mine = lax.shift_right_logical(lane, 6) == half
        for j in range(n):
            lo = max(0, j - reach)
            q = qkv_ref[g, j * tok : (j + 1) * tok, :].astype(f32)
            q = jnp.where(mine, q * HD ** (-0.5), 0.0).astype(bf16)
            key = qkv_ref[groups + g, lo * tok : (j + 1) * tok, :]
            s = dot(key, q, NT)
            bias = jnp.concatenate([tiles_ref[h, j - b] for b in range(lo, j + 1)], axis=0)
            ok = kdoc_ref[lo * tok : (j + 1) * tok, :] == qdoc_ref[:, j * tok : (j + 1) * tok]
            s = jnp.where(ok, s + bias, MASKED)
            peak = jnp.max(s, axis=0, keepdims=True)
            e = jnp.exp(s - peak)
            total = jnp.sum(e, axis=0, keepdims=True)
            p = (e * (1.0 / total)).astype(bf16)
            lse_ref[pl.ds(h, 1), j * tok : (j + 1) * tok] = peak + jnp.log(total)
            vt = vt_scr[pl.ds(pl.multiple_of(h * HD, HD), HD), lo * tok : (j + 1) * tok]
            ot_scr[pl.ds(pl.multiple_of(h * HD, HD), HD), j * tok : (j + 1) * tok] = dot(vt, p)
        return carry

    lax.fori_loop(0, heads, head_body, 0)
    att_ref[...] = ot_scr[...].T[:, : heads * HD].astype(bf16)


def unshear_rows(tile):
    rows = tile.shape[0]
    wide = jnp.concatenate([tile, jnp.zeros_like(tile)], axis=1)
    span = 2 * rows
    count = rows
    while count > 1:
        count //= 2
        wide = wide[:count] + pltpu.roll(wide[count : 2 * count], span - count, axis=1)
    return wide


def attn_bwd_kernel(
    m, n, reach, heads, first, idx_ref, gain_ref, w_ref, tiles_ref, kdoc_ref, qdoc_ref, qkv_ref, lse_ref, grad_ref, *rest
):
    x_refs = rest[:n]
    rest = rest[n:]
    if not first:
        old_w_ref, old_small_ref, old_band_ref = rest[:3]
        rest = rest[3:]
    part_refs = rest[:n]
    new_w_ref, new_small_ref, new_band_ref, normed_scr, da_scr, kt_scr, dqt_scr, dkv_scr, dqkv_scr, acc_scr = rest[n:]
    tok = x_refs[0].shape[1]
    groups = qkv_ref.shape[0] // 3
    spans = tiles_ref.shape[1]
    wide = groups * LANES
    me = idx_ref[0]
    gain = gain_ref[...]
    for r in range(n):
        start = pl.multiple_of(jnp.bitwise_xor(me, r) * tok, tok)
        x = x_refs[r][m].astype(f32)
        normed_scr[pl.ds(start, tok), :] = (x * rsq(x) * gain).astype(bf16)
    if heads * HD < wide:
        da_scr[...] = jnp.zeros_like(da_scr)
    for d in range(n):
        for g in range(groups):
            cols = min(LANES, heads * HD - g * LANES)
            da_scr[g, d * tok : (d + 1) * tok, :cols] = grad_ref[d, :, g * LANES : g * LANES + cols]
    for g in range(groups):
        kt_scr[g * LANES : (g + 1) * LANES, :] = qkv_ref[groups + g].astype(f32).T.astype(bf16)
    dkv_scr[...] = jnp.zeros_like(dkv_scr)
    dqt_scr[...] = jnp.zeros_like(dqt_scr)
    acc_scr[...] = jnp.zeros_like(acc_scr)

    def head_body(h, carry):
        g = lax.shift_right_logical(h, 1)
        half = jnp.bitwise_and(h, 1)
        lane = lax.broadcasted_iota(jnp.int32, (tok, LANES), 1)
        mine = lax.shift_right_logical(lane, 6) == half
        for j in range(n):
            lo = max(0, j - reach)
            rows = slice(lo * tok, (j + 1) * tok)
            cols = slice(j * tok, (j + 1) * tok)
            q = qkv_ref[g, cols, :].astype(f32)
            q = jnp.where(mine, q * HD ** (-0.5), 0.0).astype(bf16)
            da = jnp.where(mine, da_scr[g, cols, :].astype(f32), 0.0).astype(bf16)
            s = dot(qkv_ref[groups + g, rows, :], q, NT)
            bias = jnp.concatenate([tiles_ref[h, j - b] for b in range(lo, j + 1)], axis=0)
            ok = kdoc_ref[rows, :] == qdoc_ref[:, cols]
            s = jnp.where(ok, s + bias, MASKED)
            p = jnp.exp(s - lse_ref[pl.ds(h, 1), cols])
            pg = dot(qkv_ref[2 * groups + g, rows, :], da, NT)
            centre = jnp.sum(p * pg, axis=0, keepdims=True)
            sg = (p * (pg - centre)).astype(bf16)
            for b in range(lo, j + 1):
                acc_scr[h, j - b] += sg[(b - lo) * tok : (b - lo + 1) * tok].astype(f32)
            dkv_scr[g, rows, :] += dot(sg, q)
            dkv_scr[groups + g, rows, :] += dot(p.astype(bf16), da)
            at = pl.ds(pl.multiple_of(h * HD, HD), HD)
            dqt_scr[at, cols] = dot(kt_scr[at, rows], sg) * HD ** (-0.5)
        return carry

    lax.fori_loop(0, heads, head_body, 0)
    for g in range(groups):
        dqkv_scr[:, g * LANES : (g + 1) * LANES] = dqt_scr[g * LANES : (g + 1) * LANES, :].T.astype(bf16)
    for c in range(2 * groups):
        dqkv_scr[:, wide + c * LANES : wide + (c + 1) * LANES] = dkv_scr[c].astype(bf16)
    small = None
    for r in range(n):
        start = pl.multiple_of(jnp.bitwise_xor(me, r) * tok, tok)
        x = x_refs[r][m].astype(f32)
        part = dot(dqkv_scr[pl.ds(start, tok), :], w_ref[...], NT)
        part_refs[r][...] = part.astype(bf16)
        term = jnp.sum(part * (x * rsq(x)), axis=0, keepdims=True)
        small = term if small is None else small + term
    new_w = dot(normed_scr[...], dqkv_scr[...], TN)
    if not first:
        new_w = new_w + old_w_ref[...]
        small = small + old_small_ref[0:1, :]
    new_w_ref[...] = new_w.astype(new_w_ref.dtype)
    new_small_ref[...] = jnp.broadcast_to(small, new_small_ref.shape)
    new_band_ref[...] = jnp.zeros_like(new_band_ref)
    for h in range(heads):
        lines = [unshear_rows(acc_scr[h, s]) for s in range(spans)]
        for s in range(spans):
            value = lines[s][:, :tok]
            if s + 1 < spans:
                value = value + lines[s + 1][:, tok:]
            if not first:
                value = value + old_band_ref[h : h + 1, s * tok : (s + 1) * tok]
            new_band_ref[h : h + 1, s * tok : (s + 1) * tok] = value


def mid_kernel(m, heads, x_ref, att_ref, dense_ref, gain_ref, places_ref, mixed_ref, rows_ref):
    n, tok, part = att_ref.shape
    width = x_ref.shape[-1]
    total = rows_ref.shape[0]
    mixed = x_ref[m].astype(f32)
    for d in range(n):
        size = min(part, width - d * part)
        if size > 0:
            mixed = mixed + dot(att_ref[d][:, :size], dense_ref[d * part : d * part + size, :width])
    mixed_ref[...] = mixed
    normed = (mixed * rsq(mixed) * gain_ref[...]).astype(bf16)
    slot = lax.broadcasted_iota(jnp.int32, (total, tok), 0)
    picks = jnp.where(slot == places_ref[m, 0:1, :], 1.0, 0.0)
    picks = picks + jnp.where(slot == places_ref[m, 1:2, :], 1.0, 0.0)
    rows_ref[...] = dot(picks.astype(bf16), normed).astype(bf16)


def expert_kernel(m, e_ref, x_ref, c_ref, ids_ref, dense_ref, win_ref, wback_ref, out_ref, hid_ref, pre_ref, g_ref, acc_scr, grad_scr):
    f = pl.program_id(0)
    width = x_ref.shape[-1]

    @pl.when(f == 0)
    def _():
        logits = dot(x_ref[...], dense_ref[...])
        lane = lax.broadcasted_iota(jnp.int32, logits.shape, 1)
        own = jnp.sum(jnp.where(lane == e_ref[0], logits, 0.0), axis=1, keepdims=True)
        other = jnp.sum(jnp.where(lane == ids_ref[:, m : m + 1], logits, 0.0), axis=1, keepdims=True)
        peak = jnp.maximum(own, other)
        own = jnp.exp(own - peak)
        gate = own / (own + jnp.exp(other - peak))
        grad = (gate * c_ref[...].astype(f32)).astype(bf16)
        grad_scr[...] = grad
        g_ref[...] = grad
        acc_scr[...] = jnp.zeros_like(acc_scr)

    pre = dot(x_ref[...], win_ref[...])
    c0 = 0.7978845608028654
    square = pre * pre
    t = jnp.tanh(pre * (c0 + (c0 * 0.044715) * square))
    hidden = (0.5 * pre * (1.0 + t)).astype(bf16)
    hid_ref[...] = hidden
    slope = 0.5 * (1.0 + t) + 0.5 * pre * (1.0 - t * t) * (c0 + (3 * c0 * 0.044715) * square)
    acc_scr[:, :width] += dot(hidden, wback_ref[...])
    pre_grad = (dot(grad_scr[...], wback_ref[...], NT) * slope).astype(bf16)
    pre_ref[...] = pre_grad
    acc_scr[:, width:] += dot(pre_grad, win_ref[...], NT)

    @pl.when(f == pl.num_programs(0) - 1)
    def _():
        out_ref[...] = acc_scr[...].astype(bf16)


def grad_back_kernel(pos_ref, h0_ref, h1_ref, g0_ref, g1_ref, out_ref):
    out_ref[...] = (dot(h0_ref[...], g0_ref[...], TN) + dot(h1_ref[...], g1_ref[...], TN)).astype(bf16)


def grad_in_kernel(pos_ref, x0_ref, x1_ref, p0_ref, p1_ref, out_ref):
    value = (dot(x0_ref[...], p0_ref[...], TN) + dot(x1_ref[...], p1_ref[...], TN)).astype(bf16)
    n, rows, _ = out_ref.shape
    for b in range(n):
        out_ref[pos_ref[b]] = value[b * rows : (b + 1) * rows]


def combine_kernel(m, first, back_ref, places_ref, routes_ref, mixed_ref, cot_ref, att_ref, dense_ref, gain_ref, *rest):
    if not first:
        old_ref = rest[0]
        rest = rest[1:]
    out_ref, da_ref, mg_ref, new_ref = rest
    n, tok, part = att_ref.shape
    width = mixed_ref.shape[-1]
    total = back_ref.shape[0]
    mixed = mixed_ref[...]
    gain = gain_ref[...]
    rr = rsq(mixed)
    normed = (mixed * rr * gain).astype(bf16)
    router = dense_ref[:, width:]
    logits = dot(normed, router)
    lane = lax.broadcasted_iota(jnp.int32, logits.shape, 1)
    route = [lane == routes_ref[m, :, k : k + 1] for k in range(TOP)]
    chosen = [jnp.sum(jnp.where(r, logits, 0.0), axis=1, keepdims=True) for r in route]
    peak = jnp.maximum(chosen[0], chosen[1])
    powers = [jnp.exp(c - peak) for c in chosen]
    whole = powers[0] + powers[1]
    gates = [v / whole for v in powers]
    slot = lax.broadcasted_iota(jnp.int32, (tok, total), 1)
    hits = [jnp.where(slot == places_ref[m, :, k : k + 1], 1.0, 0.0) for k in range(TOP)]
    results = back_ref[:, :width]
    returned = [dot(h.astype(bf16), results) for h in hits]
    moe = gates[0] * returned[0] + gates[1] * returned[1]
    out_ref[...] = (mixed + moe).astype(bf16)
    up = cot_ref[m].astype(f32)
    gate_grad = [jnp.sum(up * v, axis=1, keepdims=True) for v in returned]
    centre = gates[0] * gate_grad[0] + gates[1] * gate_grad[1]
    chosen_grad = [gates[k] * (gate_grad[k] - centre) for k in range(TOP)]
    logit_grad = jnp.where(route[0], chosen_grad[0], 0.0) + jnp.where(route[1], chosen_grad[1], 0.0)
    high = logit_grad.astype(bf16)
    low = (logit_grad - high.astype(f32)).astype(bf16)
    normed_grad = dot((hits[0] + hits[1]).astype(bf16), back_ref[:, width:])
    normed_grad = normed_grad + dot(high, router, NT) + dot(low, router, NT)
    router_grad = dot(normed, high, TN) + dot(normed, low, TN)
    scaled = mixed * rr
    gain_part = jnp.sum(normed_grad * scaled, axis=0, keepdims=True)
    ng = gain * normed_grad
    mixed_grad = up + rr * (ng - scaled * jnp.mean(ng * scaled, axis=-1, keepdims=True))
    mg_ref[...] = mixed_grad
    branch = mixed_grad.astype(bf16)
    gain_col = jnp.broadcast_to(gain_part, (LANES, width)).T
    lane = lax.broadcasted_iota(jnp.int32, gain_col.shape, 1)
    extra = jnp.where(lane == LANES - 1, gain_col, router_grad)
    if not first:
        extra = extra + old_ref[:, width:].astype(f32)
    new_ref[:, width:] = extra.astype(new_ref.dtype)
    for d in range(n):
        size = min(part, width - d * part)
        if size <= 0:
            da_ref[d] = jnp.zeros((tok, part), bf16)
            continue
        at = slice(d * part, d * part + size)
        piece = dot(branch, dense_ref[at, :width], NT).astype(bf16)
        if size < part:
            piece = jnp.concatenate([piece, jnp.zeros((tok, part - size), bf16)], axis=1)
        da_ref[d] = piece
        grad = dot(att_ref[d][:, :size], branch, TN)
        if not first:
            grad = grad + old_ref[at, :width].astype(f32)
        new_ref[at, :width] = grad.astype(new_ref.dtype)


def token_grad_kernel(m, x_ref, mg_ref, gain_ref, *rest):
    parts, out_ref = rest[:-1], rest[-1]
    grad = parts[0][...].astype(f32)
    for p in parts[1:]:
        grad = grad + p[...].astype(f32)
    x = x_ref[m].astype(f32)
    r = rsq(x)
    scaled = x * r
    ng = gain_ref[...] * grad
    out_ref[...] = (
        mg_ref[...] + r * (ng - scaled * jnp.mean(ng * scaled, axis=-1, keepdims=True))
    ).astype(bf16)


def swap(x, axis, by):
    return lax.ppermute(x, axis, [(i, i ^ by) for i in range(lax.axis_size(axis))])


def exchange(x, axes):
    return lax.all_to_all(x, axes, split_axis=0, concat_axis=0, tiled=True)


def bit_reversed(n):
    bits = n.bit_length() - 1
    return [int(format(r, "b").zfill(bits)[::-1], 2) if bits else 0 for r in range(n)]


def halving_sum(x, axis):
    by = 1
    while x.shape[0] > 1:
        half = x.shape[0] // 2
        came = swap(x[half:], axis, by)
        x = x[:half].astype(f32) + came.astype(f32)
        if half > 1:
            x = x.astype(bf16)
        by *= 2
    return x[0]


def shards(
    tokens, doc_lengths, routes, slots, w_qkv, w_out, rel_bias, gain_attn, gain_ffn, w_router, w_in, w_back, cotangent
):
    micros, _, tok, width = tokens.shape
    n = lax.axis_size("dp")
    experts = lax.axis_size("expert")
    me = lax.axis_index("dp")
    my_expert = lax.axis_index("expert")
    reach = min((WINDOW - 2) // tok + 1, n - 1)
    spans = reach + 1
    capacity = (9 * tok * TOP + 8 * experts - 1) // (8 * experts)
    total = experts * capacity
    length = n * tok
    heads = -(-H // n)
    groups = -(-heads // 2)
    part = heads * HD
    wide = groups * LANES
    ff = w_in.shape[2]
    own_rows = w_qkv.shape[0]
    both = ("dp", "expert")
    tokens, cotangent = tokens[:, 0], cotangent[:, 0]
    routes, slots = routes[:, 0], slots[:, 0]
    idx = me.astype(jnp.int32).reshape(1)

    q_cols = w_qkv.reshape(own_rows, 3, H, HD)
    q_cols = jnp.pad(q_cols, ((0, 0), (0, 0), (0, heads * n - H), (0, 0)))
    q_cols = q_cols.reshape(own_rows, 3, n, part).transpose(2, 0, 1, 3).reshape(n, own_rows, 3 * part)
    send_cols = -(-(3 * part + 1) // LANES) * LANES
    gain_cols = jnp.broadcast_to(gain_attn[None, :, None], (n, own_rows, 1))
    q_cols = jnp.concatenate(
        [q_cols, gain_cols, jnp.zeros((n, own_rows, send_cols - 3 * part - 1), bf16)], axis=2
    )
    q_cols = jnp.broadcast_to(q_cols[:, None], (n, experts, own_rows, send_cols)).reshape(
        n * experts, own_rows, send_cols
    )
    w_mine = exchange(q_cols, both).reshape(width, send_cols)
    gain_a = w_mine[:, 3 * part].astype(f32)[None]
    w_heads = jnp.pad(
        w_mine[:, : 3 * part].reshape(width, 3, part), ((0, 0), (0, 0), (0, wide - part))
    ).reshape(width, 3 * wide)
    dense = jnp.concatenate(
        [
            w_out,
            w_router,
            jnp.zeros((own_rows, LANES - experts - 1), bf16),
            gain_ffn[:, None],
        ],
        axis=1,
    )
    dense = lax.all_gather(dense, both, axis=0, tiled=True)
    gain_f = dense[:, width + LANES - 1].astype(f32)[None]

    blocks = {0: tokens}
    by = n // 2
    while by:
        for r in list(blocks):
            blocks[r ^ by] = swap(blocks[r], "dp", by)
        by //= 2
    xs = [blocks[r] for r in range(n)]

    bias = jnp.pad(rel_bias.astype(f32).T, ((0, heads * n - H), (0, 0)))
    bias = lax.dynamic_slice_in_dim(bias, me * heads, heads, 0)[:, : spans * tok]
    band = jnp.concatenate(
        [
            jnp.full((heads, tok), MASKED, f32),
            bias,
            jnp.full((heads, spans * tok - bias.shape[1]), MASKED, f32),
        ],
        axis=1,
    )
    band = jnp.pad(band, ((0, -heads % 8), (0, 0)))
    (tiles,) = call(
        functools.partial(tiles_kernel, spans, tok),
        [((heads, spans, tok, tok), f32)],
        "bias_tiles",
        n_in=1,
    )(band)

    places = jnp.where(slots >= 0, routes * capacity + slots, total)
    places_row = places.transpose(0, 2, 1)
    other_row = routes[..., ::-1].transpose(0, 2, 1)
    doc_ends = jnp.cumsum(doc_lengths[:, 0], axis=-1)
    positions = jnp.arange(length, dtype=jnp.int32)
    docs = jnp.sum((doc_ends[:, None, :] <= positions[None, :, None]).astype(jnp.int32), axis=2)

    cot_rows, ids = call(
        dispatch_cot_kernel,
        [((total, micros * width), bf16), ((total, micros), jnp.int32)],
        "dispatch_cotangent",
        flops=2 * micros * total * tok * width,
        n_in=3,
    )(places_row, other_row, cotangent)
    ids = exchange(ids.reshape(experts, capacity, micros).transpose(0, 2, 1), "expert")
    ids = ids.transpose(0, 2, 1).reshape(total, micros)
    cot_rows, w_heads = lax.optimization_barrier((cot_rows, w_heads))
    cot_rows = exchange(cot_rows.reshape(experts, capacity, micros * width), "expert").reshape(
        total, micros * width
    )

    att = []
    saved = []
    pair_flops = 2 * heads * LANES * tok * tok * sum(min(j, reach) + 1 for j in range(n))
    for m in range(micros):
        kdoc, qdoc = docs[m][:, None], docs[m][None]
        att_m, qkv, lse = call(
            functools.partial(attn_fwd_kernel, m, n, reach, heads),
            [((length, part), bf16), ((3 * groups, length, LANES), bf16), ((8, length), f32)],
            "attention_forward",
            flops=2 * length * width * 3 * wide + 2 * pair_flops,
            scratch=[pltpu.VMEM((wide, length), bf16), pltpu.VMEM((wide, length), f32)],
            n_smem=1,
            n_in=5 + n,
        )(idx, gain_a, w_heads, tiles, kdoc, qdoc, *xs)
        att.append(exchange(att_m.reshape(n, tok, part), "dp"))
        saved.append((kdoc, qdoc, qkv, lse))

    mixed = []
    arrived = []
    for m in range(micros):
        mixed_m, rows = call(
            functools.partial(mid_kernel, m, heads),
            [((tok, width), f32), ((total, width), bf16)],
            "mix_and_dispatch",
            flops=2 * tok * width * width + 2 * total * tok * width,
            n_in=5,
        )(tokens, att[m], dense, gain_f, places_row)
        mixed.append(mixed_m)
        arrived.append(exchange(rows.reshape(experts, capacity, width), "expert").reshape(total, width))

    tile = 512
    back = []
    kept = []
    for m in range(micros):
        whole = lambda shape, c=0: pl.BlockSpec(shape, lambda f, c=c: (0, c))
        out, hid, pre, g = pl.pallas_call(
            functools.partial(expert_kernel, m),
            out_shape=[
                jax.ShapeDtypeStruct((total, 2 * width), bf16),
                jax.ShapeDtypeStruct((total, ff), bf16),
                jax.ShapeDtypeStruct((total, ff), bf16),
                jax.ShapeDtypeStruct((total, width), bf16),
            ],
            grid=(ff // tile,),
            in_specs=[
                pl.BlockSpec(memory_space=pltpu.SMEM),
                whole((total, width)),
                whole((total, width), m),
                whole((total, micros)),
                whole((width, LANES), width // LANES),
                pl.BlockSpec((None, width, tile), lambda f: (0, 0, f)),
                pl.BlockSpec((None, tile, width), lambda f: (0, f, 0)),
            ],
            out_specs=[
                whole((total, 2 * width)),
                pl.BlockSpec((total, tile), lambda f: (0, f)),
                pl.BlockSpec((total, tile), lambda f: (0, f)),
                whole((total, width)),
            ],
            scratch_shapes=[pltpu.VMEM((total, 2 * width), f32), pltpu.VMEM((total, width), bf16)],
            compiler_params=pltpu.CompilerParams(vmem_limit_bytes=48 * MIB),
            cost_estimate=pl.CostEstimate(
                flops=8 * total * width * ff, transcendentals=total * ff, bytes_accessed=20 * MIB
            ),
            name="expert",
        )(my_expert.astype(jnp.int32).reshape(1), arrived[m], cot_rows, ids, dense, w_in, w_back)
        back.append(exchange(out.reshape(experts, capacity, 2 * width), "expert").reshape(total, 2 * width))
        kept.append((hid, pre, g))

    order = jnp.asarray(bit_reversed(n), jnp.int32)[jnp.bitwise_xor(jnp.arange(n, dtype=jnp.int32), me)]
    assert micros == 2
    cols = ff // n
    grad_back = pl.pallas_call(
        grad_back_kernel,
        out_shape=jax.ShapeDtypeStruct((n, cols, width), bf16),
        grid_spec=pltpu.PrefetchScalarGridSpec(
            num_scalar_prefetch=1,
            grid=(n,),
            in_specs=[
                pl.BlockSpec((total, cols), lambda b, pos: (0, b)),
                pl.BlockSpec((total, cols), lambda b, pos: (0, b)),
                pl.BlockSpec((total, width), lambda b, pos: (0, 0)),
                pl.BlockSpec((total, width), lambda b, pos: (0, 0)),
            ],
            out_specs=pl.BlockSpec((None, cols, width), lambda b, pos: (pos[b], 0, 0)),
        ),
        compiler_params=pltpu.CompilerParams(vmem_limit_bytes=48 * MIB),
        cost_estimate=pl.CostEstimate(
            flops=4 * total * width * ff, transcendentals=0, bytes_accessed=12 * MIB
        ),
        name="grad_back",
    )(order, kept[0][0], kept[1][0], kept[0][2], kept[1][2])
    grad_in = pl.pallas_call(
        grad_in_kernel,
        out_shape=jax.ShapeDtypeStruct((n, width // n, ff), bf16),
        grid_spec=pltpu.PrefetchScalarGridSpec(
            num_scalar_prefetch=1,
            grid=(ff // tile,),
            in_specs=[
                pl.BlockSpec((total, width), lambda f, pos: (0, 0)),
                pl.BlockSpec((total, width), lambda f, pos: (0, 0)),
                pl.BlockSpec((total, tile), lambda f, pos: (0, f)),
                pl.BlockSpec((total, tile), lambda f, pos: (0, f)),
            ],
            out_specs=pl.BlockSpec((n, width // n, tile), lambda f, pos: (0, 0, f)),
        ),
        compiler_params=pltpu.CompilerParams(vmem_limit_bytes=48 * MIB),
        cost_estimate=pl.CostEstimate(
            flops=4 * total * width * ff, transcendentals=0, bytes_accessed=12 * MIB
        ),
        name="grad_in",
    )(order, arrived[0], arrived[1], kept[0][1], kept[1][1])
    grad_back = halving_sum(grad_back, "dp")
    grad_in = halving_sum(grad_in, "dp")

    outputs = []
    token_grads = []
    dense_grad = ()
    attn_grad = ()
    for m in range(micros):
        first, last = m == 0, m == micros - 1
        out, da, mixed_grad, *dense_grad = call(
            functools.partial(combine_kernel, m, first),
            [
                ((tok, width), bf16),
                ((n, tok, part), bf16),
                ((tok, width), f32),
                ((width, width + LANES), bf16 if last else f32),
            ],
            "combine",
            flops=6 * total * tok * width + 4 * tok * width * width,
            n_in=8 + len(dense_grad),
        )(back[m], places, routes, mixed[m], cotangent, att[m], dense, gain_f, *dense_grad)
        outputs.append(out)
        da = exchange(da, "dp")
        kdoc, qdoc, qkv, lse = saved[m]
        *parts, grad_w, grad_gain, grad_band = call(
            functools.partial(attn_bwd_kernel, m, n, reach, heads, first),
            [((tok, width), bf16)] * n
            + [
                ((width, 3 * wide), bf16 if last else f32),
                ((8, width), f32),
                ((8, spans * tok), f32),
            ],
            "attention_backward",
            flops=4 * length * width * 3 * wide + 5 * pair_flops,
            scratch=[
                pltpu.VMEM((length, width), bf16),
                pltpu.VMEM((groups, length, LANES), bf16),
                pltpu.VMEM((wide, length), bf16),
                pltpu.VMEM((wide, length), f32),
                pltpu.VMEM((2 * groups, length, LANES), f32),
                pltpu.VMEM((length, 3 * wide), bf16),
                pltpu.VMEM((heads, spans, tok, tok), f32),
            ],
            n_smem=1,
            n_in=8 + n + len(attn_grad),
        )(idx, gain_a, w_heads, tiles, kdoc, qdoc, qkv, lse, da, *xs, *attn_grad)
        attn_grad = (grad_w, grad_gain, grad_band)
        summed = [parts[0]] + [swap(parts[r], "dp", r) for r in range(1, n)]
        (token_grad,) = call(
            functools.partial(token_grad_kernel, m),
            [((tok, width), bf16)],
            "token_grad",
            n_in=3 + n,
        )(tokens, mixed_grad, gain_a, *summed)
        token_grads.append(token_grad)

    whole_count = n * experts
    dense_sum = exchange(dense_grad[0].reshape(whole_count, own_rows, width + LANES), both)
    dense_sum = jnp.sum(dense_sum.astype(f32), axis=0)
    band_flat = grad_band[:heads, :WINDOW].astype(bf16)
    band_width = band_flat.shape[1]
    per_row = -(-heads * band_width // (own_rows * LANES)) * LANES
    band_flat = jnp.pad(band_flat.reshape(-1), (0, own_rows * per_row - heads * band_width))
    band_flat = jnp.broadcast_to(
        band_flat.reshape(1, own_rows, per_row), (whole_count, own_rows, per_row)
    )
    grad_w = grad_w.reshape(width, 3, wide)[:, :, :part].reshape(width, 3 * part)
    message = jnp.concatenate(
        [
            grad_w,
            grad_gain[0].astype(bf16)[:, None],
            jnp.zeros((width, send_cols - 3 * part - 1), bf16),
        ],
        axis=1,
    ).reshape(whole_count, own_rows, send_cols)
    message = exchange(jnp.concatenate([message, band_flat], axis=2), both)
    message = message.reshape(n, experts, own_rows, send_cols + per_row).astype(f32)
    by_dp = jnp.sum(message, axis=1)
    grad_qkv = by_dp[:, :, : 3 * part].reshape(n, own_rows, 3, part).transpose(1, 2, 0, 3)
    grad_qkv = grad_qkv.reshape(own_rows, 3, n * part)[:, :, :width].reshape(own_rows, 3 * width)
    grad_gain_a = jnp.sum(by_dp[:, :, 3 * part], axis=0)
    grad_bias = by_dp[:, :, send_cols:].reshape(n, own_rows * per_row)[:, : heads * band_width]
    grad_bias = grad_bias.reshape(n * heads, band_width)[:H].T
    grad_bias = jnp.pad(grad_bias, ((0, WINDOW - band_width), (0, 0)))
    return (
        jnp.stack(outputs)[:, None],
        jnp.stack(token_grads)[:, None],
        grad_qkv,
        dense_sum[:, :width],
        grad_bias,
        grad_gain_a,
        dense_sum[:, width + LANES - 1],
        dense_sum[:, width : width + experts],
        grad_in[None],
        grad_back[None],
    )


def solution(mesh):
    return jax.shard_map(
        shards,
        mesh=mesh,
        in_specs=(
            P(None, "expert", "dp", None),
            P(None, "expert", None),
            P(None, "expert", "dp", None),
            P(None, "expert", "dp", None),
            P(("dp", "expert"), None),
            P(("dp", "expert"), None),
            P(),
            P(("dp", "expert")),
            P(("dp", "expert")),
            P(("dp", "expert"), None),
            P("expert", None, None),
            P("expert", None, None),
            P(None, "expert", "dp", None),
        ),
        out_specs=(
            P(None, "expert", "dp", None),
            P(None, "expert", "dp", None),
            P(("dp", "expert"), None),
            P(("dp", "expert"), None),
            P(),
            P(("dp", "expert")),
            P(("dp", "expert")),
            P(("dp", "expert"), None),
            P("expert", "dp", None),
            P("expert", "dp", None),
        ),
        check_vma=False,
    )
```

```python
import functools

import jax
import jax.numpy as jnp
from jax import lax
from jax.experimental import pallas as pl
from jax.experimental.pallas import tpu as pltpu
from jax.sharding import PartitionSpec as P

H = 12
HD = 64
TOP = 2
WINDOW = 1024
EPSILON = 1e-06
MASKED = -1e30
LANES = 128

bf16 = jnp.bfloat16
f32 = jnp.float32
MIB = 1 << 20

NN = (((1,), (0,)), ((), ()))
NT = (((1,), (1,)), ((), ()))
TN = (((0,), (0,)), ((), ()))


def dot(a, b, dims=NN):
    return lax.dot_general(a, b, dims, preferred_element_type=f32)


def rsq(x):
    return lax.rsqrt(jnp.mean(x * x, axis=-1, keepdims=True) + EPSILON)


def call(kernel, outs, name, smem=(), arrays=(), after=(), flops=0, scratch=(), limit=60, out_micro=()):
    def spec(x):
        if isinstance(x, tuple):
            x, i = x
            return pl.BlockSpec((None,) + x.shape[1:], lambda _: (i,) + (0,) * (x.ndim - 1))
        return pl.BlockSpec(x.shape, lambda _: (0,) * x.ndim)

    arrays = list(arrays)
    given = [x[0] if isinstance(x, tuple) else x for x in arrays]
    micro_of = {k: i for k, i, _ in out_micro}
    olds = [(k, old) for k, _, old in out_micro if old is not None]

    def out_spec(k, s):
        if k in micro_of:
            return pl.BlockSpec((None,) + s[1:], lambda _: (micro_of[k],) + (0,) * (len(s) - 1))
        return pl.BlockSpec(s, lambda _: (0,) * len(s))

    after = list(after) + [old for _, old in olds]
    aliases = {len(smem) + len(arrays) + len(after) - len(olds) + i: k for i, (k, _) in enumerate(olds)}
    size = lambda shape, dtype: int(jnp.dtype(dtype).itemsize * functools.reduce(lambda p, q: p * q, shape, 1))
    moved = sum(size(x.shape, x.dtype) for x in given) + sum(size(*o) for o in outs)
    return pl.pallas_call(
        kernel,
        grid=(1,),
        out_shape=[jax.ShapeDtypeStruct(s, d) for s, d in outs],
        in_specs=[pl.BlockSpec(memory_space=pltpu.SMEM)] * len(smem)
        + [spec(x) for x in arrays]
        + [pl.BlockSpec(memory_space=pl.ANY)] * len(after),
        out_specs=[out_spec(k, s) for k, (s, _) in enumerate(outs)],
        input_output_aliases=aliases,
        scratch_shapes=list(scratch),
        compiler_params=pltpu.CompilerParams(vmem_limit_bytes=limit * MIB),
        cost_estimate=pl.CostEstimate(flops=int(flops), transcendentals=0, bytes_accessed=moved),
        name=name,
    )(*smem, *given, *after)


def gate(x, *after):
    hbm = pl.BlockSpec(memory_space=pl.ANY)
    return pl.pallas_call(
        lambda *refs: None,
        out_shape=jax.ShapeDtypeStruct(x.shape, x.dtype),
        in_specs=[hbm] * (1 + len(after)),
        out_specs=hbm,
        input_output_aliases={0: 0},
        name="gate",
    )(x, *after)


def packed_blocks(heads):
    return 3 * (heads // 2) + (2 if heads % 2 else 1)


def gain_place(heads):
    return packed_blocks(heads) - 1, HD if heads % 2 else 0


def head_place(heads, kind, h):
    if heads % 2 and h == heads - 1:
        return 3 * (heads // 2) + kind // 2, kind % 2
    return 3 * (h // 2) + kind, h % 2


def low_lanes(shape):
    return lax.broadcasted_iota(jnp.int32, shape, 1) < HD


def move_half(block, source, target):
    return block if source == target else pltpu.roll(block, HD, axis=1)


def column_of(row):
    n = row.shape[1]
    same = lax.broadcasted_iota(jnp.int32, (n, n), 0) == lax.broadcasted_iota(jnp.int32, (n, n), 1)
    return jnp.sum(jnp.where(same, row, 0.0), axis=1, keepdims=True)


def dense_share(n, width):
    return -(-(width + LANES) // (n * LANES)) * LANES


def pack_kernel(n, w_ref, gain_ref, w_out_ref, router_ref, gain_ffn_ref, out_ref):
    count, rows, _ = out_ref.shape
    copies = count // n
    heads = -(-H // n)
    width = w_ref.shape[1] // 3
    low = low_lanes((rows, LANES))
    lane = lax.broadcasted_iota(jnp.int32, (rows, LANES), 1)
    gain = column_of(gain_ref[...].astype(f32))
    gain_block, gain_lane = gain_place(heads)
    for d in range(n):
        found = {}
        for kind in range(3):
            for h in range(heads):
                head = d * heads + h
                if head >= H:
                    continue
                block, half = head_place(heads, kind, h)
                column = kind * width + head * HD
                start = column // LANES * LANES
                piece = move_half(
                    w_ref[:, start : start + LANES].astype(f32), (column - start) // HD, half
                )
                found[block, half] = piece
        for block in range(packed_blocks(heads)):
            none = jnp.zeros((rows, LANES), f32)
            value = jnp.where(low, found.get((block, 0), none), found.get((block, 1), none))
            if block == gain_block:
                value = jnp.where(lane == gain_lane, gain, value)
            value = value.astype(bf16)
            for e in range(copies):
                out_ref[d * copies + e, :, block * LANES : (block + 1) * LANES] = value
    share = dense_share(n, width)
    gain = column_of(gain_ffn_ref[...].astype(f32))
    router = jnp.concatenate(
        [router_ref[...].astype(f32), jnp.zeros((rows, LANES - router_ref.shape[1]), f32)], axis=1
    )
    router = jnp.where(lane == LANES - 1, gain, router).astype(bf16)
    for d in range(n):
        for c in range(0, share, LANES):
            column = d * share + c
            if column < width:
                value = w_out_ref[:, column : column + LANES]
            elif column == width:
                value = router
            else:
                value = jnp.zeros((rows, LANES), bf16)
            at = packed_blocks(heads) * LANES + c
            for e in range(copies):
                out_ref[d * copies + e, :, at : at + LANES] = value


def unpack_qkv(heads, w_ref, w_scr):
    groups = -(-heads // 2)
    rows = w_ref.shape[0]
    low = low_lanes((rows, LANES))
    for kind in range(3):
        for g in range(groups):
            block, half = head_place(heads, kind, 2 * g)
            value = w_ref[:, block * LANES : (block + 1) * LANES]
            if 2 * g + 1 == heads:
                value = jnp.where(low, move_half(value.astype(f32), half, 0), 0.0).astype(bf16)
            at = (kind * groups + g) * LANES
            w_scr[:, at : at + LANES] = value
    block, lane = gain_place(heads)
    turned = w_ref[:, block * LANES : (block + 1) * LANES].astype(f32).T
    return turned[lane : lane + 1]


def pack_grad(heads, grad, gain_row, extra, out_ref):
    groups = -(-heads // 2)
    rows = grad.shape[0]
    low = low_lanes((rows, LANES))
    lane = lax.broadcasted_iota(jnp.int32, (rows, LANES), 1)
    part = lambda kind, g: grad[:, (kind * groups + g) * LANES : (kind * groups + g + 1) * LANES]
    blocks = [part(kind, g) for g in range(heads // 2) for kind in range(3)]
    if heads % 2:
        g = groups - 1
        blocks.append(jnp.where(low, part(0, g), pltpu.roll(part(1, g), HD, axis=1)))
        blocks.append(jnp.where(low, part(2, g), 0.0))
    else:
        blocks.append(jnp.zeros((rows, LANES), f32))
    gain_col = jnp.broadcast_to(gain_row, (LANES, rows)).T
    _, gain_lane = gain_place(heads)
    blocks[-1] = jnp.where(lane == gain_lane, gain_col, blocks[-1])
    blocks[-1] = jnp.where(lane > gain_lane, pltpu.roll(extra, gain_lane + 1, axis=1), blocks[-1])
    for i, block in enumerate(blocks):
        out_ref[:, i * LANES : (i + 1) * LANES] = block.astype(bf16)


def finish_kernel(n, message_ref, qkv_ref, small_ref, gain_ref):
    count, rows, lanes = message_ref.shape
    copies = count // n
    heads = -(-H // n)
    width = qkv_ref.shape[1] // 3
    packed = packed_blocks(heads) * LANES
    low = low_lanes((rows, LANES))
    sums = []
    gain_block, gain_lane = gain_place(heads)
    gain = None
    for d in range(n):
        total = message_ref[d * copies].astype(f32)
        for e in range(1, copies):
            total = total + message_ref[d * copies + e].astype(f32)
        sums.append(total)
        small_ref[d] = total[:, packed:]
        term = total[:, gain_block * LANES : (gain_block + 1) * LANES]
        gain = term if gain is None else gain + term
    gain_ref[...] = gain
    for kind in range(3):
        for pair in range(H // 2):
            halves = []
            for to in range(2):
                head = 2 * pair + to
                block, half = head_place(heads, kind, head % heads)
                value = sums[head // heads][:, block * LANES : (block + 1) * LANES]
                halves.append(move_half(value, half, to))
            at = kind * width + pair * LANES
            qkv_ref[:, at : at + LANES] = jnp.where(low, halves[0], halves[1])


def tiles_kernel(spans, rows, band_ref, *rest):
    out_ref = rest[-1]
    heads = out_ref.shape[0]
    for h in range(heads):
        for s in range(spans):
            ahead = band_ref[h : h + 1, (s + 1) * rows : (s + 2) * rows]
            behind = band_ref[h : h + 1, s * rows : (s + 1) * rows]
            line = jnp.concatenate([ahead, behind], axis=1)
            spread = jnp.broadcast_to(line, (rows, 2 * rows))
            rolled = pltpu.roll(spread, 0, axis=1, stride=1, stride_axis=0)
            out_ref[h, s] = rolled[:, :rows]


def pick_each(places, total):
    slot = lax.broadcasted_iota(jnp.int32, (total, places.shape[1]), 0)
    return [jnp.where(slot == places[k : k + 1], 1.0, 0.0) for k in range(TOP)]


def picks_of(places, total):
    return sum(pick_each(places, total)).astype(bf16)


def dispatch_kernel(capacity, padded, places_row_ref, places_ref, other_ref, cot_ref, after_ref, out_ref):
    tok = places_ref.shape[0]
    total, width = out_ref.shape
    experts = total // padded
    lane = lax.broadcasted_iota(jnp.int32, (tok, LANES), 1)
    lines = []
    for e in range(experts):
        slot = jnp.where(lane < capacity, lane + e * padded, -1)
        found = sum(
            jnp.where(slot == places_ref[:, k : k + 1], other_ref[:, k : k + 1].astype(f32), 0.0)
            for k in range(TOP)
        )
        lines.append(jnp.sum(found, axis=0, keepdims=True))
    spare = -experts % 16
    if spare:
        lines.append(jnp.zeros((spare, LANES), f32))
    lines = jnp.concatenate(lines, axis=0).astype(bf16)
    shape = (total, lines.shape[0])
    row = lax.broadcasted_iota(jnp.int32, shape, 0)
    here = row == lax.broadcasted_iota(jnp.int32, shape, 1) * padded + capacity
    ids = dot(jnp.where(here, 1.0, 0.0).astype(bf16), lines)
    rows = dot(picks_of(places_row_ref[...], total), cot_ref[...])
    out_ref[:, :LANES] = (rows[:, :LANES] + ids).astype(bf16)
    out_ref[:, LANES:] = rows[:, LANES:].astype(bf16)


def attn_fwd_kernel(n, reach, heads, first, idx_ref, w_ref, *rest):
    if not first:
        gain_ref, *rest = rest
    tiles_ref, kdoc_ref, qdoc_ref, *rest = rest
    x_refs, rest = rest[:n], rest[n:]
    att_refs, rest = rest[:n], rest[n:]
    qkv_ref, lse_ref, *rest = rest
    if first:
        heads_ref, gain_out_ref, *rest = rest
        gain = unpack_qkv(heads, w_ref, heads_ref)
        gain_out_ref[...] = gain
        w_ref = heads_ref
    else:
        gain = gain_ref[...]
    vt_scr, ot_scr, att_scr = rest
    tok = x_refs[0].shape[0]
    part = heads * HD
    groups = qkv_ref.shape[0] // 3
    me = idx_ref[0]
    for r in range(n):
        start = pl.multiple_of(jnp.bitwise_xor(me, r) * tok, tok)
        x = x_refs[r][...].astype(f32)
        normed = (x * rsq(x) * gain).astype(bf16)
        qkv = dot(normed, w_ref[...]).astype(bf16)
        for c in range(3 * groups):
            qkv_ref[c, pl.ds(start, tok), :] = qkv[:, c * LANES : (c + 1) * LANES]
    for g in range(groups):
        vt_scr[g * LANES : (g + 1) * LANES, :] = qkv_ref[2 * groups + g].astype(f32).T.astype(bf16)
    lse_ref[...] = jnp.zeros_like(lse_ref)

    def head_body(h, carry):
        g = lax.shift_right_logical(h, 1)
        half = jnp.bitwise_and(h, 1)
        lane = lax.broadcasted_iota(jnp.int32, (tok, LANES), 1)
        mine = lax.shift_right_logical(lane, 6) == half
        for j in range(n):
            lo = max(0, j - reach)
            q = qkv_ref[g, j * tok : (j + 1) * tok, :].astype(f32)
            q = jnp.where(mine, q * HD ** (-0.5), 0.0).astype(bf16)
            key = qkv_ref[groups + g, lo * tok : (j + 1) * tok, :]
            s = dot(key, q, NT)
            bias = jnp.concatenate([tiles_ref[h, j - b] for b in range(lo, j + 1)], axis=0)
            ok = kdoc_ref[lo * tok : (j + 1) * tok, :] == qdoc_ref[:, j * tok : (j + 1) * tok]
            s = jnp.where(ok, s + bias, MASKED)
            peak = jnp.max(s, axis=0, keepdims=True)
            e = jnp.exp(s - peak)
            total = jnp.sum(e, axis=0, keepdims=True)
            p = (e * (1.0 / total)).astype(bf16)
            lse_ref[pl.ds(h, 1), j * tok : (j + 1) * tok] = peak + jnp.log(total)
            vt = vt_scr[pl.ds(pl.multiple_of(h * HD, HD), HD), lo * tok : (j + 1) * tok]
            ot_scr[pl.ds(pl.multiple_of(h * HD, HD), HD), j * tok : (j + 1) * tok] = dot(vt, p)
        return carry

    lax.fori_loop(0, heads, head_body, 0)
    att_scr[...] = ot_scr[...].T.astype(bf16)
    for r in range(n):
        start = pl.multiple_of(jnp.bitwise_xor(me, r) * tok, tok)
        att_refs[r][...] = att_scr[pl.ds(start, tok), :part]


def unshear_rows(tile):
    rows = tile.shape[0]
    wide = jnp.concatenate([tile, jnp.zeros_like(tile)], axis=1)
    span = 2 * rows
    count = rows
    while count > 1:
        count //= 2
        wide = wide[:count] + pltpu.roll(wide[count : 2 * count], span - count, axis=1)
    return wide


def attn_bwd_kernel(
    n, reach, heads, first, after, idx_ref, gain_ref, w_ref, tiles_ref, kdoc_ref, qdoc_ref, qkv_ref, lse_ref, *rest
):
    x_refs, rest = rest[:n], rest[n:]
    da_refs, rest = rest[:n], rest[n:]
    if not first:
        old_small_ref, old_band_ref, *rest = rest
    rest = rest[after:]
    part_refs, rest = rest[:n], rest[n:]
    dqkv_ref, new_small_ref, new_band_ref, da_scr, kt_scr, dqt_scr, dkv_scr, acc_scr = rest
    tok = x_refs[0].shape[0]
    groups = qkv_ref.shape[0] // 3
    spans = tiles_ref.shape[1]
    wide = groups * LANES
    me = idx_ref[0]
    gain = gain_ref[...]
    if heads * HD < wide:
        da_scr[...] = jnp.zeros_like(da_scr)
    for r in range(n):
        start = pl.multiple_of(jnp.bitwise_xor(me, r) * tok, tok)
        for g in range(groups):
            cols = min(LANES, heads * HD - g * LANES)
            da_scr[g, pl.ds(start, tok), :cols] = da_refs[r][:, g * LANES : g * LANES + cols]
    for g in range(groups):
        kt_scr[g * LANES : (g + 1) * LANES, :] = qkv_ref[groups + g].astype(f32).T.astype(bf16)
    dkv_scr[...] = jnp.zeros_like(dkv_scr)
    dqt_scr[...] = jnp.zeros_like(dqt_scr)
    acc_scr[...] = jnp.zeros_like(acc_scr)

    def head_body(h, carry):
        g = lax.shift_right_logical(h, 1)
        half = jnp.bitwise_and(h, 1)
        lane = lax.broadcasted_iota(jnp.int32, (tok, LANES), 1)
        mine = lax.shift_right_logical(lane, 6) == half
        for j in range(n):
            lo = max(0, j - reach)
            rows = slice(lo * tok, (j + 1) * tok)
            cols = slice(j * tok, (j + 1) * tok)
            q = qkv_ref[g, cols, :].astype(f32)
            q = jnp.where(mine, q * HD ** (-0.5), 0.0).astype(bf16)
            da = jnp.where(mine, da_scr[g, cols, :].astype(f32), 0.0).astype(bf16)
            s = dot(qkv_ref[groups + g, rows, :], q, NT)
            bias = jnp.concatenate([tiles_ref[h, j - b] for b in range(lo, j + 1)], axis=0)
            ok = kdoc_ref[rows, :] == qdoc_ref[:, cols]
            s = jnp.where(ok, s + bias, MASKED)
            p = jnp.exp(s - lse_ref[pl.ds(h, 1), cols])
            pg = dot(qkv_ref[2 * groups + g, rows, :], da, NT)
            centre = jnp.sum(p * pg, axis=0, keepdims=True)
            sg = (p * (pg - centre)).astype(bf16)
            for b in range(lo, j + 1):
                acc_scr[h, j - b] += sg[(b - lo) * tok : (b - lo + 1) * tok].astype(f32)
            dkv_scr[g, rows, :] += dot(sg, q)
            dkv_scr[groups + g, rows, :] += dot(p.astype(bf16), da)
            at = pl.ds(pl.multiple_of(h * HD, HD), HD)
            dqt_scr[at, cols] = dot(kt_scr[at, rows], sg) * HD ** (-0.5)
        return carry

    lax.fori_loop(0, heads, head_body, 0)
    for g in range(groups):
        dqkv_ref[:, g * LANES : (g + 1) * LANES] = dqt_scr[g * LANES : (g + 1) * LANES, :].T.astype(bf16)
    for c in range(2 * groups):
        dqkv_ref[:, wide + c * LANES : wide + (c + 1) * LANES] = dkv_scr[c].astype(bf16)
    small = None
    for r in range(n):
        start = pl.multiple_of(jnp.bitwise_xor(me, r) * tok, tok)
        x = x_refs[r][...].astype(f32)
        part = dot(dqkv_ref[pl.ds(start, tok), :], w_ref[...], NT)
        part_refs[r][...] = part.astype(bf16)
        term = jnp.sum(part * (x * rsq(x)), axis=0, keepdims=True)
        small = term if small is None else small + term
    if not first:
        small = small + old_small_ref[...]
    new_small_ref[...] = small
    new_band_ref[...] = jnp.zeros_like(new_band_ref)
    for h in range(heads):
        lines = [unshear_rows(acc_scr[h, s]) for s in range(spans)]
        for s in range(spans):
            value = lines[s][:, :tok]
            if s + 1 < spans:
                value = value + lines[s + 1][:, tok:]
            if not first:
                value = value + old_band_ref[h : h + 1, s * tok : (s + 1) * tok]
            new_band_ref[h : h + 1, s * tok : (s + 1) * tok] = value


def qkv_grad_kernel(n, heads, own_rows, first, last, idx_ref, gain_ref, dqkv_ref, *rest):
    x_refs, rest = rest[:n], rest[n:]
    if not first:
        old_w_ref, *rest = rest
    if last:
        small_ref, band_ref, extra_ref, *rest = rest
    out_ref, normed_scr = rest[-2:]
    tok = x_refs[0].shape[0]
    for r in range(n):
        start = pl.multiple_of(jnp.bitwise_xor(idx_ref[0], r) * tok, tok)
        x = x_refs[r][...].astype(f32)
        normed_scr[pl.ds(start, tok), :] = (x * rsq(x) * gain_ref[...]).astype(bf16)
    new_w = dot(normed_scr[...], dqkv_ref[...], TN)
    if not first:
        new_w = new_w + old_w_ref[...]
    if not last:
        out_ref[...] = new_w
        return
    pack_grad(heads, new_w, small_ref[...], extra_ref[...], out_ref)
    packed = packed_blocks(heads) * LANES
    width, lanes = out_ref.shape
    span = min(band_ref.shape[1], WINDOW)
    pieces = [band_ref[h : h + 1, c : c + LANES] for h in range(heads) for c in range(0, span, LANES)]
    across = (lanes - packed) // LANES
    pieces += [jnp.zeros((1, LANES), f32)] * (own_rows * across - len(pieces))
    whole = jnp.concatenate(
        [jnp.concatenate(pieces[i * across : (i + 1) * across], axis=1) for i in range(own_rows)]
        + [jnp.zeros((-own_rows % 16, across * LANES), f32)][: 1 if own_rows % 16 else 0],
        axis=0,
    ).astype(bf16)
    shape = (width, whole.shape[0])
    row = lax.rem(lax.broadcasted_iota(jnp.int32, shape, 0), jnp.int32(own_rows))
    pick = jnp.where(row == lax.broadcasted_iota(jnp.int32, shape, 1), 1.0, 0.0).astype(bf16)
    out_ref[:, packed:] = dot(pick, whole).astype(bf16)


def head_rows(me, r, part, width, n):
    at = jnp.bitwise_xor(me, r) * part
    if n * part > width:
        at = jnp.minimum(at, width - part)
    return pl.ds(pl.multiple_of(at, HD), part)


def dense_gain(dense_ref):
    width = dense_ref.shape[1] - LANES
    return dense_ref[:, width:].astype(f32).T[LANES - 1 :]


def gates_of(normed, router, routes):
    logits = dot(normed, router)
    lane = lax.broadcasted_iota(jnp.int32, logits.shape, 1)
    route = [lane == routes[:, k : k + 1] for k in range(TOP)]
    chosen = [jnp.sum(jnp.where(r, logits, 0.0), axis=1, keepdims=True) for r in route]
    peak = jnp.maximum(chosen[0], chosen[1])
    powers = [jnp.exp(c - peak) for c in chosen]
    whole = powers[0] + powers[1]
    return route, [v / whole for v in powers]


def mid_kernel(n, first, idx_ref, x_ref, places_ref, *rest):
    att_refs, rest = rest[:n], rest[n:]
    tok, part = att_refs[0].shape
    width = x_ref.shape[-1]
    me = idx_ref[0]
    if first:
        share_refs = rest[:n]
        mixed_ref, rows_ref, dense_ref, whole_scr = rest[-4:]
        share = share_refs[0].shape[1]
        for r in range(n):
            at = pl.multiple_of(jnp.bitwise_xor(me, r) * share, LANES)
            whole_scr[:, pl.ds(at, share)] = share_refs[r][...]
        dense_ref[...] = whole_scr[:, : dense_ref.shape[1]]
    else:
        dense_ref, routes_ref, cot_ref = rest[:3]
        mixed_ref, rows_ref = rest[-2:]
    mixed = x_ref[...].astype(f32)
    for r in range(n):
        at = head_rows(me, r, part, width, n)
        mixed = mixed + dot(att_refs[r][...], dense_ref[at, :width])
    mixed_ref[...] = mixed
    normed = (mixed * rsq(mixed) * dense_gain(dense_ref)).astype(bf16)
    picks = pick_each(places_ref[...], rows_ref.shape[0])
    rows_ref[:, :width] = dot(sum(picks).astype(bf16), normed).astype(bf16)
    if not first:
        _, gates = gates_of(normed, dense_ref[:, width:], routes_ref[...])
        up = cot_ref[...].astype(f32)
        rows_ref[:, width:] = sum(
            dot(picks[k].astype(bf16), (gates[k] * up).astype(bf16)) for k in range(TOP)
        ).astype(bf16)


def expert_kernel(raw, capacity, padded, idx_ref, x_ref, c_ref, dense_ref, win_ref, wback_ref, *rest):
    out_ref, hid_ref, pre_ref, g_ref, acc_scr, grad_scr, *rest = rest
    f = pl.program_id(0)
    width = x_ref.shape[-1]

    @pl.when(f == 0)
    def _():
        acc_scr[...] = jnp.zeros_like(acc_scr)
        if not raw:
            grad_scr[...] = c_ref[...]
            return
        c_scr, ids_scr = rest
        up = -(-capacity // 8) * 8
        same = lax.broadcasted_iota(jnp.int32, (up, LANES), 0) == lax.broadcasted_iota(
            jnp.int32, (up, LANES), 1
        )
        for s in range(c_ref.shape[0] // padded):
            block = c_ref[s * padded : (s + 1) * padded, :].astype(f32)
            c_scr[s * capacity : (s + 1) * capacity, :] = block[:capacity]
            line = block[capacity : capacity + 1, :LANES]
            column = jnp.sum(jnp.where(same, line, 0.0), axis=1, keepdims=True)
            ids_scr[s * capacity : (s + 1) * capacity, 0:1] = column[:capacity]
        ids = ids_scr[:, 0:1].astype(jnp.int32)
        logits = dot(x_ref[...], dense_ref[...])
        lane = lax.broadcasted_iota(jnp.int32, logits.shape, 1)
        own = jnp.sum(jnp.where(lane == idx_ref[1], logits, 0.0), axis=1, keepdims=True)
        other = jnp.sum(jnp.where(lane == ids, logits, 0.0), axis=1, keepdims=True)
        peak = jnp.maximum(own, other)
        own = jnp.exp(own - peak)
        gate = own / (own + jnp.exp(other - peak))
        grad_scr[...] = (gate * c_scr[...]).astype(bf16)

    @pl.when(f == 0)
    def _():
        g_ref[...] = grad_scr[...]

    pre = dot(x_ref[...], win_ref[...])
    c0 = 0.7978845608028654
    square = pre * pre
    t = jnp.tanh(pre * (c0 + (c0 * 0.044715) * square))
    hidden = (0.5 * pre * (1.0 + t)).astype(bf16)
    hid_ref[...] = hidden
    slope = 0.5 * (1.0 + t) + 0.5 * pre * (1.0 - t * t) * (c0 + (3 * c0 * 0.044715) * square)
    acc_scr[:, :width] += dot(hidden, wback_ref[...])
    pre_grad = (dot(grad_scr[...], wback_ref[...], NT) * slope).astype(bf16)
    pre_ref[...] = pre_grad
    acc_scr[:, width:] += dot(pre_grad, win_ref[...], NT)

    @pl.when(f == pl.num_programs(0) - 1)
    def _():
        out_ref[...] = acc_scr[...].astype(bf16)


def grad_back_kernel(src_ref, h0_ref, h1_ref, g0_ref, g1_ref, *rest):
    out_ref = rest[-1]
    out_ref[...] = (dot(h0_ref[...], g0_ref[...], TN) + dot(h1_ref[...], g1_ref[...], TN)).astype(bf16)


def grad_in_kernel(pos_ref, x0_ref, x1_ref, p0_ref, p1_ref, keep_ref, send_ref):
    value = (dot(x0_ref[...], p0_ref[...], TN) + dot(x1_ref[...], p1_ref[...], TN)).astype(bf16)
    half, rows, _ = keep_ref.shape
    for b in range(2 * half):
        at = pos_ref[b]
        block = value[b * rows : (b + 1) * rows]

        @pl.when(at < half)
        def _():
            keep_ref[at] = block

        @pl.when(at >= half)
        def _():
            send_ref[at - half] = block


def combine_kernel(n, experts, first, after, idx_ref, back_ref, places_ref, routes_ref, mixed_ref, cot_ref, dense_ref, *rest):
    att_refs, rest = rest[:n], rest[n:]
    if not first:
        old_ref, *rest = rest
    rest = rest[after:]
    out_ref, mg_ref, branch_ref, new_ref, *da_refs = rest
    tok, part = att_refs[0].shape
    width = mixed_ref.shape[-1]
    total = back_ref.shape[0]
    gain = dense_gain(dense_ref)
    mixed = mixed_ref[...]
    rr = rsq(mixed)
    normed = (mixed * rr * gain).astype(bf16)
    router = dense_ref[:, width:]
    route, gates = gates_of(normed, router, routes_ref[...])
    slot = lax.broadcasted_iota(jnp.int32, (tok, total), 1)
    hits = [jnp.where(slot == places_ref[:, k : k + 1], 1.0, 0.0) for k in range(TOP)]
    results = back_ref[:, :width]
    returned = [dot(h.astype(bf16), results) for h in hits]
    moe = gates[0] * returned[0] + gates[1] * returned[1]
    out_ref[...] = (mixed + moe).astype(bf16)
    up = cot_ref[...].astype(f32)
    gate_grad = [jnp.sum(up * v, axis=1, keepdims=True) for v in returned]
    centre = gates[0] * gate_grad[0] + gates[1] * gate_grad[1]
    chosen_grad = [gates[k] * (gate_grad[k] - centre) for k in range(TOP)]
    logit_grad = jnp.where(route[0], chosen_grad[0], 0.0) + jnp.where(route[1], chosen_grad[1], 0.0)
    high = logit_grad.astype(bf16)
    low = (logit_grad - high.astype(f32)).astype(bf16)
    normed_grad = dot((hits[0] + hits[1]).astype(bf16), back_ref[:, width:])
    normed_grad = normed_grad + dot(high, router, NT) + dot(low, router, NT)
    router_grad = dot(normed, high, TN) + dot(normed, low, TN)
    scaled = mixed * rr
    gain_part = jnp.sum(normed_grad * scaled, axis=0, keepdims=True)
    ng = gain * normed_grad
    mixed_grad = up + rr * (ng - scaled * jnp.mean(ng * scaled, axis=-1, keepdims=True))
    mg_ref[...] = mixed_grad
    branch = mixed_grad.astype(bf16)
    gain_col = jnp.broadcast_to(gain_part, (LANES, width)).T
    lane = lax.broadcasted_iota(jnp.int32, gain_col.shape, 1)
    extra = jnp.where(lane == experts, gain_col, router_grad)
    if not first:
        extra = extra + old_ref[...]
    new_ref[...] = extra
    branch_ref[...] = branch
    for r in range(n):
        at = head_rows(idx_ref[0], r, part, width, n)
        da_refs[r][...] = dot(branch, dense_ref[at, :width], NT).astype(bf16)


def dense_grad_kernel(n, micros, idx_ref, *rest):
    out_ref, scr = rest[-2:]
    part = rest[1].shape[1]
    width = out_ref.shape[2]
    experts = out_ref.shape[0]
    rows = width // (n * experts)
    for r in range(n):
        at = head_rows(idx_ref[0], r, part, width, n)

        def add_grad(at=at, r=r):
            scr[at, :] = sum(
                dot(rest[m * (n + 1) + 1 + r][...], rest[m * (n + 1)][...], TN) for m in range(micros)
            )

        if n * part > width:
            pl.when(jnp.bitwise_xor(idx_ref[0], r) * part < width)(add_grad)
        else:
            add_grad()
    for e in range(experts):
        blocks = [scr[(d * experts + e) * rows : (d * experts + e + 1) * rows, :] for d in range(n)]
        out_ref[e] = jnp.concatenate(blocks, axis=0).astype(bf16)


def token_grad_kernel(count, x_ref, mg_ref, gain_ref, *rest):
    parts, out_ref = rest[:count], rest[-1]
    grad = parts[0][...].astype(f32)
    for p in parts[1:]:
        grad = grad + p[...].astype(f32)
    x = x_ref[...].astype(f32)
    r = rsq(x)
    scaled = x * r
    ng = gain_ref[...] * grad
    out_ref[...] = (
        mg_ref[...] + r * (ng - scaled * jnp.mean(ng * scaled, axis=-1, keepdims=True))
    ).astype(bf16)


def swap(x, axis, by):
    return lax.ppermute(x, axis, [(i, i ^ by) for i in range(lax.axis_size(axis))])


def exchange(x, axes):
    return lax.all_to_all(x, axes, split_axis=0, concat_axis=0, tiled=True)


def bit_reversed(n):
    bits = n.bit_length() - 1
    return [int(format(r, "b").zfill(bits)[::-1], 2) if bits else 0 for r in range(n)]


def halving_start(keep, send, axis):
    came = swap(send, axis, 1)
    half = keep.shape[0] // 2
    far = (keep[half:].astype(f32) + came[half:].astype(f32)).astype(bf16)
    return [keep[:half], came[:half]], far


def halving_end(terms, far, axis):
    by = 2
    while far.shape[0]:
        half = terms[0].shape[0] // 2
        terms = [t for t in terms] + [swap(far, axis, by)]
        far = sum(t[half:].astype(f32) for t in terms).astype(bf16) if half else far[:0]
        terms = [t[:half] for t in terms] if half else terms
        by *= 2
    return sum(t[0].astype(f32) for t in terms)


def bits_of(axis):
    return [1 << i for i in range(lax.axis_size(axis).bit_length() - 1)][::-1]


def upper_half(axis, by):
    return lax.rem(lax.div(lax.axis_index(axis), by), 2) == 1


def by_distance(x, axis, after=()):
    blocks = {0: x}
    by = lax.axis_size(axis) // 2
    while by:
        for r in list(blocks):
            blocks[r ^ by] = swap(blocks[r], axis, by)
        by //= 2
        if after and by:
            blocks.update({r: gate(b, *after) for r, b in blocks.items() if r})
            after = ()
    return [blocks[r] for r in range(len(blocks))]


def halving_terms(parts, axis):
    terms = {r: [p] for r, p in enumerate(parts)}
    total = parts[0]
    by = 1
    while by < len(parts):
        for r in [r for r in terms if r & by]:
            held = terms.pop(r)
            total = held[0] if len(held) == 1 else sum(t.astype(f32) for t in held).astype(bf16)
            terms[r ^ by].append(swap(total, axis, by))
        by *= 2
    return terms[0], total


def shards(
    tokens, doc_lengths, routes, slots, w_qkv, w_out, rel_bias, gain_attn, gain_ffn, w_router, w_in, w_back, cotangent
):
    micros, _, tok, width = tokens.shape
    n = lax.axis_size("dp")
    experts = lax.axis_size("expert")
    me = lax.axis_index("dp")
    my_expert = lax.axis_index("expert")
    reach = min((WINDOW - 2) // tok + 1, n - 1)
    spans = reach + 1
    capacity = (9 * tok * TOP + 8 * experts - 1) // (8 * experts)
    total = experts * capacity
    length = n * tok
    heads = -(-H // n)
    groups = -(-heads // 2)
    part = heads * HD
    wide = groups * LANES
    ff = w_in.shape[2]
    own_rows = w_qkv.shape[0]
    whole_count = n * experts
    both = ("dp", "expert")
    tokens, cotangent = tokens[:, 0], cotangent[:, 0]
    routes, slots = routes[:, 0], slots[:, 0]
    idx = jnp.stack([me, my_expert]).astype(jnp.int32)

    packed = packed_blocks(heads) * LANES
    share = dense_share(n, width)
    (columns,) = call(
        functools.partial(pack_kernel, n),
        [((whole_count, own_rows, packed + share), bf16)],
        "pack",
        arrays=[w_qkv, gain_attn[None], w_out, w_router, gain_ffn[None]],
    )
    w_mine = exchange(columns, both).reshape(width, packed + share)

    places = jnp.where(slots >= 0, routes * capacity + slots, total)
    places_row = places.transpose(0, 2, 1)
    padded = -(-(capacity + 1) // 8) * 8
    padded_places = jnp.where(slots[0] >= 0, routes[0] * padded + slots[0], experts * padded)
    (cot_rows,) = call(
        functools.partial(dispatch_kernel, capacity, padded),
        [((experts * padded, width), bf16)],
        "dispatch_cotangent",
        arrays=[padded_places.T, padded_places, routes[0, :, ::-1], (cotangent, 0)],
        after=[columns],
        flops=2 * total * tok * width,
    )

    bias = jnp.pad(rel_bias.astype(f32).T, ((0, heads * n - H), (0, 0)))
    bias = lax.dynamic_slice_in_dim(bias, me * heads, heads, 0)[:, : spans * tok]
    band = jnp.concatenate(
        [
            jnp.full((heads, tok), MASKED, f32),
            bias,
            jnp.full((heads, spans * tok - bias.shape[1]), MASKED, f32),
        ],
        axis=1,
    )
    band = jnp.pad(band, ((0, -heads % 8), (0, 0)))
    (tiles,) = call(
        functools.partial(tiles_kernel, spans, tok),
        [((heads, spans, tok, tok), f32)],
        "bias_tiles",
        arrays=[band],
        after=[columns],
    )
    doc_ends = jnp.cumsum(doc_lengths[:, 0], axis=-1)
    positions = jnp.arange(length, dtype=jnp.int32)
    docs = jnp.sum((doc_ends[:, None, :] <= positions[None, :, None]).astype(jnp.int32), axis=2)
    kdocs, qdocs = docs[:, :, None], docs[:, None, :]

    xs = by_distance(tokens, "dp", [cot_rows, tiles, kdocs])

    cot_rows = gate(cot_rows, w_mine, tiles, xs[-1], kdocs)
    cot_rows = exchange(cot_rows.reshape(experts, padded, width), "expert").reshape(-1, width)

    att = []
    saved = []
    pair_flops = 2 * heads * LANES * tok * tok * sum(min(j, reach) + 1 for j in range(n))
    w_heads = w_mine
    gain_a = None
    for m in range(micros):
        first = m == 0
        made = call(
            functools.partial(attn_fwd_kernel, n, reach, heads, first),
            [((tok, part), bf16)] * n
            + [((3 * groups, length, LANES), bf16), ((8, length), f32)]
            + ([((width, 3 * wide), bf16), ((1, width), f32)] if first else []),
            "attention_forward",
            smem=[idx],
            arrays=[
                w_heads,
                *([] if first else [gain_a]),
                tiles,
                (kdocs, m),
                (qdocs, m),
                *[(x, m) for x in xs],
            ],
            flops=2 * length * width * 3 * wide + 2 * pair_flops,
            scratch=[
                pltpu.VMEM((wide, length), bf16),
                pltpu.VMEM((wide, length), f32),
                pltpu.VMEM((length, wide), bf16),
            ],
        )
        att_m, (qkv, lse, *more) = made[:n], made[n:]
        if first:
            w_heads, gain_a = more
        att.append([att_m[0]] + [swap(att_m[r], "dp", r) for r in range(1, n)])
        saved.append((qkv, lse))

    shares = by_distance(w_mine[:, packed:], "dp", [saved[0][1]])
    mixed = []
    arrived = []
    dense = None
    for m in range(micros):
        first = m == 0
        mixed_m, rows, *more = call(
            functools.partial(mid_kernel, n, first),
            [((tok, width), f32), ((total, width if first else 2 * width), bf16)]
            + ([((width, width + LANES), bf16)] if first else []),
            "mix_and_dispatch",
            smem=[idx],
            arrays=[(tokens, m), (places_row, m), *att[m], *(shares if first else [dense, (routes, m), (cotangent, m)])],
            after=[cot_rows] if first else [],
            scratch=[pltpu.VMEM((width, n * share), bf16)] if first else [],
            flops=2 * tok * width * width + 2 * total * tok * width,
        )
        if first:
            (dense,) = more
        mixed.append(mixed_m)
        arrived.append(exchange(rows.reshape(experts, capacity, -1), "expert").reshape(total, -1))

    tile = 512
    results = []
    kept = []
    for m in range(micros):
        whole = lambda shape, c=0: pl.BlockSpec(shape, lambda f, c=c: (0, c))
        out, hid, pre, g = pl.pallas_call(
            functools.partial(expert_kernel, m == 0, capacity, padded),
            out_shape=[
                jax.ShapeDtypeStruct((total, 2 * width), bf16),
                jax.ShapeDtypeStruct((total, ff), bf16),
                jax.ShapeDtypeStruct((total, ff), bf16),
                jax.ShapeDtypeStruct((total, width), bf16),
            ],
            grid=(ff // tile,),
            in_specs=[
                pl.BlockSpec(memory_space=pltpu.SMEM),
                whole((total, width)),
                whole(cot_rows.shape) if m == 0 else whole((total, width), 1),
                whole((width, LANES), width // LANES),
                pl.BlockSpec((None, width, tile), lambda f: (0, 0, f)),
                pl.BlockSpec((None, tile, width), lambda f: (0, f, 0)),
            ],
            out_specs=[
                whole((total, 2 * width)),
                pl.BlockSpec((total, tile), lambda f: (0, f)),
                pl.BlockSpec((total, tile), lambda f: (0, f)),
                whole((total, width)),
            ],
            scratch_shapes=[
                pltpu.VMEM((total, 2 * width), f32),
                pltpu.VMEM((total, width), bf16),
            ]
            + ([pltpu.VMEM((total, width), f32), pltpu.VMEM((total, LANES), f32)] if m == 0 else []),
            compiler_params=pltpu.CompilerParams(vmem_limit_bytes=60 * MIB),
            cost_estimate=pl.CostEstimate(
                flops=8 * total * width * ff, transcendentals=total * ff, bytes_accessed=20 * MIB
            ),
            name="expert",
        )(idx, arrived[m], cot_rows if m == 0 else arrived[m], dense, w_in, w_back)
        results.append(out)
        kept.append((hid, pre, g))

    assert micros == 2
    reverse = jnp.asarray(bit_reversed(n), jnp.int32)
    nth = jnp.arange(n, dtype=jnp.int32)
    places_of = reverse[jnp.bitwise_xor(nth, me)]
    blocks_at = jnp.bitwise_xor(reverse, me)
    cols = ff // n
    cost = pl.CostEstimate(flops=2 * total * width * ff, transcendentals=0, bytes_accessed=6 * MIB)

    def grad_back_half(blocks, *after):
        return pl.pallas_call(
            grad_back_kernel,
            out_shape=jax.ShapeDtypeStruct((n // 2, cols, width), bf16),
            grid_spec=pltpu.PrefetchScalarGridSpec(
                num_scalar_prefetch=1,
                grid=(n // 2,),
                in_specs=[
                    pl.BlockSpec((total, cols), lambda b, src: (0, src[b])),
                    pl.BlockSpec((total, cols), lambda b, src: (0, src[b])),
                    pl.BlockSpec((total, width), lambda b, src: (0, 0)),
                    pl.BlockSpec((total, width), lambda b, src: (0, 0)),
                ]
                + [pl.BlockSpec(memory_space=pl.ANY)] * len(after),
                out_specs=pl.BlockSpec((None, cols, width), lambda b, src: (b, 0, 0)),
            ),
            compiler_params=pltpu.CompilerParams(vmem_limit_bytes=60 * MIB),
            cost_estimate=cost,
            name="grad_back",
        )(blocks, kept[0][0], kept[1][0], kept[0][2], kept[1][2], *after)

    half_block = pl.BlockSpec((n // 2, width // n, tile), lambda f, pos: (0, 0, f))
    in_keep, in_send = pl.pallas_call(
        grad_in_kernel,
        out_shape=[jax.ShapeDtypeStruct((n // 2, width // n, ff), bf16)] * 2,
        grid_spec=pltpu.PrefetchScalarGridSpec(
            num_scalar_prefetch=1,
            grid=(ff // tile,),
            in_specs=[
                pl.BlockSpec((total, width), lambda f, pos: (0, 0)),
                pl.BlockSpec((total, width), lambda f, pos: (0, 0)),
                pl.BlockSpec((total, tile), lambda f, pos: (0, f)),
                pl.BlockSpec((total, tile), lambda f, pos: (0, f)),
            ],
            out_specs=[half_block, half_block],
        ),
        compiler_params=pltpu.CompilerParams(vmem_limit_bytes=60 * MIB),
        cost_estimate=pl.CostEstimate(
            flops=4 * total * width * ff, transcendentals=0, bytes_accessed=12 * MIB
        ),
        name="grad_in",
    )(places_of, arrived[0], arrived[1], kept[0][1], kept[1][1])
    in_terms, in_far = halving_start(in_keep, in_send, "dp")
    back_send = grad_back_half(blocks_at[n // 2 :], in_keep)
    back_keep = grad_back_half(blocks_at[: n // 2], back_send)
    results[1] = gate(results[1], back_send)
    back = [
        exchange(r.reshape(experts, capacity, 2 * width), "expert").reshape(total, 2 * width) for r in results
    ]
    back_terms, back_far = halving_start(back_keep, back_send, "dp")

    out = token_grad = None
    dense_grad = []
    branches = []
    attn_grad = []
    grad_w = []
    across = -(-heads * min(spans * tok, WINDOW) // (own_rows * LANES)) * LANES
    for m in range(micros):
        first, last = m == 0, m == micros - 1
        after = [] if first else [grad_w[0], back_keep, grad_in]
        out, mixed_grad, branch, new_grad, *da = call(
            functools.partial(combine_kernel, n, experts, first, len(after) + (out is not None)),
            [
                ((micros, tok, width), bf16),
                ((tok, width), f32),
                ((tok, width), bf16),
                ((width, LANES), f32),
            ]
            + [((tok, part), bf16)] * n,
            "combine",
            smem=[idx],
            arrays=[
                back[m],
                (places, m),
                (routes, m),
                mixed[m],
                (cotangent, m),
                dense,
                *att[m],
                *dense_grad,
            ],
            after=after,
            flops=6 * total * tok * width + 4 * tok * width * width,
            out_micro=[(0, m, out)],
        )
        dense_grad = [new_grad]
        branches += [branch, *att[m]]
        da = [da[0]] + [swap(da[r], "dp", r) for r in range(1, n)]
        qkv, lse = saved[m]
        if first:
            far = gate(in_far, *da[1:])
            grad_in = halving_end(in_terms, far, "dp")
            after = [far]
        else:
            far = gate(back_far, *da[1:])
            grad_back = halving_end(back_terms, far, "dp")
            after = [far]
        made = call(
            functools.partial(attn_bwd_kernel, n, reach, heads, first, len(after)),
            [((tok, width), bf16)] * n
            + [((length, 3 * wide), bf16), ((1, width), f32), ((8, spans * tok), f32)],
            "attention_backward",
            smem=[idx],
            arrays=[
                gain_a,
                w_heads,
                tiles,
                (kdocs, m),
                (qdocs, m),
                qkv,
                lse,
                *[(x, m) for x in xs],
                *da,
                *attn_grad,
            ],
            after=after,
            flops=2 * length * width * 3 * wide + 5 * pair_flops,
            scratch=[
                pltpu.VMEM((groups, length, LANES), bf16),
                pltpu.VMEM((wide, length), bf16),
                pltpu.VMEM((wide, length), f32),
                pltpu.VMEM((2 * groups, length, LANES), f32),
                pltpu.VMEM((heads, spans, tok, tok), f32),
            ],
        )
        parts, (dqkv, *attn_grad) = made[:n], made[n:]
        summed, sent_last = halving_terms(parts, "dp")
        grad_w = call(
            functools.partial(qkv_grad_kernel, n, heads, own_rows, first, last),
            [((width, packed + across), bf16) if last else ((width, 3 * wide), f32)],
            "qkv_grad",
            smem=[idx],
            arrays=[gain_a, dqkv, *[(x, m) for x in xs], *grad_w, *([*attn_grad, *dense_grad] if last else [])],
            flops=2 * length * width * 3 * wide,
            scratch=[pltpu.VMEM((length, width), bf16)],
        )
        (token_grad,) = call(
            functools.partial(token_grad_kernel, len(summed)),
            [((micros, tok, width), bf16)],
            "token_grad",
            arrays=[(tokens, m), mixed_grad, gain_a, *summed],
            out_micro=[(0, m, token_grad)],
        )

    (dense_grad,) = call(
        functools.partial(dense_grad_kernel, n, micros),
        [((experts, n * own_rows, width), bf16)],
        "dense_grad",
        smem=[idx],
        arrays=branches,
        flops=2 * micros * tok * width * width,
        scratch=[pltpu.VMEM((width, width), f32)],
    )
    dense_came = exchange(dense_grad, "expert")
    message = gate(grad_w[0], dense_came, grad_back, sent_last)
    dense_sum = jnp.sum(dense_came.astype(f32), axis=0).astype(bf16).reshape(n, own_rows, width)
    dense_sum = gate(dense_sum, sent_last)
    mine = lambda r: lax.dynamic_index_in_dim(dense_sum, jnp.bitwise_xor(me, r), 0, keepdims=False)
    dense_terms, _ = halving_terms([mine(r) for r in range(n)], "dp")
    dense_sum = sum(t.astype(f32) for t in dense_terms)
    message = exchange(message.reshape(whole_count, own_rows, packed + across), both)
    grad_qkv, small, extra = call(
        functools.partial(finish_kernel, n),
        [((own_rows, 3 * width), f32), ((n, own_rows, across), f32), ((own_rows, LANES), f32)],
        "finish",
        arrays=[message],
    )
    _, gain_lane = gain_place(heads)
    span = min(spans * tok, WINDOW)
    grad_bias = small.reshape(n, own_rows * across)[:, : heads * span]
    grad_bias = grad_bias.reshape(n * heads, span)[:H].T
    grad_bias = jnp.pad(grad_bias, ((0, WINDOW - span), (0, 0)))
    return (
        out[:, None],
        token_grad[:, None],
        grad_qkv,
        dense_sum,
        grad_bias,
        extra[:, gain_lane],
        extra[:, gain_lane + 1 + experts],
        extra[:, gain_lane + 1 : gain_lane + 1 + experts],
        grad_in[None],
        grad_back[None],
    )


def solution(mesh):
    return jax.shard_map(
        shards,
        mesh=mesh,
        in_specs=(
            P(None, "expert", "dp", None),
            P(None, "expert", None),
            P(None, "expert", "dp", None),
            P(None, "expert", "dp", None),
            P(("dp", "expert"), None),
            P(("dp", "expert"), None),
            P(),
            P(("dp", "expert")),
            P(("dp", "expert")),
            P(("dp", "expert"), None),
            P("expert", None, None),
            P("expert", None, None),
            P(None, "expert", "dp", None),
        ),
        out_specs=(
            P(None, "expert", "dp", None),
            P(None, "expert", "dp", None),
            P(("dp", "expert"), None),
            P(("dp", "expert"), None),
            P(),
            P(("dp", "expert")),
            P(("dp", "expert")),
            P(("dp", "expert"), None),
            P("expert", "dp", None),
            P("expert", "dp", None),
        ),
        check_vma=False,
    )
```

```python
import functools

import jax
import jax.numpy as jnp
from jax import lax
from jax.experimental import pallas as pl
from jax.experimental.pallas import tpu as pltpu
from jax.sharding import PartitionSpec as P

H = 12
HD = 64
TOP = 2
WINDOW = 1024
EPSILON = 1e-06
MASKED = -1e30
LANES = 128

bf16 = jnp.bfloat16
f32 = jnp.float32
MIB = 1 << 20

NN = (((1,), (0,)), ((), ()))
NT = (((1,), (1,)), ((), ()))
TN = (((0,), (0,)), ((), ()))


def dot(a, b, dims=NN):
    return lax.dot_general(a, b, dims, preferred_element_type=f32)


def rsq(x):
    return lax.rsqrt(jnp.mean(x * x, axis=-1, keepdims=True) + EPSILON)


def call(kernel, outs, name, smem=(), arrays=(), after=(), flops=0, scratch=(), limit=60, out_micro=(), hbm=(), hbm_out=()):
    def spec(x):
        if isinstance(x, tuple):
            x, i = x
            return pl.BlockSpec((None,) + x.shape[1:], lambda _: (i,) + (0,) * (x.ndim - 1))
        return pl.BlockSpec(x.shape, lambda _: (0,) * x.ndim)

    arrays = list(arrays)
    given = [x[0] if isinstance(x, tuple) else x for x in arrays]
    micro_of = {k: i for k, i, _ in out_micro}
    olds = [(k, old) for k, _, old in out_micro if old is not None]

    def out_spec(k, s):
        if k in hbm_out:
            return pl.BlockSpec(memory_space=pl.ANY)
        if k in micro_of:
            return pl.BlockSpec((None,) + s[1:], lambda _: (micro_of[k],) + (0,) * (len(s) - 1))
        return pl.BlockSpec(s, lambda _: (0,) * len(s))

    after = list(hbm) + list(after) + [old for _, old in olds]
    aliases = {len(smem) + len(arrays) + len(after) - len(olds) + i: k for i, (k, _) in enumerate(olds)}
    size = lambda shape, dtype: int(jnp.dtype(dtype).itemsize * functools.reduce(lambda p, q: p * q, shape, 1))
    moved = sum(size(x.shape, x.dtype) for x in given) + sum(size(*o) for o in outs)
    return pl.pallas_call(
        kernel,
        grid=(1,),
        out_shape=[jax.ShapeDtypeStruct(s, d) for s, d in outs],
        in_specs=[pl.BlockSpec(memory_space=pltpu.SMEM)] * len(smem)
        + [spec(x) for x in arrays]
        + [pl.BlockSpec(memory_space=pl.ANY)] * len(after),
        out_specs=[out_spec(k, s) for k, (s, _) in enumerate(outs)],
        input_output_aliases=aliases,
        scratch_shapes=list(scratch),
        compiler_params=pltpu.CompilerParams(vmem_limit_bytes=limit * MIB),
        cost_estimate=pl.CostEstimate(flops=int(flops), transcendentals=0, bytes_accessed=moved),
        name=name,
    )(*smem, *given, *after)


def gate(x, *after):
    hbm = pl.BlockSpec(memory_space=pl.ANY)
    return pl.pallas_call(
        lambda *refs: None,
        out_shape=jax.ShapeDtypeStruct(x.shape, x.dtype),
        in_specs=[hbm] * (1 + len(after)),
        out_specs=hbm,
        input_output_aliases={0: 0},
        name="gate",
    )(x, *after)


def packed_blocks(heads):
    return 3 * (heads // 2) + (2 if heads % 2 else 1)


def gain_place(heads):
    return packed_blocks(heads) - 1, HD if heads % 2 else 0


def head_place(heads, kind, h):
    if heads % 2 and h == heads - 1:
        return 3 * (heads // 2) + kind // 2, kind % 2
    return 3 * (h // 2) + kind, h % 2


def low_lanes(shape):
    return lax.broadcasted_iota(jnp.int32, shape, 1) < HD


def move_half(block, source, target):
    return block if source == target else pltpu.roll(block, HD, axis=1)


def column_of(row):
    n = row.shape[1]
    same = lax.broadcasted_iota(jnp.int32, (n, n), 0) == lax.broadcasted_iota(jnp.int32, (n, n), 1)
    return jnp.sum(jnp.where(same, row, 0.0), axis=1, keepdims=True)


def dense_share(n, width):
    return -(-(width + LANES) // (n * LANES)) * LANES


def pack_kernel(n, w_ref, gain_ref, w_out_ref, router_ref, gain_ffn_ref, out_ref):
    count, rows, _ = out_ref.shape
    copies = count // n
    heads = -(-H // n)
    width = w_ref.shape[1] // 3
    low = low_lanes((rows, LANES))
    lane = lax.broadcasted_iota(jnp.int32, (rows, LANES), 1)
    gain = column_of(gain_ref[...].astype(f32))
    gain_block, gain_lane = gain_place(heads)
    for d in range(n):
        found = {}
        for kind in range(3):
            for h in range(heads):
                head = d * heads + h
                if head >= H:
                    continue
                block, half = head_place(heads, kind, h)
                column = kind * width + head * HD
                start = column // LANES * LANES
                piece = move_half(
                    w_ref[:, start : start + LANES].astype(f32), (column - start) // HD, half
                )
                found[block, half] = piece
        for block in range(packed_blocks(heads)):
            none = jnp.zeros((rows, LANES), f32)
            value = jnp.where(low, found.get((block, 0), none), found.get((block, 1), none))
            if block == gain_block:
                value = jnp.where(lane == gain_lane, gain, value)
            value = value.astype(bf16)
            for e in range(copies):
                out_ref[d * copies + e, :, block * LANES : (block + 1) * LANES] = value
    share = dense_share(n, width)
    gain = column_of(gain_ffn_ref[...].astype(f32))
    router = jnp.concatenate(
        [router_ref[...].astype(f32), jnp.zeros((rows, LANES - router_ref.shape[1]), f32)], axis=1
    )
    router = jnp.where(lane == LANES - 1, gain, router).astype(bf16)
    for d in range(n):
        for c in range(0, share, LANES):
            column = d * share + c
            if column < width:
                value = w_out_ref[:, column : column + LANES]
            elif column == width:
                value = router
            else:
                value = jnp.zeros((rows, LANES), bf16)
            at = packed_blocks(heads) * LANES + c
            for e in range(copies):
                out_ref[d * copies + e, :, at : at + LANES] = value


def unpack_qkv(heads, w_ref, w_scr):
    groups = -(-heads // 2)
    rows = w_ref.shape[0]
    low = low_lanes((rows, LANES))
    for kind in range(3):
        for g in range(groups):
            block, half = head_place(heads, kind, 2 * g)
            value = w_ref[:, block * LANES : (block + 1) * LANES]
            if 2 * g + 1 == heads:
                value = jnp.where(low, move_half(value.astype(f32), half, 0), 0.0).astype(bf16)
            at = (kind * groups + g) * LANES
            w_scr[:, at : at + LANES] = value
    block, lane = gain_place(heads)
    turned = w_ref[:, block * LANES : (block + 1) * LANES].astype(f32).T
    return turned[lane : lane + 1]


def pack_grad(heads, grad, gain_row, extra, out_ref):
    groups = -(-heads // 2)
    rows = grad.shape[0]
    low = low_lanes((rows, LANES))
    lane = lax.broadcasted_iota(jnp.int32, (rows, LANES), 1)
    part = lambda kind, g: grad[:, (kind * groups + g) * LANES : (kind * groups + g + 1) * LANES]
    blocks = [part(kind, g) for g in range(heads // 2) for kind in range(3)]
    if heads % 2:
        g = groups - 1
        blocks.append(jnp.where(low, part(0, g), pltpu.roll(part(1, g), HD, axis=1)))
        blocks.append(jnp.where(low, part(2, g), 0.0))
    else:
        blocks.append(jnp.zeros((rows, LANES), f32))
    gain_col = jnp.broadcast_to(gain_row, (LANES, rows)).T
    _, gain_lane = gain_place(heads)
    blocks[-1] = jnp.where(lane == gain_lane, gain_col, blocks[-1])
    blocks[-1] = jnp.where(lane > gain_lane, pltpu.roll(extra, gain_lane + 1, axis=1), blocks[-1])
    for i, block in enumerate(blocks):
        out_ref[:, i * LANES : (i + 1) * LANES] = block.astype(bf16)


def finish_kernel(n, across, message_ref, qkv_ref, bias_ref, router_ref, gain_ref, gain_ffn_ref, dense_ref):
    count, rows, lanes = message_ref.shape
    copies = count // n
    heads = -(-H // n)
    width = qkv_ref.shape[1] // 3
    packed = packed_blocks(heads) * LANES
    low = low_lanes((rows, LANES))
    sums = []
    gain_block, gain_lane = gain_place(heads)
    gain = None
    for d in range(n):
        total = message_ref[d * copies].astype(f32)
        for e in range(1, copies):
            total = total + message_ref[d * copies + e].astype(f32)
        sums.append(total)
        term = total[:, gain_block * LANES : (gain_block + 1) * LANES]
        gain = term if gain is None else gain + term
    count = router_ref.shape[1]
    router_ref[...] = gain[:, gain_lane + 1 : gain_lane + 1 + count]
    turned = jnp.concatenate([gain, jnp.zeros((-rows % 8, LANES), f32)], axis=0).T if rows % 8 else gain.T
    gain_ref[...] = turned[gain_lane : gain_lane + 1, :rows]
    gain_ffn_ref[...] = turned[gain_lane + 1 + count : gain_lane + 2 + count, :rows]
    wide = across // LANES
    lines = min(WINDOW, rows * across // heads) // LANES
    for c in range(lines):
        found = []
        for head in range(H):
            row, place = divmod(head % heads * lines + c, wide)
            at = packed + place * LANES
            found.append(sums[head // heads][row : row + 1, at : at + LANES])
        bias_ref[:, c * LANES : (c + 1) * LANES] = jnp.concatenate(found, axis=0)
    if lines * LANES < WINDOW:
        bias_ref[:, lines * LANES :] = jnp.zeros((H, WINDOW - lines * LANES), f32)
    half = dense_ref.shape[1] // 2
    for core in range(2):
        dense_ref[:, core * half : (core + 1) * half] = sum(t[:, lanes - half :] for t in sums[core::2])
    for kind in range(3):
        for pair in range(H // 2):
            halves = []
            for to in range(2):
                head = 2 * pair + to
                block, half = head_place(heads, kind, head % heads)
                value = sums[head // heads][:, block * LANES : (block + 1) * LANES]
                halves.append(move_half(value, half, to))
            at = kind * width + pair * LANES
            qkv_ref[:, at : at + LANES] = jnp.where(low, halves[0], halves[1])


def tiles_kernel(spans, rows, band_ref, *rest):
    out_ref = rest[-1]
    heads = out_ref.shape[0]
    for h in range(heads):
        for s in range(spans):
            ahead = band_ref[h : h + 1, (s + 1) * rows : (s + 2) * rows]
            behind = band_ref[h : h + 1, s * rows : (s + 1) * rows]
            line = jnp.concatenate([ahead, behind], axis=1)
            spread = jnp.broadcast_to(line, (rows, 2 * rows))
            rolled = pltpu.roll(spread, 0, axis=1, stride=1, stride_axis=0)
            out_ref[h, s] = rolled[:, :rows]


def pick_each(places, total):
    slot = lax.broadcasted_iota(jnp.int32, (total, places.shape[1]), 0)
    return [jnp.where(slot == places[k : k + 1], 1.0, 0.0) for k in range(TOP)]


def picks_of(places, total):
    return sum(pick_each(places, total)).astype(bf16)


def dispatch_kernel(capacity, padded, places_row_ref, places_ref, other_ref, cot_ref, after_ref, out_ref):
    tok = places_ref.shape[0]
    total, width = out_ref.shape
    experts = total // padded
    lane = lax.broadcasted_iota(jnp.int32, (tok, LANES), 1)
    lines = []
    for e in range(experts):
        slot = jnp.where(lane < capacity, lane + e * padded, -1)
        found = sum(
            jnp.where(slot == places_ref[:, k : k + 1], other_ref[:, k : k + 1].astype(f32), 0.0)
            for k in range(TOP)
        )
        lines.append(jnp.sum(found, axis=0, keepdims=True))
    spare = -experts % 16
    if spare:
        lines.append(jnp.zeros((spare, LANES), f32))
    lines = jnp.concatenate(lines, axis=0).astype(bf16)
    shape = (total, lines.shape[0])
    row = lax.broadcasted_iota(jnp.int32, shape, 0)
    here = row == lax.broadcasted_iota(jnp.int32, shape, 1) * padded + capacity
    ids = dot(jnp.where(here, 1.0, 0.0).astype(bf16), lines)
    rows = dot(picks_of(places_row_ref[...], total), cot_ref[...])
    out_ref[:, :LANES] = (rows[:, :LANES] + ids).astype(bf16)
    out_ref[:, LANES:] = rows[:, LANES:].astype(bf16)


def attn_fwd_kernel(n, reach, heads, first, idx_ref, w_ref, *rest):
    if not first:
        gain_ref, *rest = rest
    kdoc_ref, qdoc_ref, *rest = rest
    x_refs, rest = rest[:n], rest[n:]
    tiles_hbm, *rest = rest
    att_refs, rest = rest[:n], rest[n:]
    qkv_hbm, lse_ref, *rest = rest
    if first:
        heads_ref, gain_out_ref, *rest = rest
        gain = unpack_qkv(heads, w_ref, heads_ref)
        gain_out_ref[...] = gain
        w_ref = heads_ref
    else:
        gain = gain_ref[...]
    vt_scr, ot_scr, att_scr, tiles_ref, qkv_ref, tiles_sem, qkv_sem = rest
    tiles_copy = pltpu.make_async_copy(tiles_hbm, tiles_ref, tiles_sem)
    tiles_copy.start()
    tok = x_refs[0].shape[0]
    part = heads * HD
    groups = qkv_ref.shape[0] // 3
    me = idx_ref[0]
    for r in range(n):
        start = pl.multiple_of(jnp.bitwise_xor(me, r) * tok, tok)
        x = x_refs[r][...].astype(f32)
        normed = (x * rsq(x) * gain).astype(bf16)
        qkv = dot(normed, w_ref[...]).astype(bf16)
        for c in range(3 * groups):
            qkv_ref[c, pl.ds(start, tok), :] = qkv[:, c * LANES : (c + 1) * LANES]
    for g in range(groups):
        vt_scr[g * LANES : (g + 1) * LANES, :] = qkv_ref[2 * groups + g].astype(f32).T.astype(bf16)
    lse_ref[...] = jnp.zeros_like(lse_ref)
    qkv_copy = pltpu.make_async_copy(qkv_ref, qkv_hbm, qkv_sem)
    qkv_copy.start()
    tiles_copy.wait()

    lane = lax.broadcasted_iota(jnp.int32, (tok, LANES), 1)
    halves = [lane < HD, lane >= HD]

    def scores(h, j):
        lo = max(0, j - reach)
        q = qkv_ref[h // 2, j * tok : (j + 1) * tok, :].astype(f32)
        q = jnp.where(halves[h % 2], q * HD ** (-0.5), 0.0).astype(bf16)
        return dot(qkv_ref[groups + h // 2, lo * tok : (j + 1) * tok, :], q, NT)

    def attend(h, j, s):
        lo = max(0, j - reach)
        rows, cols = slice(lo * tok, (j + 1) * tok), slice(j * tok, (j + 1) * tok)
        bias = jnp.concatenate([tiles_ref[h, j - b] for b in range(lo, j + 1)], axis=0)
        s = jnp.where(kdoc_ref[rows, :] == qdoc_ref[:, cols], s + bias, MASKED)
        peak = jnp.max(s, axis=0, keepdims=True)
        e = jnp.exp(s - peak)
        total = jnp.sum(e, axis=0, keepdims=True)
        p = (e * (1.0 / total)).astype(bf16)
        lse_ref[h : h + 1, cols] = peak + jnp.log(total)
        return p

    def values(h, j, p):
        lo = max(0, j - reach)
        rows, cols = slice(lo * tok, (j + 1) * tok), slice(j * tok, (j + 1) * tok)
        ot_scr[h * HD : (h + 1) * HD, cols] = dot(vt_scr[h * HD : (h + 1) * HD, rows], p)

    work = [(h, j) for h in range(heads) for j in range(n)]
    ahead = scores(*work[0])
    for i, at in enumerate(work):
        s = ahead
        if i + 1 < len(work):
            ahead = scores(*work[i + 1])
        now = (*at, attend(*at, s))
        if i:
            values(*late)
        late = now
    values(*late)
    att_scr[...] = ot_scr[...].T.astype(bf16)
    for r in range(n):
        start = pl.multiple_of(jnp.bitwise_xor(me, r) * tok, tok)
        att_refs[r][...] = att_scr[pl.ds(start, tok), :part]
    qkv_copy.wait()


def unshear(tiles):
    rows = tiles[0].shape[0]
    span = 2 * rows
    wide = [jnp.concatenate([t, jnp.zeros_like(t)], axis=1) for t in tiles]
    count = rows
    while count > 8:
        count //= 2
        wide = [w[:count] + pltpu.roll(w[count:], span - count, axis=1) for w in wide]
    wide = jnp.concatenate(wide, axis=0)
    row = lax.broadcasted_iota(jnp.int32, wide.shape, 0)
    for bit in (4, 2, 1):
        wide = jnp.where(jnp.bitwise_and(row, bit) > 0, pltpu.roll(wide, span - bit, axis=1), wide)
    return [
        jnp.sum(wide[i * count : (i + 1) * count], axis=0, keepdims=True) for i in range(len(tiles))
    ]


def attn_bwd_kernel(
    n, reach, heads, first, after, idx_ref, kdoc_ref, qdoc_ref, qkv_ref, lse_ref, *rest
):
    da_refs, rest = rest[:n], rest[n:]
    if not first:
        old_small_ref, old_band_ref, *rest = rest
    tiles_hbm, w_hbm, *rest = rest
    x_hbms, rest = rest[:n], rest[n + after :]
    part_refs, rest = rest[:n], rest[n:]
    dqkv_ref, new_small_ref, new_band_ref, da_scr, kt_scr, dqt_scr, dkv_scr, acc_scr, *rest = rest
    tiles_ref, w_ref, x_scr, tiles_sem, w_sem, *x_sems = rest
    tiles_copy = pltpu.make_async_copy(tiles_hbm, tiles_ref, tiles_sem)
    tiles_copy.start()
    late_copies = [pltpu.make_async_copy(w_hbm, w_ref, w_sem)]
    late_copies += [
        pltpu.make_async_copy(x_hbms[r], x_scr.at[r], x_sems[r]) for r in range(n)
    ]
    tok = da_refs[0].shape[0]
    groups = qkv_ref.shape[0] // 3
    spans = tiles_ref.shape[1]
    wide = groups * LANES
    me = idx_ref[0]
    if heads * HD < wide:
        da_scr[...] = jnp.zeros_like(da_scr)
    for r in range(n):
        start = pl.multiple_of(jnp.bitwise_xor(me, r) * tok, tok)
        for g in range(groups):
            cols = min(LANES, heads * HD - g * LANES)
            da_scr[g, pl.ds(start, tok), :cols] = da_refs[r][:, g * LANES : g * LANES + cols]
    for g in range(groups):
        kt_scr[g * LANES : (g + 1) * LANES, :] = qkv_ref[groups + g].astype(f32).T.astype(bf16)
    dkv_scr[...] = jnp.zeros_like(dkv_scr)
    dqt_scr[...] = jnp.zeros_like(dqt_scr)
    acc_scr[...] = jnp.zeros_like(acc_scr)
    tiles_copy.wait()
    for copy in late_copies:
        copy.start()

    lane = lax.broadcasted_iota(jnp.int32, (tok, LANES), 1)
    halves = [lane < HD, lane >= HD]

    def places(j):
        lo = max(0, j - reach)
        return lo, slice(lo * tok, (j + 1) * tok), slice(j * tok, (j + 1) * tok)

    def products(h, j):
        _, rows, cols = places(j)
        q = qkv_ref[h // 2, cols, :].astype(f32)
        q = jnp.where(halves[h % 2], q * HD ** (-0.5), 0.0).astype(bf16)
        da = jnp.where(halves[h % 2], da_scr[h // 2, cols, :].astype(f32), 0.0).astype(bf16)
        s = dot(qkv_ref[groups + h // 2, rows, :], q, NT)
        return q, da, s, dot(qkv_ref[2 * groups + h // 2, rows, :], da, NT)

    def score_grads(h, j, s, pg):
        lo, rows, cols = places(j)
        bias = jnp.concatenate([tiles_ref[h, j - b] for b in range(lo, j + 1)], axis=0)
        s = jnp.where(kdoc_ref[rows, :] == qdoc_ref[:, cols], s + bias, MASKED)
        p = jnp.exp(s - lse_ref[h : h + 1, cols])
        centre = jnp.sum(p * pg, axis=0, keepdims=True)
        sg = (p * (pg - centre)).astype(bf16)
        for b in range(lo, j + 1):
            acc_scr[h, j - b] += sg[(b - lo) * tok : (b - lo + 1) * tok].astype(f32)
        return p.astype(bf16), sg

    def gather(h, j, q, da, p, sg):
        _, rows, cols = places(j)
        dkv_scr[h // 2, rows, :] += dot(sg, q)
        dkv_scr[groups + h // 2, rows, :] += dot(p, da)
        at = slice(h * HD, (h + 1) * HD)
        dqt_scr[at, cols] = dot(kt_scr[at, rows], sg) * HD ** (-0.5)

    work = [(h, j) for h in range(heads) for j in range(n)]
    ahead = products(*work[0])
    for i, at in enumerate(work):
        q, da, s, pg = ahead
        if i + 1 < len(work):
            ahead = products(*work[i + 1])
        now = (*at, q, da, *score_grads(*at, s, pg))
        if i:
            gather(*late)
        late = now
    gather(*late)
    for g in range(groups):
        dqkv_ref[:, g * LANES : (g + 1) * LANES] = dqt_scr[g * LANES : (g + 1) * LANES, :].T.astype(bf16)
    for c in range(2 * groups):
        dqkv_ref[:, wide + c * LANES : wide + (c + 1) * LANES] = dkv_scr[c].astype(bf16)
    small = None
    for copy in late_copies:
        copy.wait()
    for r in range(n):
        start = pl.multiple_of(jnp.bitwise_xor(me, r) * tok, tok)
        x = x_scr[r].astype(f32)
        part = dot(dqkv_ref[pl.ds(start, tok), :], w_ref[...], NT)
        part_refs[r][...] = part.astype(bf16)
        term = jnp.sum(part * (x * rsq(x)), axis=0, keepdims=True)
        small = term if small is None else small + term
    if not first:
        small = small + old_small_ref[...]
    new_small_ref[...] = small
    new_band_ref[...] = jnp.zeros_like(new_band_ref)
    lines = unshear([acc_scr[h, s] for h in range(heads) for s in range(spans)])
    for h in range(heads):
        for s in range(spans):
            value = lines[h * spans + s][:, :tok]
            if s + 1 < spans:
                value = value + lines[h * spans + s + 1][:, tok:]
            if not first:
                value = value + old_band_ref[h : h + 1, s * tok : (s + 1) * tok]
            new_band_ref[h : h + 1, s * tok : (s + 1) * tok] = value


def qkv_grad_kernel(n, heads, own_rows, first, last, after, idx_ref, gain_ref, dqkv_ref, *rest):
    x_refs, rest = rest[:n], rest[n:]
    if not first:
        old_w_ref, *rest = rest
    if last:
        small_ref, band_ref, extra_ref, dense_ref, came_ref, *rest = rest
    rest = rest[after:]
    out_ref, normed_scr = rest[-2:]
    tok = x_refs[0].shape[0]
    for r in range(n):
        start = pl.multiple_of(jnp.bitwise_xor(idx_ref[0], r) * tok, tok)
        x = x_refs[r][...].astype(f32)
        normed_scr[pl.ds(start, tok), :] = (x * rsq(x) * gain_ref[...]).astype(bf16)
    new_w = dot(normed_scr[...], dqkv_ref[...], TN)
    if not first:
        new_w = new_w + old_w_ref[...]
    if not last:
        out_ref[...] = new_w
        return
    pack_grad(heads, new_w, small_ref[...], extra_ref[...], out_ref)
    packed = packed_blocks(heads) * LANES
    width, lanes = out_ref.shape
    span = min(band_ref.shape[1], WINDOW)
    pieces = [band_ref[h : h + 1, c : c + LANES] for h in range(heads) for c in range(0, span, LANES)]
    dense = dense_ref.shape[1]
    out_ref[:, lanes - dense :] = (dense_ref[...].astype(f32) + came_ref[...].astype(f32)).astype(bf16)
    across = (lanes - packed - dense) // LANES
    pieces += [jnp.zeros((1, LANES), f32)] * (own_rows * across - len(pieces))
    whole = jnp.concatenate(
        [jnp.concatenate(pieces[i * across : (i + 1) * across], axis=1) for i in range(own_rows)]
        + [jnp.zeros((-own_rows % 16, across * LANES), f32)][: 1 if own_rows % 16 else 0],
        axis=0,
    ).astype(bf16)
    shape = (width, whole.shape[0])
    row = lax.rem(lax.broadcasted_iota(jnp.int32, shape, 0), jnp.int32(own_rows))
    pick = jnp.where(row == lax.broadcasted_iota(jnp.int32, shape, 1), 1.0, 0.0).astype(bf16)
    out_ref[:, packed : lanes - dense] = dot(pick, whole).astype(bf16)


def head_rows(me, r, part, width, n):
    at = jnp.bitwise_xor(me, r) * part
    if n * part > width:
        at = jnp.minimum(at, width - part)
    return pl.ds(pl.multiple_of(at, HD), part)


def dense_gain(dense_ref):
    width = dense_ref.shape[1] - LANES
    return dense_ref[:, width:].astype(f32).T[LANES - 1 :]


def gates_of(normed, router, routes):
    logits = dot(normed, router)
    lane = lax.broadcasted_iota(jnp.int32, logits.shape, 1)
    route = [lane == routes[:, k : k + 1] for k in range(TOP)]
    chosen = [jnp.sum(jnp.where(r, logits, 0.0), axis=1, keepdims=True) for r in route]
    peak = jnp.maximum(chosen[0], chosen[1])
    powers = [jnp.exp(c - peak) for c in chosen]
    whole = powers[0] + powers[1]
    return route, [v / whole for v in powers]


def mid_kernel(n, first, idx_ref, x_ref, places_ref, *rest):
    att_refs, rest = rest[:n], rest[n:]
    tok, part = att_refs[0].shape
    width = x_ref.shape[-1]
    me = idx_ref[0]
    if first:
        share_refs = rest[:n]
        mixed_ref, rows_ref, dense_ref, whole_scr = rest[-4:]
        share = share_refs[0].shape[1]
        for r in range(n):
            at = pl.multiple_of(jnp.bitwise_xor(me, r) * share, LANES)
            whole_scr[:, pl.ds(at, share)] = share_refs[r][...]
        dense_ref[...] = whole_scr[:, : dense_ref.shape[1]]
    else:
        dense_ref, routes_ref, cot_ref = rest[:3]
        mixed_ref, rows_ref = rest[-2:]
    mixed = x_ref[...].astype(f32)
    for r in range(n):
        at = head_rows(me, r, part, width, n)
        mixed = mixed + dot(att_refs[r][...], dense_ref[at, :width])
    mixed_ref[...] = mixed
    normed = (mixed * rsq(mixed) * dense_gain(dense_ref)).astype(bf16)
    picks = pick_each(places_ref[...], rows_ref.shape[0])
    rows_ref[:, :width] = dot(sum(picks).astype(bf16), normed).astype(bf16)
    if not first:
        _, gates = gates_of(normed, dense_ref[:, width:], routes_ref[...])
        up = cot_ref[...].astype(f32)
        rows_ref[:, width:] = sum(
            dot(picks[k].astype(bf16), (gates[k] * up).astype(bf16)) for k in range(TOP)
        ).astype(bf16)


def expert_kernel(raw, capacity, padded, src_ref, pos_ref, idx_ref, x_ref, c_ref, dense_ref, win_ref, wback_ref, *rest):
    if raw:
        out_ref, in_ref, back_ref, acc_scr, grad_scr, *rest = rest
    else:
        old_in_ref, old_back_ref, out_ref, in_keep_ref, in_send_ref, back_keep_ref, back_send_ref = rest[:7]
        acc_scr, grad_scr = rest[7:]
    f = pl.program_id(0)
    width = x_ref.shape[-1]

    @pl.when(f == 0)
    def _():
        acc_scr[...] = jnp.zeros_like(acc_scr)
        if not raw:
            grad_scr[...] = c_ref[...]
            return
        c_scr, ids_scr = rest
        up = -(-capacity // 8) * 8
        same = lax.broadcasted_iota(jnp.int32, (up, LANES), 0) == lax.broadcasted_iota(
            jnp.int32, (up, LANES), 1
        )
        for s in range(c_ref.shape[0] // padded):
            block = c_ref[s * padded : (s + 1) * padded, :].astype(f32)
            c_scr[s * capacity : (s + 1) * capacity, :] = block[:capacity]
            line = block[capacity : capacity + 1, :LANES]
            column = jnp.sum(jnp.where(same, line, 0.0), axis=1, keepdims=True)
            ids_scr[s * capacity : (s + 1) * capacity, 0:1] = column[:capacity]
        ids = ids_scr[:, 0:1].astype(jnp.int32)
        logits = dot(x_ref[...], dense_ref[...])
        lane = lax.broadcasted_iota(jnp.int32, logits.shape, 1)
        own = jnp.sum(jnp.where(lane == idx_ref[1], logits, 0.0), axis=1, keepdims=True)
        other = jnp.sum(jnp.where(lane == ids, logits, 0.0), axis=1, keepdims=True)
        peak = jnp.maximum(own, other)
        own = jnp.exp(own - peak)
        gate = own / (own + jnp.exp(other - peak))
        grad_scr[...] = (gate * c_scr[...]).astype(bf16)

    pre = dot(x_ref[...], win_ref[...])
    c0 = 0.7978845608028654
    square = pre * pre
    t = jnp.tanh(pre * (c0 + (c0 * 0.044715) * square))
    hidden = (0.5 * pre * (1.0 + t)).astype(bf16)
    slope = 0.5 * (1.0 + t) + 0.5 * pre * (1.0 - t * t) * (c0 + (3 * c0 * 0.044715) * square)
    acc_scr[:, :width] += dot(hidden, wback_ref[...])
    pre_grad = (dot(grad_scr[...], wback_ref[...], NT) * slope).astype(bf16)
    acc_scr[:, width:] += dot(pre_grad, win_ref[...], NT)
    grad_in = dot(x_ref[...], pre_grad, TN)
    grad_back = dot(hidden, grad_scr[...], TN)
    if raw:
        in_ref[...] = grad_in.astype(bf16)
        back_ref[...] = grad_back.astype(bf16)
    else:
        grad_in = (grad_in + old_in_ref[...].astype(f32)).astype(bf16)
        grad_back = (grad_back + old_back_ref[...].astype(f32)).astype(bf16)
        half, rows, _ = in_keep_ref.shape
        for b in range(2 * half):
            at = pos_ref[b]
            block = grad_in[b * rows : (b + 1) * rows]

            @pl.when(at < half)
            def _():
                in_keep_ref[at] = block

            @pl.when(at >= half)
            def _():
                in_send_ref[at - half] = block

        @pl.when(f < half)
        def _():
            back_send_ref[...] = grad_back

        @pl.when(f >= half)
        def _():
            back_keep_ref[...] = grad_back

    @pl.when(f == pl.num_programs(0) - 1)
    def _():
        out_ref[...] = acc_scr[...].astype(bf16)


def combine_kernel(n, experts, first, after, idx_ref, back_ref, places_ref, routes_ref, mixed_ref, cot_ref, dense_ref, *rest):
    att_refs, rest = rest[:n], rest[n:]
    if not first:
        old_ref, *rest = rest
    rest = rest[after:]
    out_ref, mg_ref, branch_ref, new_ref, *da_refs = rest
    tok, part = att_refs[0].shape
    width = mixed_ref.shape[-1]
    total = back_ref.shape[0]
    gain = dense_gain(dense_ref)
    mixed = mixed_ref[...]
    rr = rsq(mixed)
    normed = (mixed * rr * gain).astype(bf16)
    router = dense_ref[:, width:]
    route, gates = gates_of(normed, router, routes_ref[...])
    slot = lax.broadcasted_iota(jnp.int32, (tok, total), 1)
    hits = [jnp.where(slot == places_ref[:, k : k + 1], 1.0, 0.0) for k in range(TOP)]
    results = back_ref[:, :width]
    returned = [dot(h.astype(bf16), results) for h in hits]
    moe = gates[0] * returned[0] + gates[1] * returned[1]
    out_ref[...] = (mixed + moe).astype(bf16)
    up = cot_ref[...].astype(f32)
    gate_grad = [jnp.sum(up * v, axis=1, keepdims=True) for v in returned]
    centre = gates[0] * gate_grad[0] + gates[1] * gate_grad[1]
    chosen_grad = [gates[k] * (gate_grad[k] - centre) for k in range(TOP)]
    logit_grad = jnp.where(route[0], chosen_grad[0], 0.0) + jnp.where(route[1], chosen_grad[1], 0.0)
    high = logit_grad.astype(bf16)
    low = (logit_grad - high.astype(f32)).astype(bf16)
    normed_grad = dot((hits[0] + hits[1]).astype(bf16), back_ref[:, width:])
    normed_grad = normed_grad + dot(high, router, NT) + dot(low, router, NT)
    router_grad = dot(normed, high, TN) + dot(normed, low, TN)
    scaled = mixed * rr
    gain_part = jnp.sum(normed_grad * scaled, axis=0, keepdims=True)
    ng = gain * normed_grad
    mixed_grad = up + rr * (ng - scaled * jnp.mean(ng * scaled, axis=-1, keepdims=True))
    mg_ref[...] = mixed_grad
    branch = mixed_grad.astype(bf16)
    gain_col = jnp.broadcast_to(gain_part, (LANES, width)).T
    lane = lax.broadcasted_iota(jnp.int32, gain_col.shape, 1)
    extra = jnp.where(lane == experts, gain_col, router_grad)
    if not first:
        extra = extra + old_ref[...]
    new_ref[...] = extra
    branch_ref[...] = branch
    for r in range(n):
        at = head_rows(idx_ref[0], r, part, width, n)
        da_refs[r][...] = dot(branch, dense_ref[at, :width], NT).astype(bf16)


def dense_grad_kernel(n, micros, idx_ref, *rest):
    keep_ref, send_ref, scr = rest[-3:]
    part = rest[1].shape[1]
    width, half = keep_ref.shape[0], keep_ref.shape[1]
    for r in range(n):
        at = head_rows(idx_ref[0], r, part, width, n)

        def add_grad(at=at, r=r):
            scr[at, :] = sum(
                dot(rest[m * (n + 1) + 1 + r][...], rest[m * (n + 1)][...], TN) for m in range(micros)
            )

        if n * part > width:
            pl.when(jnp.bitwise_xor(idx_ref[0], r) * part < width)(add_grad)
        else:
            add_grad()
    upper = jnp.bitwise_and(idx_ref[0], 1) == 1
    low, high = scr[:, :half], scr[:, half:]
    keep_ref[...] = jnp.where(upper, high, low).astype(bf16)
    send_ref[...] = jnp.where(upper, low, high).astype(bf16)


def token_grad_kernel(count, x_ref, mg_ref, gain_ref, *rest):
    parts, out_ref = rest[:count], rest[-1]
    grad = parts[0][...].astype(f32)
    for p in parts[1:]:
        grad = grad + p[...].astype(f32)
    x = x_ref[...].astype(f32)
    r = rsq(x)
    scaled = x * r
    ng = gain_ref[...] * grad
    out_ref[...] = (
        mg_ref[...] + r * (ng - scaled * jnp.mean(ng * scaled, axis=-1, keepdims=True))
    ).astype(bf16)


def swap(x, axis, by):
    return lax.ppermute(x, axis, [(i, i ^ by) for i in range(lax.axis_size(axis))])


def exchange(x, axes):
    return lax.all_to_all(x, axes, split_axis=0, concat_axis=0, tiled=True)


def bit_reversed(n):
    bits = n.bit_length() - 1
    return [int(format(r, "b").zfill(bits)[::-1], 2) if bits else 0 for r in range(n)]


def halving_start(keep, send, axis):
    came = swap(send, axis, 1)
    half, rows = keep.shape[0] // 2, keep.shape[1] // 2
    pieces = []
    for piece in (slice(0, rows), slice(rows, None)):
        far = (keep[half:, piece].astype(f32) + came[half:, piece].astype(f32)).astype(bf16)
        pieces.append(([keep[:half, piece], came[:half, piece]], far))
    return pieces


def halving_end(terms, far, axis):
    by = 2
    while True:
        half = terms[0].shape[0] // 2
        came = swap(far, axis, by)
        terms = terms + [came]
        if not half:
            return sum(t[0].astype(f32) for t in terms), came
        far = sum(t[half:].astype(f32) for t in terms).astype(bf16)
        terms = [t[:half] for t in terms]
        by *= 2


def bits_of(axis):
    return [1 << i for i in range(lax.axis_size(axis).bit_length() - 1)][::-1]


def upper_half(axis, by):
    return lax.rem(lax.div(lax.axis_index(axis), by), 2) == 1


def by_distance(x, axis, after=()):
    blocks = {0: x}
    by = lax.axis_size(axis) // 2
    while by:
        for r in list(blocks):
            blocks[r ^ by] = swap(blocks[r], axis, by)
        by //= 2
        if after and by:
            blocks.update({r: gate(b, *after) for r, b in blocks.items() if r})
            after = ()
    return [blocks[r] for r in range(len(blocks))]


def halving_terms(parts, axis):
    terms = {r: [p] for r, p in enumerate(parts)}
    total = parts[0]
    by = 1
    while by < len(parts):
        for r in [r for r in terms if r & by]:
            held = terms.pop(r)
            total = held[0] if len(held) == 1 else sum(t.astype(f32) for t in held).astype(bf16)
            terms[r ^ by].append(swap(total, axis, by))
        by *= 2
    return terms[0], total


def shards(
    tokens, doc_lengths, routes, slots, w_qkv, w_out, rel_bias, gain_attn, gain_ffn, w_router, w_in, w_back, cotangent
):
    micros, _, tok, width = tokens.shape
    n = lax.axis_size("dp")
    experts = lax.axis_size("expert")
    me = lax.axis_index("dp")
    my_expert = lax.axis_index("expert")
    reach = min((WINDOW - 2) // tok + 1, n - 1)
    spans = reach + 1
    capacity = (9 * tok * TOP + 8 * experts - 1) // (8 * experts)
    total = experts * capacity
    length = n * tok
    heads = -(-H // n)
    groups = -(-heads // 2)
    part = heads * HD
    wide = groups * LANES
    ff = w_in.shape[2]
    own_rows = w_qkv.shape[0]
    whole_count = n * experts
    both = ("dp", "expert")
    tokens, cotangent = tokens[:, 0], cotangent[:, 0]
    routes, slots = routes[:, 0], slots[:, 0]
    idx = jnp.stack([me, my_expert]).astype(jnp.int32)

    packed = packed_blocks(heads) * LANES
    share = dense_share(n, width)
    (columns,) = call(
        functools.partial(pack_kernel, n),
        [((whole_count, own_rows, packed + share), bf16)],
        "pack",
        arrays=[w_qkv, gain_attn[None], w_out, w_router, gain_ffn[None]],
    )
    w_mine = exchange(columns, both).reshape(width, packed + share)

    places = jnp.where(slots >= 0, routes * capacity + slots, total)
    places_row = places.transpose(0, 2, 1)
    padded = -(-(capacity + 1) // 8) * 8
    padded_places = jnp.where(slots[0] >= 0, routes[0] * padded + slots[0], experts * padded)
    (cot_rows,) = call(
        functools.partial(dispatch_kernel, capacity, padded),
        [((experts * padded, width), bf16)],
        "dispatch_cotangent",
        arrays=[padded_places.T, padded_places, routes[0, :, ::-1], (cotangent, 0)],
        after=[columns],
        flops=2 * total * tok * width,
    )

    bias = jnp.pad(rel_bias.astype(f32).T, ((0, heads * n - H), (0, 0)))
    bias = lax.dynamic_slice_in_dim(bias, me * heads, heads, 0)[:, : spans * tok]
    band = jnp.concatenate(
        [
            jnp.full((heads, tok), MASKED, f32),
            bias,
            jnp.full((heads, spans * tok - bias.shape[1]), MASKED, f32),
        ],
        axis=1,
    )
    band = jnp.pad(band, ((0, -heads % 8), (0, 0)))
    (tiles,) = call(
        functools.partial(tiles_kernel, spans, tok),
        [((heads, spans, tok, tok), f32)],
        "bias_tiles",
        arrays=[band],
        after=[columns],
    )
    doc_ends = jnp.cumsum(doc_lengths[:, 0], axis=-1)
    positions = jnp.arange(length, dtype=jnp.int32)
    docs = jnp.sum((doc_ends[:, None, :] <= positions[None, :, None]).astype(jnp.int32), axis=2)
    kdocs, qdocs = docs[:, :, None], docs[:, None, :]

    assert micros == 2
    xs = [by_distance(tokens[0], "dp", [cot_rows, tiles, kdocs])]

    cot_rows = gate(cot_rows, w_mine, tiles, xs[0][-1], kdocs)
    cot_rows = exchange(cot_rows.reshape(experts, padded, width), "expert").reshape(-1, width)

    att = []
    saved = []
    pair_flops = 2 * heads * LANES * tok * tok * sum(min(j, reach) + 1 for j in range(n))
    w_heads = w_mine
    gain_a = None
    for m in range(micros):
        first = m == 0
        if not first:
            xs.append(by_distance(tokens[1], "dp", [saved[0][1]]))
        made = call(
            functools.partial(attn_fwd_kernel, n, reach, heads, first),
            [((tok, part), bf16)] * n
            + [((3 * groups, length, LANES), bf16), ((8, length), f32)]
            + ([((width, 3 * wide), bf16), ((1, width), f32)] if first else []),
            "attention_forward",
            smem=[idx],
            arrays=[
                w_heads,
                *([] if first else [gain_a]),
                (kdocs, m),
                (qdocs, m),
                *xs[m],
            ],
            hbm=[tiles],
            hbm_out=[n],
            flops=2 * length * width * 3 * wide + 2 * pair_flops,
            scratch=[
                pltpu.VMEM((wide, length), bf16),
                pltpu.VMEM((wide, length), f32),
                pltpu.VMEM((length, wide), bf16),
                pltpu.VMEM(tiles.shape, f32),
                pltpu.VMEM((3 * groups, length, LANES), bf16),
                pltpu.SemaphoreType.DMA,
                pltpu.SemaphoreType.DMA,
            ],
        )
        att_m, (qkv, lse, *more) = made[:n], made[n:]
        if first:
            w_heads, gain_a = more
        att.append([att_m[0]] + [swap(att_m[r], "dp", r) for r in range(1, n)])
        saved.append((qkv, lse))

    shares = by_distance(w_mine[:, packed:], "dp", [saved[0][1]])
    mixed = []
    arrived = []
    dense = None
    for m in range(micros):
        first = m == 0
        mixed_m, rows, *more = call(
            functools.partial(mid_kernel, n, first),
            [((tok, width), f32), ((total, width if first else 2 * width), bf16)]
            + ([((width, width + LANES), bf16)] if first else []),
            "mix_and_dispatch",
            smem=[idx],
            arrays=[(tokens, m), (places_row, m), *att[m], *(shares if first else [dense, (routes, m), (cotangent, m)])],
            after=[cot_rows, xs[1][-1]] if first else [],
            scratch=[pltpu.VMEM((width, n * share), bf16)] if first else [],
            flops=2 * tok * width * width + 2 * total * tok * width,
        )
        if first:
            (dense,) = more
        mixed.append(mixed_m)
        arrived.append(exchange(rows.reshape(experts, capacity, -1), "expert").reshape(total, -1))

    cols = ff // n
    reverse = jnp.asarray(bit_reversed(n), jnp.int32)
    pos = reverse[jnp.bitwise_xor(jnp.arange(n, dtype=jnp.int32), me)]
    src = jnp.bitwise_xor(jnp.roll(reverse, -(n // 2)), me)
    whole = lambda shape, c=0: pl.BlockSpec(shape, lambda f, *_, c=c: (0, c))
    in_block = pl.BlockSpec((width, cols), lambda f, src, pos: (0, src[f]))
    back_block = pl.BlockSpec((cols, width), lambda f, src, pos: (src[f], 0))
    half_block = pl.BlockSpec((n // 2, width // n, cols), lambda f, src, pos: (0, 0, src[f]))
    results = []
    grads = []
    for m in range(micros):
        raw = m == 0
        result, *grads = pl.pallas_call(
            functools.partial(expert_kernel, raw, capacity, padded),
            out_shape=[jax.ShapeDtypeStruct((total, 2 * width), bf16)]
            + (
                [jax.ShapeDtypeStruct((width, ff), bf16), jax.ShapeDtypeStruct((ff, width), bf16)]
                if raw
                else [jax.ShapeDtypeStruct((n // 2, width // n, ff), bf16)] * 2
                + [jax.ShapeDtypeStruct((n // 2, cols, width), bf16)] * 2
            ),
            grid_spec=pltpu.PrefetchScalarGridSpec(
                num_scalar_prefetch=2,
                grid=(n,),
                in_specs=[
                    pl.BlockSpec(memory_space=pltpu.SMEM),
                    whole((total, width)),
                    whole(cot_rows.shape) if raw else whole((total, width), 1),
                    whole((width, LANES), width // LANES),
                    pl.BlockSpec((None, width, cols), lambda f, src, pos: (0, 0, src[f])),
                    pl.BlockSpec((None, cols, width), lambda f, src, pos: (0, src[f], 0)),
                ]
                + ([] if raw else [in_block, back_block]),
                out_specs=[whole((total, 2 * width))]
                + (
                    [in_block, back_block]
                    if raw
                    else [
                        half_block,
                        half_block,
                        pl.BlockSpec(
                            (None, cols, width), lambda f, src, pos: (jnp.maximum(f - n // 2, 0), 0, 0)
                        ),
                        pl.BlockSpec(
                            (None, cols, width), lambda f, src, pos: (jnp.minimum(f, n // 2 - 1), 0, 0)
                        ),
                    ]
                ),
                scratch_shapes=[
                    pltpu.VMEM((total, 2 * width), f32),
                    pltpu.VMEM((total, width), bf16),
                ]
                + ([pltpu.VMEM((total, width), f32), pltpu.VMEM((total, LANES), f32)] if raw else []),
            ),
            compiler_params=pltpu.CompilerParams(vmem_limit_bytes=60 * MIB),
            cost_estimate=pl.CostEstimate(
                flops=12 * total * width * ff, transcendentals=total * ff, bytes_accessed=24 * MIB
            ),
            name="expert",
        )(src, pos, idx, arrived[m], cot_rows if raw else arrived[m], dense, w_in, w_back, *grads)
        results.append(result)
    back = [
        exchange(r.reshape(experts, capacity, 2 * width), "expert").reshape(total, 2 * width) for r in results
    ]
    in_keep, in_send, back_keep, back_send = grads
    pieces = halving_start(in_keep, gate(in_send, back[0]), "dp")
    pieces += halving_start(back_keep, gate(back_send, back[0]), "dp")

    out = token_grad = None
    dense_grad = []
    branches = []
    attn_grad = []
    grad_w = []
    ends = []
    across = -(-heads * min(spans * tok, WINDOW) // (own_rows * LANES)) * LANES
    lanes = packed + across + width // 2
    for m in range(micros):
        first, last = m == 0, m == micros - 1
        after = [] if first else [grad_w[0], ends[0][1], ends[1][1]]
        out, mixed_grad, branch, new_grad, *da = call(
            functools.partial(combine_kernel, n, experts, first, len(after) + (out is not None)),
            [
                ((micros, tok, width), bf16),
                ((tok, width), f32),
                ((tok, width), bf16),
                ((width, LANES), f32),
            ]
            + [((tok, part), bf16)] * n,
            "combine",
            smem=[idx],
            arrays=[
                back[m],
                (places, m),
                (routes, m),
                mixed[m],
                (cotangent, m),
                dense,
                *att[m],
                *dense_grad,
            ],
            after=after,
            flops=6 * total * tok * width + 4 * tok * width * width,
            out_micro=[(0, m, out)],
        )
        dense_grad = [new_grad]
        branches += [branch, *att[m]]
        da = [da[0]] + [swap(da[r], "dp", r) for r in range(1, n)]
        qkv, lse = saved[m]
        after = []
        for terms, far in pieces[:3] if first else pieces[3:]:
            far = gate(far, *da[1:])
            after.append(far)
            ends.append(halving_end(terms, far, "dp"))
        if not first:
            dense_halves = call(
                functools.partial(dense_grad_kernel, n, micros),
                [((width, width // 2), bf16)] * 2,
                "dense_grad",
                smem=[idx],
                arrays=branches,
                flops=2 * micros * tok * width * width,
                scratch=[pltpu.VMEM((width, width), f32)],
            )
            after += [ends[2][1], dense_halves[1]]
        made = call(
            functools.partial(attn_bwd_kernel, n, reach, heads, first, len(after)),
            [((tok, width), bf16)] * n
            + [((length, 3 * wide), bf16), ((1, width), f32), ((8, spans * tok), f32)],
            "attention_backward",
            smem=[idx],
            arrays=[(kdocs, m), (qdocs, m), qkv, lse, *da, *attn_grad],
            hbm=[tiles, w_heads, *xs[m]],
            after=after,
            flops=2 * length * width * 3 * wide + 5 * pair_flops,
            scratch=[
                pltpu.VMEM((groups, length, LANES), bf16),
                pltpu.VMEM((wide, length), bf16),
                pltpu.VMEM((wide, length), f32),
                pltpu.VMEM((2 * groups, length, LANES), f32),
                pltpu.VMEM((heads, spans, tok, tok), f32),
                pltpu.VMEM(tiles.shape, f32),
                pltpu.VMEM((width, 3 * wide), bf16),
                pltpu.VMEM((n, tok, width), bf16),
            ]
            + [pltpu.SemaphoreType.DMA] * (2 + n),
        )
        parts, (dqkv, *attn_grad) = made[:n], made[n:]
        summed, sent_last = halving_terms(parts, "dp")
        dense_parts = []
        if last:
            dense_parts = [dense_halves[0], swap(dense_halves[1], "dp", 1)]
        late = []
        grad_w = call(
            functools.partial(qkv_grad_kernel, n, heads, own_rows, first, last, len(late)),
            [((width, lanes), bf16) if last else ((width, 3 * wide), f32)],
            "qkv_grad",
            smem=[idx],
            arrays=[gain_a, dqkv, *xs[m], *grad_w, *([*attn_grad, *dense_grad, *dense_parts] if last else [])],
            after=late,
            flops=2 * length * width * 3 * wide,
            scratch=[pltpu.VMEM((length, width), bf16)],
        )
        (token_grad,) = call(
            functools.partial(token_grad_kernel, len(summed)),
            [((micros, tok, width), bf16)],
            "token_grad",
            arrays=[(tokens, m), mixed_grad, gain_a, *summed],
            out_micro=[(0, m, token_grad)],
        )

    message = gate(grad_w[0], sent_last)
    message = exchange(message.reshape(whole_count, own_rows, lanes), both)
    grad_qkv, grad_bias, grad_router, grad_gain_a, grad_gain_f, dense_sum = call(
        functools.partial(finish_kernel, n, across),
        [
            ((own_rows, 3 * width), f32),
            ((H, WINDOW), f32),
            ((own_rows, experts), f32),
            ((1, own_rows), f32),
            ((1, own_rows), f32),
            ((own_rows, width), f32),
        ],
        "finish",
        arrays=[message],
    )
    return (
        out[:, None],
        token_grad[:, None],
        grad_qkv,
        dense_sum,
        grad_bias.T,
        grad_gain_a[0],
        grad_gain_f[0],
        grad_router,
        jnp.concatenate([ends[0][0], ends[1][0]])[None],
        jnp.concatenate([ends[2][0], ends[3][0]])[None],
    )


def solution(mesh):
    return jax.shard_map(
        shards,
        mesh=mesh,
        in_specs=(
            P(None, "expert", "dp", None),
            P(None, "expert", None),
            P(None, "expert", "dp", None),
            P(None, "expert", "dp", None),
            P(("dp", "expert"), None),
            P(("dp", "expert"), None),
            P(),
            P(("dp", "expert")),
            P(("dp", "expert")),
            P(("dp", "expert"), None),
            P("expert", None, None),
            P("expert", None, None),
            P(None, "expert", "dp", None),
        ),
        out_specs=(
            P(None, "expert", "dp", None),
            P(None, "expert", "dp", None),
            P(("dp", "expert"), None),
            P(("dp", "expert"), None),
            P(),
            P(("dp", "expert")),
            P(("dp", "expert")),
            P(("dp", "expert"), None),
            P("expert", "dp", None),
            P("expert", "dp", None),
        ),
        check_vma=False,
    )
```

```python
import functools

import jax
import jax.numpy as jnp
from jax import lax
from jax.experimental import pallas as pl
from jax.experimental.pallas import tpu as pltpu
from jax.sharding import PartitionSpec as P

H = 12
HD = 64
TOP = 2
WINDOW = 1024
EPSILON = 1e-06
MASKED = -1e30
LANES = 128

bf16 = jnp.bfloat16
f32 = jnp.float32
MIB = 1 << 20

NN = (((1,), (0,)), ((), ()))
NT = (((1,), (1,)), ((), ()))
TN = (((0,), (0,)), ((), ()))


def dot(a, b, dims=NN):
    return lax.dot_general(a, b, dims, preferred_element_type=f32)


def rsq(x):
    return lax.rsqrt(jnp.mean(x * x, axis=-1, keepdims=True) + EPSILON)


def call(kernel, outs, name, smem=(), arrays=(), after=(), flops=0, scratch=(), limit=60, out_micro=(), hbm=(), hbm_out=()):
    def spec(x):
        if isinstance(x, tuple):
            x, i = x
            return pl.BlockSpec((None,) + x.shape[1:], lambda _: (i,) + (0,) * (x.ndim - 1))
        return pl.BlockSpec(x.shape, lambda _: (0,) * x.ndim)

    arrays = list(arrays)
    given = [x[0] if isinstance(x, tuple) else x for x in arrays]
    micro_of = {k: i for k, i, _ in out_micro}
    olds = [(k, old) for k, _, old in out_micro if old is not None]

    def out_spec(k, s):
        if k in hbm_out:
            return pl.BlockSpec(memory_space=pl.ANY)
        if k in micro_of:
            return pl.BlockSpec((None,) + s[1:], lambda _: (micro_of[k],) + (0,) * (len(s) - 1))
        return pl.BlockSpec(s, lambda _: (0,) * len(s))

    after = list(hbm) + list(after) + [old for _, old in olds]
    aliases = {len(smem) + len(arrays) + len(after) - len(olds) + i: k for i, (k, _) in enumerate(olds)}
    size = lambda shape, dtype: int(jnp.dtype(dtype).itemsize * functools.reduce(lambda p, q: p * q, shape, 1))
    moved = sum(size(x.shape, x.dtype) for x in given) + sum(size(*o) for o in outs)
    return pl.pallas_call(
        kernel,
        grid=(1,),
        out_shape=[jax.ShapeDtypeStruct(s, d) for s, d in outs],
        in_specs=[pl.BlockSpec(memory_space=pltpu.SMEM)] * len(smem)
        + [spec(x) for x in arrays]
        + [pl.BlockSpec(memory_space=pl.ANY)] * len(after),
        out_specs=[out_spec(k, s) for k, (s, _) in enumerate(outs)],
        input_output_aliases=aliases,
        scratch_shapes=list(scratch),
        compiler_params=pltpu.CompilerParams(vmem_limit_bytes=limit * MIB),
        cost_estimate=pl.CostEstimate(flops=int(flops), transcendentals=0, bytes_accessed=moved),
        name=name,
    )(*smem, *given, *after)


def gate(x, *after):
    hbm = pl.BlockSpec(memory_space=pl.ANY)
    return pl.pallas_call(
        lambda *refs: None,
        out_shape=jax.ShapeDtypeStruct(x.shape, x.dtype),
        in_specs=[hbm] * (1 + len(after)),
        out_specs=hbm,
        input_output_aliases={0: 0},
        name="gate",
    )(x, *after)


def packed_blocks(heads):
    return 3 * (heads // 2) + (2 if heads % 2 else 1)


def gain_place(heads):
    return packed_blocks(heads) - 1, HD if heads % 2 else 0


def head_place(heads, kind, h):
    if heads % 2 and h == heads - 1:
        return 3 * (heads // 2) + kind // 2, kind % 2
    return 3 * (h // 2) + kind, h % 2


def low_lanes(shape):
    return lax.broadcasted_iota(jnp.int32, shape, 1) < HD


def move_half(block, source, target):
    return block if source == target else pltpu.roll(block, HD, axis=1)


def column_of(row):
    n = row.shape[1]
    same = lax.broadcasted_iota(jnp.int32, (n, n), 0) == lax.broadcasted_iota(jnp.int32, (n, n), 1)
    return jnp.sum(jnp.where(same, row, 0.0), axis=1, keepdims=True)


def dense_share(n, width):
    return -(-(width + LANES) // (n * LANES)) * LANES


def pack_kernel(n, w_ref, gain_ref, w_out_ref, router_ref, gain_ffn_ref, out_ref):
    count, rows, _ = out_ref.shape
    copies = count // n
    heads = -(-H // n)
    width = w_ref.shape[1] // 3
    low = low_lanes((rows, LANES))
    lane = lax.broadcasted_iota(jnp.int32, (rows, LANES), 1)
    gain = column_of(gain_ref[...].astype(f32))
    gain_block, gain_lane = gain_place(heads)
    for d in range(n):
        found = {}
        for kind in range(3):
            for h in range(heads):
                head = d * heads + h
                if head >= H:
                    continue
                block, half = head_place(heads, kind, h)
                column = kind * width + head * HD
                start = column // LANES * LANES
                piece = move_half(
                    w_ref[:, start : start + LANES].astype(f32), (column - start) // HD, half
                )
                found[block, half] = piece
        for block in range(packed_blocks(heads)):
            none = jnp.zeros((rows, LANES), f32)
            value = jnp.where(low, found.get((block, 0), none), found.get((block, 1), none))
            if block == gain_block:
                value = jnp.where(lane == gain_lane, gain, value)
            value = value.astype(bf16)
            for e in range(copies):
                out_ref[d * copies + e, :, block * LANES : (block + 1) * LANES] = value
    share = dense_share(n, width)
    gain = column_of(gain_ffn_ref[...].astype(f32))
    router = jnp.concatenate(
        [router_ref[...].astype(f32), jnp.zeros((rows, LANES - router_ref.shape[1]), f32)], axis=1
    )
    router = jnp.where(lane == LANES - 1, gain, router).astype(bf16)
    for d in range(n):
        for c in range(0, share, LANES):
            column = d * share + c
            if column < width:
                value = w_out_ref[:, column : column + LANES]
            elif column == width:
                value = router
            else:
                value = jnp.zeros((rows, LANES), bf16)
            at = packed_blocks(heads) * LANES + c
            for e in range(copies):
                out_ref[d * copies + e, :, at : at + LANES] = value


def unpack_qkv(heads, w_ref, w_scr):
    groups = -(-heads // 2)
    rows = w_ref.shape[0]
    low = low_lanes((rows, LANES))
    for kind in range(3):
        for g in range(groups):
            block, half = head_place(heads, kind, 2 * g)
            value = w_ref[:, block * LANES : (block + 1) * LANES]
            if 2 * g + 1 == heads:
                value = jnp.where(low, move_half(value.astype(f32), half, 0), 0.0).astype(bf16)
            at = (kind * groups + g) * LANES
            w_scr[:, at : at + LANES] = value
    block, lane = gain_place(heads)
    turned = w_ref[:, block * LANES : (block + 1) * LANES].astype(f32).T
    return turned[lane : lane + 1]


def pack_grad(heads, grad, gain_row, extra, out_ref):
    groups = -(-heads // 2)
    rows = grad.shape[0]
    low = low_lanes((rows, LANES))
    lane = lax.broadcasted_iota(jnp.int32, (rows, LANES), 1)
    part = lambda kind, g: grad[:, (kind * groups + g) * LANES : (kind * groups + g + 1) * LANES]
    blocks = [part(kind, g) for g in range(heads // 2) for kind in range(3)]
    if heads % 2:
        g = groups - 1
        blocks.append(jnp.where(low, part(0, g), pltpu.roll(part(1, g), HD, axis=1)))
        blocks.append(jnp.where(low, part(2, g), 0.0))
    else:
        blocks.append(jnp.zeros((rows, LANES), f32))
    gain_col = jnp.broadcast_to(gain_row, (LANES, rows)).T
    _, gain_lane = gain_place(heads)
    blocks[-1] = jnp.where(lane == gain_lane, gain_col, blocks[-1])
    blocks[-1] = jnp.where(lane > gain_lane, pltpu.roll(extra, gain_lane + 1, axis=1), blocks[-1])
    for i, block in enumerate(blocks):
        out_ref[:, i * LANES : (i + 1) * LANES] = block.astype(bf16)


def finish_kernel(n, across, message_ref, qkv_ref, bias_ref, router_ref, gain_ref, gain_ffn_ref, dense_ref):
    count, rows, lanes = message_ref.shape
    copies = count // n
    heads = -(-H // n)
    width = qkv_ref.shape[1] // 3
    packed = packed_blocks(heads) * LANES
    low = low_lanes((rows, LANES))
    sums = []
    gain_block, gain_lane = gain_place(heads)
    gain = None
    for d in range(n):
        total = message_ref[d * copies].astype(f32)
        for e in range(1, copies):
            total = total + message_ref[d * copies + e].astype(f32)
        sums.append(total)
        term = total[:, gain_block * LANES : (gain_block + 1) * LANES]
        gain = term if gain is None else gain + term
    count = router_ref.shape[0]
    turned = jnp.concatenate([gain, jnp.zeros((-rows % 8, LANES), f32)], axis=0).T if rows % 8 else gain.T
    router_ref[...] = turned[gain_lane + 1 : gain_lane + 1 + count, :rows]
    gain_ref[...] = turned[gain_lane : gain_lane + 1, :rows]
    gain_ffn_ref[...] = turned[gain_lane + 1 + count : gain_lane + 2 + count, :rows]
    wide = across // LANES
    lines = min(WINDOW, rows * across // heads) // LANES
    for c in range(lines):
        found = []
        for head in range(H):
            row, place = divmod(head % heads * lines + c, wide)
            at = packed + place * LANES
            found.append(sums[head // heads][row : row + 1, at : at + LANES])
        bias_ref[:, c * LANES : (c + 1) * LANES] = jnp.concatenate(found, axis=0)
    if lines * LANES < WINDOW:
        bias_ref[:, lines * LANES :] = jnp.zeros((H, WINDOW - lines * LANES), f32)
    half = dense_ref.shape[1] // 2
    for core in range(2):
        dense_ref[:, core * half : (core + 1) * half] = sum(t[:, lanes - half :] for t in sums[core::2])
    for kind in range(3):
        for pair in range(H // 2):
            halves = []
            for to in range(2):
                head = 2 * pair + to
                block, half = head_place(heads, kind, head % heads)
                value = sums[head // heads][:, block * LANES : (block + 1) * LANES]
                halves.append(move_half(value, half, to))
            at = kind * width + pair * LANES
            qkv_ref[:, at : at + LANES] = jnp.where(low, halves[0], halves[1])


def tiles_kernel(spans, rows, band_ref, *rest):
    out_ref = rest[-1]
    heads = out_ref.shape[0]
    for h in range(heads):
        for s in range(spans):
            ahead = band_ref[h : h + 1, (s + 1) * rows : (s + 2) * rows]
            behind = band_ref[h : h + 1, s * rows : (s + 1) * rows]
            line = jnp.concatenate([ahead, behind], axis=1)
            spread = jnp.broadcast_to(line, (rows, 2 * rows))
            rolled = pltpu.roll(spread, 0, axis=1, stride=1, stride_axis=0)
            out_ref[h, s] = rolled[:, :rows]


def pick_each(places, total):
    slot = lax.broadcasted_iota(jnp.int32, (total, places.shape[1]), 0)
    return [jnp.where(slot == places[k : k + 1], 1.0, 0.0) for k in range(TOP)]


def picks_of(places, total):
    return sum(pick_each(places, total)).astype(bf16)


def dispatch_kernel(capacity, padded, places_row_ref, places_ref, other_ref, cot_ref, after_ref, out_ref):
    tok = places_ref.shape[0]
    total, width = out_ref.shape
    experts = total // padded
    lane = lax.broadcasted_iota(jnp.int32, (tok, LANES), 1)
    lines = []
    for e in range(experts):
        slot = jnp.where(lane < capacity, lane + e * padded, -1)
        found = sum(
            jnp.where(slot == places_ref[:, k : k + 1], other_ref[:, k : k + 1].astype(f32), 0.0)
            for k in range(TOP)
        )
        lines.append(jnp.sum(found, axis=0, keepdims=True))
    spare = -experts % 16
    if spare:
        lines.append(jnp.zeros((spare, LANES), f32))
    lines = jnp.concatenate(lines, axis=0).astype(bf16)
    shape = (total, lines.shape[0])
    row = lax.broadcasted_iota(jnp.int32, shape, 0)
    here = row == lax.broadcasted_iota(jnp.int32, shape, 1) * padded + capacity
    ids = dot(jnp.where(here, 1.0, 0.0).astype(bf16), lines)
    rows = dot(picks_of(places_row_ref[...], total), cot_ref[...])
    out_ref[:, :LANES] = (rows[:, :LANES] + ids).astype(bf16)
    out_ref[:, LANES:] = rows[:, LANES:].astype(bf16)


def attn_fwd_kernel(n, reach, heads, first, idx_ref, w_ref, *rest):
    if not first:
        gain_ref, *rest = rest
    kdoc_ref, qdoc_ref, *rest = rest
    x_refs, rest = rest[:n], rest[n:]
    tiles_hbm, *rest = rest
    att_refs, rest = rest[:n], rest[n:]
    qkv_hbm, lse_ref, *rest = rest
    if first:
        heads_ref, gain_out_ref, *rest = rest
        gain = unpack_qkv(heads, w_ref, heads_ref)
        gain_out_ref[...] = gain
        w_ref = heads_ref
    else:
        gain = gain_ref[...]
    vt_scr, ot_scr, att_scr, tiles_ref, qkv_ref, tiles_sem, qkv_sem = rest
    tiles_copy = pltpu.make_async_copy(tiles_hbm, tiles_ref, tiles_sem)
    tiles_copy.start()
    tok = x_refs[0].shape[0]
    part = heads * HD
    groups = qkv_ref.shape[0] // 3
    me = idx_ref[0]
    for r in range(n):
        start = pl.multiple_of(jnp.bitwise_xor(me, r) * tok, tok)
        x = x_refs[r][...].astype(f32)
        normed = (x * rsq(x) * gain).astype(bf16)
        qkv = dot(normed, w_ref[...]).astype(bf16)
        for c in range(3 * groups):
            qkv_ref[c, pl.ds(start, tok), :] = qkv[:, c * LANES : (c + 1) * LANES]
    for g in range(groups):
        vt_scr[g * LANES : (g + 1) * LANES, :] = qkv_ref[2 * groups + g].astype(f32).T.astype(bf16)
    lse_ref[...] = jnp.zeros_like(lse_ref)
    qkv_copy = pltpu.make_async_copy(qkv_ref, qkv_hbm, qkv_sem)
    qkv_copy.start()
    tiles_copy.wait()

    lane = lax.broadcasted_iota(jnp.int32, (tok, LANES), 1)
    halves = [lane < HD, lane >= HD]

    def scores(h, j):
        lo = max(0, j - reach)
        q = qkv_ref[h // 2, j * tok : (j + 1) * tok, :].astype(f32)
        q = jnp.where(halves[h % 2], q * HD ** (-0.5), 0.0).astype(bf16)
        return dot(qkv_ref[groups + h // 2, lo * tok : (j + 1) * tok, :], q, NT)

    def attend(h, j, s):
        lo = max(0, j - reach)
        rows, cols = slice(lo * tok, (j + 1) * tok), slice(j * tok, (j + 1) * tok)
        bias = jnp.concatenate([tiles_ref[h, j - b] for b in range(lo, j + 1)], axis=0)
        s = jnp.where(kdoc_ref[rows, :] == qdoc_ref[:, cols], s + bias, MASKED)
        peak = jnp.max(s, axis=0, keepdims=True)
        e = jnp.exp(s - peak)
        total = jnp.sum(e, axis=0, keepdims=True)
        p = (e * (1.0 / total)).astype(bf16)
        lse_ref[h : h + 1, cols] = peak + jnp.log(total)
        return p

    def values(h, j, p):
        lo = max(0, j - reach)
        rows, cols = slice(lo * tok, (j + 1) * tok), slice(j * tok, (j + 1) * tok)
        ot_scr[h * HD : (h + 1) * HD, cols] = dot(vt_scr[h * HD : (h + 1) * HD, rows], p)

    work = [(h, j) for h in range(heads) for j in range(n)]
    ahead = scores(*work[0])
    for i, at in enumerate(work):
        s = ahead
        if i + 1 < len(work):
            ahead = scores(*work[i + 1])
        now = (*at, attend(*at, s))
        if i:
            values(*late)
        late = now
    values(*late)
    att_scr[...] = ot_scr[...].T.astype(bf16)
    for r in range(n):
        start = pl.multiple_of(jnp.bitwise_xor(me, r) * tok, tok)
        att_refs[r][...] = att_scr[pl.ds(start, tok), :part]
    qkv_copy.wait()


def unshear(tiles):
    rows = tiles[0].shape[0]
    span = 2 * rows
    wide = [jnp.concatenate([t, jnp.zeros_like(t)], axis=1) for t in tiles]
    count = rows
    while count > 8:
        count //= 2
        wide = [w[:count] + pltpu.roll(w[count:], span - count, axis=1) for w in wide]
    wide = jnp.concatenate(wide, axis=0)
    row = lax.broadcasted_iota(jnp.int32, wide.shape, 0)
    for bit in (4, 2, 1):
        wide = jnp.where(jnp.bitwise_and(row, bit) > 0, pltpu.roll(wide, span - bit, axis=1), wide)
    return [
        jnp.sum(wide[i * count : (i + 1) * count], axis=0, keepdims=True) for i in range(len(tiles))
    ]


def attn_bwd_kernel(
    n, reach, heads, first, after, idx_ref, kdoc_ref, qdoc_ref, qkv_ref, lse_ref, *rest
):
    da_refs, rest = rest[:n], rest[n:]
    if not first:
        old_small_ref, old_band_ref, *rest = rest
    tiles_hbm, w_hbm, *rest = rest
    x_hbms, rest = rest[:n], rest[n + after :]
    part_refs, rest = rest[:n], rest[n:]
    dqkv_ref, new_small_ref, new_band_ref, da_scr, kt_scr, dqt_scr, dkv_scr, acc_scr, *rest = rest
    tiles_ref, w_ref, x_scr, tiles_sem, w_sem, *x_sems = rest
    tiles_copy = pltpu.make_async_copy(tiles_hbm, tiles_ref, tiles_sem)
    tiles_copy.start()
    late_copies = [pltpu.make_async_copy(w_hbm, w_ref, w_sem)]
    late_copies += [
        pltpu.make_async_copy(x_hbms[r], x_scr.at[r], x_sems[r]) for r in range(n)
    ]
    tok = da_refs[0].shape[0]
    groups = qkv_ref.shape[0] // 3
    spans = tiles_ref.shape[1]
    wide = groups * LANES
    me = idx_ref[0]
    if heads * HD < wide:
        da_scr[...] = jnp.zeros_like(da_scr)
    for r in range(n):
        start = pl.multiple_of(jnp.bitwise_xor(me, r) * tok, tok)
        for g in range(groups):
            cols = min(LANES, heads * HD - g * LANES)
            da_scr[g, pl.ds(start, tok), :cols] = da_refs[r][:, g * LANES : g * LANES + cols]
    for g in range(groups):
        kt_scr[g * LANES : (g + 1) * LANES, :] = qkv_ref[groups + g].astype(f32).T.astype(bf16)
    dkv_scr[...] = jnp.zeros_like(dkv_scr)
    dqt_scr[...] = jnp.zeros_like(dqt_scr)
    acc_scr[...] = jnp.zeros_like(acc_scr)
    tiles_copy.wait()
    for copy in late_copies:
        copy.start()

    lane = lax.broadcasted_iota(jnp.int32, (tok, LANES), 1)
    halves = [lane < HD, lane >= HD]

    def places(j):
        lo = max(0, j - reach)
        return lo, slice(lo * tok, (j + 1) * tok), slice(j * tok, (j + 1) * tok)

    def products(h, j):
        _, rows, cols = places(j)
        q = qkv_ref[h // 2, cols, :].astype(f32)
        q = jnp.where(halves[h % 2], q * HD ** (-0.5), 0.0).astype(bf16)
        da = jnp.where(halves[h % 2], da_scr[h // 2, cols, :].astype(f32), 0.0).astype(bf16)
        s = dot(qkv_ref[groups + h // 2, rows, :], q, NT)
        return q, da, s, dot(qkv_ref[2 * groups + h // 2, rows, :], da, NT)

    def score_grads(h, j, s, pg):
        lo, rows, cols = places(j)
        bias = jnp.concatenate([tiles_ref[h, j - b] for b in range(lo, j + 1)], axis=0)
        s = jnp.where(kdoc_ref[rows, :] == qdoc_ref[:, cols], s + bias, MASKED)
        p = jnp.exp(s - lse_ref[h : h + 1, cols])
        centre = jnp.sum(p * pg, axis=0, keepdims=True)
        sg = (p * (pg - centre)).astype(bf16)
        for b in range(lo, j + 1):
            acc_scr[h, j - b] += sg[(b - lo) * tok : (b - lo + 1) * tok].astype(f32)
        return p.astype(bf16), sg

    def gather(h, j, q, da, p, sg):
        _, rows, cols = places(j)
        dkv_scr[h // 2, rows, :] += dot(sg, q)
        dkv_scr[groups + h // 2, rows, :] += dot(p, da)
        at = slice(h * HD, (h + 1) * HD)
        dqt_scr[at, cols] = dot(kt_scr[at, rows], sg) * HD ** (-0.5)

    work = [(h, j) for h in range(heads) for j in range(n)]
    ahead = products(*work[0])
    for i, at in enumerate(work):
        q, da, s, pg = ahead
        if i + 1 < len(work):
            ahead = products(*work[i + 1])
        now = (*at, q, da, *score_grads(*at, s, pg))
        if i:
            gather(*late)
        late = now
    gather(*late)
    for g in range(groups):
        dqkv_ref[:, g * LANES : (g + 1) * LANES] = dqt_scr[g * LANES : (g + 1) * LANES, :].T.astype(bf16)
    for c in range(2 * groups):
        dqkv_ref[:, wide + c * LANES : wide + (c + 1) * LANES] = dkv_scr[c].astype(bf16)
    small = None
    for copy in late_copies:
        copy.wait()
    for r in range(n):
        start = pl.multiple_of(jnp.bitwise_xor(me, r) * tok, tok)
        x = x_scr[r].astype(f32)
        part = dot(dqkv_ref[pl.ds(start, tok), :], w_ref[...], NT)
        part_refs[r][...] = part.astype(bf16)
        term = jnp.sum(part * (x * rsq(x)), axis=0, keepdims=True)
        small = term if small is None else small + term
    if not first:
        small = small + old_small_ref[...]
    new_small_ref[...] = small
    new_band_ref[...] = jnp.zeros_like(new_band_ref)
    lines = unshear([acc_scr[h, s] for h in range(heads) for s in range(spans)])
    for h in range(heads):
        for s in range(spans):
            value = lines[h * spans + s][:, :tok]
            if s + 1 < spans:
                value = value + lines[h * spans + s + 1][:, tok:]
            if not first:
                value = value + old_band_ref[h : h + 1, s * tok : (s + 1) * tok]
            new_band_ref[h : h + 1, s * tok : (s + 1) * tok] = value


def qkv_grad_kernel(n, heads, own_rows, first, last, idx_ref, gain_ref, *rest):
    x_refs, rest = rest[:n], rest[n:]
    if last:
        small_ref, band_ref, extra_ref, *rest = rest
    count = 1 + (not first) + 2 * last
    hbms, (out_ref, normed_scr, *rest) = rest[:count], rest[count:]
    copies = [pltpu.make_async_copy(*c) for c in zip(hbms, rest[:count], rest[count:])]
    for copy in copies:
        copy.start()
    dqkv_ref = rest[0]
    if not first:
        old_w_ref = rest[1]
    if last:
        dense_ref, came_ref = rest[count - 2 : count]
    tok = x_refs[0].shape[0]
    for r in range(n):
        start = pl.multiple_of(jnp.bitwise_xor(idx_ref[0], r) * tok, tok)
        x = x_refs[r][...].astype(f32)
        normed_scr[pl.ds(start, tok), :] = (x * rsq(x) * gain_ref[...]).astype(bf16)
    copies[0].wait()
    new_w = dot(normed_scr[...], dqkv_ref[...], TN)
    for copy in copies[1:]:
        copy.wait()
    if not first:
        new_w = new_w + old_w_ref[...].astype(f32)
    if not last:
        out_ref[...] = new_w.astype(bf16)
        return
    pack_grad(heads, new_w, small_ref[...], extra_ref[...], out_ref)
    packed = packed_blocks(heads) * LANES
    width, lanes = out_ref.shape
    span = min(band_ref.shape[1], WINDOW)
    pieces = [band_ref[h : h + 1, c : c + LANES] for h in range(heads) for c in range(0, span, LANES)]
    dense = dense_ref.shape[1]
    out_ref[:, lanes - dense :] = (dense_ref[...].astype(f32) + came_ref[...].astype(f32)).astype(bf16)
    across = (lanes - packed - dense) // LANES
    pieces += [jnp.zeros((1, LANES), f32)] * (own_rows * across - len(pieces))
    whole = jnp.concatenate(
        [jnp.concatenate(pieces[i * across : (i + 1) * across], axis=1) for i in range(own_rows)]
        + [jnp.zeros((-own_rows % 16, across * LANES), f32)][: 1 if own_rows % 16 else 0],
        axis=0,
    ).astype(bf16)
    shape = (width, whole.shape[0])
    row = lax.rem(lax.broadcasted_iota(jnp.int32, shape, 0), jnp.int32(own_rows))
    pick = jnp.where(row == lax.broadcasted_iota(jnp.int32, shape, 1), 1.0, 0.0).astype(bf16)
    out_ref[:, packed : lanes - dense] = dot(pick, whole).astype(bf16)


def head_rows(me, r, part, width, n):
    at = jnp.bitwise_xor(me, r) * part
    if n * part > width:
        at = jnp.minimum(at, width - part)
    return pl.ds(pl.multiple_of(at, HD), part)


def dense_gain(dense_ref):
    width = dense_ref.shape[1] - LANES
    return dense_ref[:, width:].astype(f32).T[LANES - 1 :]


def gates_of(normed, router, routes):
    logits = dot(normed, router)
    lane = lax.broadcasted_iota(jnp.int32, logits.shape, 1)
    route = [lane == routes[:, k : k + 1] for k in range(TOP)]
    chosen = [jnp.sum(jnp.where(r, logits, 0.0), axis=1, keepdims=True) for r in route]
    peak = jnp.maximum(chosen[0], chosen[1])
    powers = [jnp.exp(c - peak) for c in chosen]
    whole = powers[0] + powers[1]
    return route, [v / whole for v in powers]


def mid_kernel(n, first, idx_ref, x_ref, places_ref, *rest):
    att_refs, rest = rest[:n], rest[n:]
    tok, part = att_refs[0].shape
    width = x_ref.shape[-1]
    me = idx_ref[0]
    if first:
        share_refs = rest[:n]
        mixed_ref, rows_ref, dense_ref, whole_scr = rest[-4:]
        share = share_refs[0].shape[1]
        for r in range(n):
            at = pl.multiple_of(jnp.bitwise_xor(me, r) * share, LANES)
            whole_scr[:, pl.ds(at, share)] = share_refs[r][...]
        dense_ref[...] = whole_scr[:, : dense_ref.shape[1]]
    else:
        dense_ref, routes_ref, cot_ref = rest[:3]
        mixed_ref, rows_ref = rest[-2:]
    mixed = x_ref[...].astype(f32)
    for r in range(n):
        at = head_rows(me, r, part, width, n)
        mixed = mixed + dot(att_refs[r][...], dense_ref[at, :width])
    mixed_ref[...] = mixed
    normed = (mixed * rsq(mixed) * dense_gain(dense_ref)).astype(bf16)
    picks = pick_each(places_ref[...], rows_ref.shape[0])
    rows_ref[:, :width] = dot(sum(picks).astype(bf16), normed).astype(bf16)
    if not first:
        _, gates = gates_of(normed, dense_ref[:, width:], routes_ref[...])
        up = cot_ref[...].astype(f32)
        rows_ref[:, width:] = sum(
            dot(picks[k].astype(bf16), (gates[k] * up).astype(bf16)) for k in range(TOP)
        ).astype(bf16)


def expert_kernel(raw, capacity, padded, src_ref, pos_ref, idx_ref, x_ref, c_ref, dense_ref, win_ref, wback_ref, *rest):
    if raw:
        out_ref, in_ref, back_ref, acc_scr, grad_scr, *rest = rest
    else:
        old_in_ref, old_back_ref, out_ref, in_keep_ref, in_send_ref, back_keep_ref, back_send_ref = rest[:7]
        acc_scr, grad_scr = rest[7:]
    f = pl.program_id(0)
    width = x_ref.shape[-1]

    @pl.when(f == 0)
    def _():
        acc_scr[...] = jnp.zeros_like(acc_scr)
        if not raw:
            grad_scr[...] = c_ref[...]
            return
        c_scr, ids_scr = rest
        up = -(-capacity // 8) * 8
        same = lax.broadcasted_iota(jnp.int32, (up, LANES), 0) == lax.broadcasted_iota(
            jnp.int32, (up, LANES), 1
        )
        for s in range(c_ref.shape[0] // padded):
            block = c_ref[s * padded : (s + 1) * padded, :].astype(f32)
            c_scr[s * capacity : (s + 1) * capacity, :] = block[:capacity]
            line = block[capacity : capacity + 1, :LANES]
            column = jnp.sum(jnp.where(same, line, 0.0), axis=1, keepdims=True)
            ids_scr[s * capacity : (s + 1) * capacity, 0:1] = column[:capacity]
        ids = ids_scr[:, 0:1].astype(jnp.int32)
        logits = dot(x_ref[...], dense_ref[...])
        lane = lax.broadcasted_iota(jnp.int32, logits.shape, 1)
        own = jnp.sum(jnp.where(lane == idx_ref[1], logits, 0.0), axis=1, keepdims=True)
        other = jnp.sum(jnp.where(lane == ids, logits, 0.0), axis=1, keepdims=True)
        peak = jnp.maximum(own, other)
        own = jnp.exp(own - peak)
        gate = own / (own + jnp.exp(other - peak))
        grad_scr[...] = (gate * c_scr[...]).astype(bf16)

    pre = dot(x_ref[...], win_ref[...])
    c0 = 0.7978845608028654
    square = pre * pre
    t = jnp.tanh(pre * (c0 + (c0 * 0.044715) * square))
    hidden = (0.5 * pre * (1.0 + t)).astype(bf16)
    slope = 0.5 * (1.0 + t) + 0.5 * pre * (1.0 - t * t) * (c0 + (3 * c0 * 0.044715) * square)
    acc_scr[:, :width] += dot(hidden, wback_ref[...])
    pre_grad = (dot(grad_scr[...], wback_ref[...], NT) * slope).astype(bf16)
    acc_scr[:, width:] += dot(pre_grad, win_ref[...], NT)
    grad_in = dot(x_ref[...], pre_grad, TN)
    grad_back = dot(hidden, grad_scr[...], TN)
    if raw:
        in_ref[...] = grad_in.astype(bf16)
        back_ref[...] = grad_back.astype(bf16)
    else:
        grad_in = (grad_in + old_in_ref[...].astype(f32)).astype(bf16)
        grad_back = (grad_back + old_back_ref[...].astype(f32)).astype(bf16)
        half, rows, _ = in_keep_ref.shape
        for b in range(2 * half):
            at = pos_ref[b]
            block = grad_in[b * rows : (b + 1) * rows]

            @pl.when(at < half)
            def _():
                in_keep_ref[at] = block

            @pl.when(at >= half)
            def _():
                in_send_ref[at - half] = block

        @pl.when(f < half)
        def _():
            back_send_ref[...] = grad_back

        @pl.when(f >= half)
        def _():
            back_keep_ref[...] = grad_back

    @pl.when(f == pl.num_programs(0) - 1)
    def _():
        out_ref[...] = acc_scr[...].astype(bf16)


def combine_kernel(n, experts, first, after, idx_ref, back_ref, places_ref, routes_ref, mixed_ref, cot_ref, dense_ref, *rest):
    att_refs, rest = rest[:n], rest[n:]
    if not first:
        old_ref, *rest = rest
    rest = rest[after:]
    out_ref, mg_ref, branch_ref, new_ref, *da_refs = rest
    tok, part = att_refs[0].shape
    width = mixed_ref.shape[-1]
    total = back_ref.shape[0]
    gain = dense_gain(dense_ref)
    mixed = mixed_ref[...]
    rr = rsq(mixed)
    normed = (mixed * rr * gain).astype(bf16)
    router = dense_ref[:, width:]
    route, gates = gates_of(normed, router, routes_ref[...])
    slot = lax.broadcasted_iota(jnp.int32, (tok, total), 1)
    hits = [jnp.where(slot == places_ref[:, k : k + 1], 1.0, 0.0) for k in range(TOP)]
    results = back_ref[:, :width]
    returned = [dot(h.astype(bf16), results) for h in hits]
    moe = gates[0] * returned[0] + gates[1] * returned[1]
    out_ref[...] = (mixed + moe).astype(bf16)
    up = cot_ref[...].astype(f32)
    gate_grad = [jnp.sum(up * v, axis=1, keepdims=True) for v in returned]
    centre = gates[0] * gate_grad[0] + gates[1] * gate_grad[1]
    chosen_grad = [gates[k] * (gate_grad[k] - centre) for k in range(TOP)]
    logit_grad = jnp.where(route[0], chosen_grad[0], 0.0) + jnp.where(route[1], chosen_grad[1], 0.0)
    high = logit_grad.astype(bf16)
    low = (logit_grad - high.astype(f32)).astype(bf16)
    normed_grad = dot((hits[0] + hits[1]).astype(bf16), back_ref[:, width:])
    normed_grad = normed_grad + dot(high, router, NT) + dot(low, router, NT)
    router_grad = dot(normed, high, TN) + dot(normed, low, TN)
    scaled = mixed * rr
    gain_part = jnp.sum(normed_grad * scaled, axis=0, keepdims=True)
    ng = gain * normed_grad
    mixed_grad = up + rr * (ng - scaled * jnp.mean(ng * scaled, axis=-1, keepdims=True))
    mg_ref[...] = mixed_grad
    branch = mixed_grad.astype(bf16)
    gain_col = jnp.broadcast_to(gain_part, (LANES, width)).T
    lane = lax.broadcasted_iota(jnp.int32, gain_col.shape, 1)
    extra = jnp.where(lane == experts, gain_col, router_grad)
    if not first:
        extra = extra + old_ref[...]
    new_ref[...] = extra
    branch_ref[...] = branch
    for r in range(n):
        at = head_rows(idx_ref[0], r, part, width, n)
        da_refs[r][...] = dot(branch, dense_ref[at, :width], NT).astype(bf16)


def dense_grad_kernel(n, micros, idx_ref, *rest):
    keep_ref, send_ref, scr = rest[-3:]
    part = rest[1].shape[1]
    width, half = keep_ref.shape[0], keep_ref.shape[1]
    for r in range(n):
        at = head_rows(idx_ref[0], r, part, width, n)

        def add_grad(at=at, r=r):
            scr[at, :] = sum(
                dot(rest[m * (n + 1) + 1 + r][...], rest[m * (n + 1)][...], TN) for m in range(micros)
            )

        if n * part > width:
            pl.when(jnp.bitwise_xor(idx_ref[0], r) * part < width)(add_grad)
        else:
            add_grad()
    upper = jnp.bitwise_and(idx_ref[0], 1) == 1
    low, high = scr[:, :half], scr[:, half:]
    keep_ref[...] = jnp.where(upper, high, low).astype(bf16)
    send_ref[...] = jnp.where(upper, low, high).astype(bf16)


def token_grad_kernel(count, x_ref, mg_ref, gain_ref, *rest):
    parts, out_ref = rest[:count], rest[-1]
    grad = parts[0][...].astype(f32)
    for p in parts[1:]:
        grad = grad + p[...].astype(f32)
    x = x_ref[...].astype(f32)
    r = rsq(x)
    scaled = x * r
    ng = gain_ref[...] * grad
    out_ref[...] = (
        mg_ref[...] + r * (ng - scaled * jnp.mean(ng * scaled, axis=-1, keepdims=True))
    ).astype(bf16)


def swap(x, axis, by):
    return lax.ppermute(x, axis, [(i, i ^ by) for i in range(lax.axis_size(axis))])


def exchange(x, axes):
    return lax.all_to_all(x, axes, split_axis=0, concat_axis=0, tiled=True)


def bit_reversed(n):
    bits = n.bit_length() - 1
    return [int(format(r, "b").zfill(bits)[::-1], 2) if bits else 0 for r in range(n)]


def add_kernel(*refs):
    count = len(refs) // 4
    for i in range(count):
        total = refs[2 * i][...].astype(f32) + refs[2 * i + 1][...].astype(f32)
        rows = total.shape[1] // 2
        refs[2 * count + 2 * i][...] = total[:, :rows].astype(bf16)
        refs[2 * count + 2 * i + 1][...] = total[:, rows:].astype(bf16)


def halving_start(grads, axis):
    cames = [swap(send, axis, 1) for _, send in grads]
    arrays = []
    specs = []
    outs = []
    out_specs = []
    for (keep, _), came in zip(grads, cames):
        half, (rows, cols) = keep.shape[0] // 2, keep.shape[1:]
        arrays += [keep, came]
        specs += [pl.BlockSpec((half, rows, cols), lambda _: (1, 0, 0))] * 2
        outs += [jax.ShapeDtypeStruct((half, rows // 2, cols), bf16)] * 2
        out_specs += [pl.BlockSpec((half, rows // 2, cols), lambda _: (0, 0, 0))] * 2
    fars = pl.pallas_call(
        add_kernel,
        grid=(1,),
        out_shape=outs,
        in_specs=specs,
        out_specs=out_specs,
        compiler_params=pltpu.CompilerParams(vmem_limit_bytes=60 * MIB),
        name="add",
    )(*arrays)
    pieces = []
    for i, ((keep, _), came) in enumerate(zip(grads, cames)):
        half, rows = keep.shape[0] // 2, keep.shape[1] // 2
        for j, piece in enumerate((slice(0, rows), slice(rows, None))):
            pieces.append(([keep[:half, piece], came[:half, piece]], fars[2 * i + j]))
    return pieces


def halving_end(terms, far, axis):
    by = 2
    while True:
        half = terms[0].shape[0] // 2
        came = swap(far, axis, by)
        terms = terms + [came]
        if not half:
            return sum(t[0].astype(f32) for t in terms), came
        far = sum(t[half:].astype(f32) for t in terms).astype(bf16)
        terms = [t[:half] for t in terms]
        by *= 2


def bits_of(axis):
    return [1 << i for i in range(lax.axis_size(axis).bit_length() - 1)][::-1]


def upper_half(axis, by):
    return lax.rem(lax.div(lax.axis_index(axis), by), 2) == 1


def by_distance(x, axis, after=(), came=None):
    blocks = {0: x}
    by = lax.axis_size(axis) // 2
    if came is not None:
        blocks[by] = gate(came, *after)
        after = ()
        by //= 2
    while by:
        for r in list(blocks):
            blocks[r ^ by] = swap(blocks[r], axis, by)
        by //= 2
        if after and by:
            blocks.update({r: gate(b, *after) for r, b in blocks.items() if r})
            after = ()
    return [blocks[r] for r in range(len(blocks))]


def sum_kernel(count, *refs):
    refs[-1][...] = sum(r[...].astype(f32) for r in refs[:count]).astype(bf16)


def halving_terms(parts, axis, after=lambda: ()):
    terms = {r: [p] for r, p in enumerate(parts)}
    total = parts[0]
    by = 1
    while by < len(parts):
        for r in [r for r in terms if r & by]:
            held = terms.pop(r)
            total = held[0]
            if len(held) > 1:
                (total,) = call(
                    functools.partial(sum_kernel, len(held)),
                    [(total.shape, bf16)],
                    "sum",
                    arrays=held,
                    after=after(),
                )
            terms[r ^ by].append(swap(total, axis, by))
        by *= 2
    return terms[0], total


def shards(
    tokens, doc_lengths, routes, slots, w_qkv, w_out, rel_bias, gain_attn, gain_ffn, w_router, w_in, w_back, cotangent
):
    micros, _, tok, width = tokens.shape
    n = lax.axis_size("dp")
    experts = lax.axis_size("expert")
    me = lax.axis_index("dp")
    my_expert = lax.axis_index("expert")
    reach = min((WINDOW - 2) // tok + 1, n - 1)
    spans = reach + 1
    capacity = (9 * tok * TOP + 8 * experts - 1) // (8 * experts)
    total = experts * capacity
    length = n * tok
    heads = -(-H // n)
    groups = -(-heads // 2)
    part = heads * HD
    wide = groups * LANES
    ff = w_in.shape[2]
    own_rows = w_qkv.shape[0]
    whole_count = n * experts
    both = ("dp", "expert")
    tokens, cotangent = tokens[:, 0], cotangent[:, 0]
    routes, slots = routes[:, 0], slots[:, 0]
    idx = jnp.stack([me, my_expert]).astype(jnp.int32)

    packed = packed_blocks(heads) * LANES
    share = dense_share(n, width)
    (columns,) = call(
        functools.partial(pack_kernel, n),
        [((whole_count, own_rows, packed + share), bf16)],
        "pack",
        arrays=[w_qkv, gain_attn[None], w_out, w_router, gain_ffn[None]],
    )
    w_mine = exchange(columns, both).reshape(width, packed + share)

    places = jnp.where(slots >= 0, routes * capacity + slots, total)
    places_row = places.transpose(0, 2, 1)
    padded = -(-(capacity + 1) // 8) * 8
    padded_places = jnp.where(slots[0] >= 0, routes[0] * padded + slots[0], experts * padded)
    (cot_rows,) = call(
        functools.partial(dispatch_kernel, capacity, padded),
        [((experts * padded, width), bf16)],
        "dispatch_cotangent",
        arrays=[padded_places.T, padded_places, routes[0, :, ::-1], (cotangent, 0)],
        after=[columns],
        flops=2 * total * tok * width,
    )

    bias = jnp.pad(rel_bias.astype(f32).T, ((0, heads * n - H), (0, 0)))
    bias = lax.dynamic_slice_in_dim(bias, me * heads, heads, 0)[:, : spans * tok]
    band = jnp.concatenate(
        [
            jnp.full((heads, tok), MASKED, f32),
            bias,
            jnp.full((heads, spans * tok - bias.shape[1]), MASKED, f32),
        ],
        axis=1,
    )
    band = jnp.pad(band, ((0, -heads % 8), (0, 0)))
    (tiles,) = call(
        functools.partial(tiles_kernel, spans, tok),
        [((heads, spans, tok, tok), f32)],
        "bias_tiles",
        arrays=[band],
        after=[columns],
    )
    doc_ends = jnp.cumsum(doc_lengths[:, 0], axis=-1)
    positions = jnp.arange(length, dtype=jnp.int32)
    docs = jnp.sum((doc_ends[:, None, :] <= positions[None, :, None]).astype(jnp.int32), axis=2)
    kdocs, qdocs = docs[:, :, None], docs[:, None, :]

    assert micros == 2
    xs = [by_distance(tokens[0], "dp", [cot_rows, tiles, kdocs])]
    second = swap(gate(tokens[1], tiles), "dp", n // 2)

    cot_rows = gate(cot_rows, w_mine, tiles, xs[0][-1], kdocs, second)
    cot_rows = exchange(cot_rows.reshape(experts, padded, width), "expert").reshape(-1, width)

    att = []
    saved = []
    pair_flops = 2 * heads * LANES * tok * tok * sum(min(j, reach) + 1 for j in range(n))
    w_heads = w_mine
    gain_a = None
    for m in range(micros):
        first = m == 0
        if not first:
            xs.append(by_distance(tokens[1], "dp", [saved[0][1]], second))
        made = call(
            functools.partial(attn_fwd_kernel, n, reach, heads, first),
            [((tok, part), bf16)] * n
            + [((3 * groups, length, LANES), bf16), ((8, length), f32)]
            + ([((width, 3 * wide), bf16), ((1, width), f32)] if first else []),
            "attention_forward",
            smem=[idx],
            arrays=[
                w_heads,
                *([] if first else [gain_a]),
                (kdocs, m),
                (qdocs, m),
                *xs[m],
            ],
            hbm=[tiles],
            hbm_out=[n],
            flops=2 * length * width * 3 * wide + 2 * pair_flops,
            scratch=[
                pltpu.VMEM((wide, length), bf16),
                pltpu.VMEM((wide, length), f32),
                pltpu.VMEM((length, wide), bf16),
                pltpu.VMEM(tiles.shape, f32),
                pltpu.VMEM((3 * groups, length, LANES), bf16),
                pltpu.SemaphoreType.DMA,
                pltpu.SemaphoreType.DMA,
            ],
        )
        att_m, (qkv, lse, *more) = made[:n], made[n:]
        if first:
            w_heads, gain_a = more
        att.append([att_m[0]] + [swap(att_m[r], "dp", r) for r in range(1, n)])
        saved.append((qkv, lse))

    shares = by_distance(w_mine[:, packed:], "dp", [saved[0][1]])
    mixed = []
    arrived = []
    dense = None
    for m in range(micros):
        first = m == 0
        mixed_m, rows, *more = call(
            functools.partial(mid_kernel, n, first),
            [((tok, width), f32), ((total, width if first else 2 * width), bf16)]
            + ([((width, width + LANES), bf16)] if first else []),
            "mix_and_dispatch",
            smem=[idx],
            arrays=[(tokens, m), (places_row, m), *att[m], *(shares if first else [dense, (routes, m), (cotangent, m)])],
            after=[xs[1][-1]] if first else [],
            scratch=[pltpu.VMEM((width, n * share), bf16)] if first else [],
            flops=2 * tok * width * width + 2 * total * tok * width,
        )
        if first:
            (dense,) = more
            rows = gate(rows, cot_rows)
        mixed.append(mixed_m)
        arrived.append(exchange(rows.reshape(experts, capacity, -1), "expert").reshape(total, -1))

    cols = ff // n
    reverse = jnp.asarray(bit_reversed(n), jnp.int32)
    pos = reverse[jnp.bitwise_xor(jnp.arange(n, dtype=jnp.int32), me)]
    src = jnp.bitwise_xor(jnp.roll(reverse, -(n // 2)), me)
    whole = lambda shape, c=0: pl.BlockSpec(shape, lambda f, *_, c=c: (0, c))
    in_block = pl.BlockSpec((width, cols), lambda f, src, pos: (0, src[f]))
    back_block = pl.BlockSpec((cols, width), lambda f, src, pos: (src[f], 0))
    half_block = pl.BlockSpec((n // 2, width // n, cols), lambda f, src, pos: (0, 0, src[f]))
    results = []
    grads = []
    for m in range(micros):
        raw = m == 0
        result, *grads = pl.pallas_call(
            functools.partial(expert_kernel, raw, capacity, padded),
            out_shape=[jax.ShapeDtypeStruct((total, 2 * width), bf16)]
            + (
                [jax.ShapeDtypeStruct((width, ff), bf16), jax.ShapeDtypeStruct((ff, width), bf16)]
                if raw
                else [jax.ShapeDtypeStruct((n // 2, width // n, ff), bf16)] * 2
                + [jax.ShapeDtypeStruct((n // 2, cols, width), bf16)] * 2
            ),
            grid_spec=pltpu.PrefetchScalarGridSpec(
                num_scalar_prefetch=2,
                grid=(n,),
                in_specs=[
                    pl.BlockSpec(memory_space=pltpu.SMEM),
                    whole((total, width)),
                    whole(cot_rows.shape) if raw else whole((total, width), 1),
                    whole((width, LANES), width // LANES),
                    pl.BlockSpec((None, width, cols), lambda f, src, pos: (0, 0, src[f])),
                    pl.BlockSpec((None, cols, width), lambda f, src, pos: (0, src[f], 0)),
                ]
                + ([] if raw else [in_block, back_block]),
                out_specs=[whole((total, 2 * width))]
                + (
                    [in_block, back_block]
                    if raw
                    else [
                        half_block,
                        half_block,
                        pl.BlockSpec(
                            (None, cols, width), lambda f, src, pos: (jnp.maximum(f - n // 2, 0), 0, 0)
                        ),
                        pl.BlockSpec(
                            (None, cols, width), lambda f, src, pos: (jnp.minimum(f, n // 2 - 1), 0, 0)
                        ),
                    ]
                ),
                scratch_shapes=[
                    pltpu.VMEM((total, 2 * width), f32),
                    pltpu.VMEM((total, width), bf16),
                ]
                + ([pltpu.VMEM((total, width), f32), pltpu.VMEM((total, LANES), f32)] if raw else []),
            ),
            compiler_params=pltpu.CompilerParams(vmem_limit_bytes=60 * MIB),
            cost_estimate=pl.CostEstimate(
                flops=12 * total * width * ff, transcendentals=total * ff, bytes_accessed=24 * MIB
            ),
            name="expert",
        )(src, pos, idx, arrived[m], cot_rows if raw else arrived[m], dense, w_in, w_back, *grads)
        results.append(result)
    in_keep, in_send, back_keep, back_send = grads
    pieces = halving_start([(in_keep, in_send), (back_keep, back_send)], "dp")
    results[1] = gate(results[1], *[far for _, far in pieces])
    back = [
        exchange(r.reshape(experts, capacity, 2 * width), "expert").reshape(total, 2 * width) for r in results
    ]

    out = token_grad = None
    dense_grad = []
    branches = []
    attn_grad = []
    grad_w = []
    ends = [halving_end(*pieces[0], "dp")]
    across = -(-heads * min(spans * tok, WINDOW) // (own_rows * LANES)) * LANES
    lanes = packed + across + width // 2
    for m in range(micros):
        first, last = m == 0, m == micros - 1
        after = [] if first else [grad_w[0], ends[0][1], ends[1][1], first_sent]
        out, mixed_grad, branch, new_grad, *da = call(
            functools.partial(combine_kernel, n, experts, first, len(after) + (out is not None)),
            [
                ((micros, tok, width), bf16),
                ((tok, width), f32),
                ((tok, width), bf16),
                ((width, LANES), f32),
            ]
            + [((tok, part), bf16)] * n,
            "combine",
            smem=[idx],
            arrays=[
                back[m],
                (places, m),
                (routes, m),
                mixed[m],
                (cotangent, m),
                dense,
                *att[m],
                *dense_grad,
            ],
            after=after,
            flops=6 * total * tok * width + 4 * tok * width * width,
            out_micro=[(0, m, out)],
        )
        dense_grad = [new_grad]
        branches += [branch, *att[m]]
        da = [da[0]] + [swap(da[r], "dp", r) for r in range(1, n)]
        qkv, lse = saved[m]
        after = []
        for terms, far in pieces[1:3] if first else pieces[3:]:
            far = gate(far, *da[1:])
            after.append(far)
            ends.append(halving_end(terms, far, "dp"))
        if not first:
            dense_halves = call(
                functools.partial(dense_grad_kernel, n, micros),
                [((width, width // 2), bf16)] * 2,
                "dense_grad",
                smem=[idx],
                arrays=branches,
                flops=2 * micros * tok * width * width,
                scratch=[pltpu.VMEM((width, width), f32)],
            )
            after += [ends[2][1], dense_halves[1]]
        made = call(
            functools.partial(attn_bwd_kernel, n, reach, heads, first, len(after)),
            [((tok, width), bf16)] * n
            + [((length, 3 * wide), bf16), ((1, width), f32), ((8, spans * tok), f32)],
            "attention_backward",
            smem=[idx],
            arrays=[(kdocs, m), (qdocs, m), qkv, lse, *da, *attn_grad],
            hbm=[tiles, w_heads, *xs[m]],
            after=after,
            flops=2 * length * width * 3 * wide + 5 * pair_flops,
            scratch=[
                pltpu.VMEM((groups, length, LANES), bf16),
                pltpu.VMEM((wide, length), bf16),
                pltpu.VMEM((wide, length), f32),
                pltpu.VMEM((2 * groups, length, LANES), f32),
                pltpu.VMEM((heads, spans, tok, tok), f32),
                pltpu.VMEM(tiles.shape, f32),
                pltpu.VMEM((width, 3 * wide), bf16),
                pltpu.VMEM((n, tok, width), bf16),
            ]
            + [pltpu.SemaphoreType.DMA] * (2 + n),
        )
        parts, (dqkv, *attn_grad) = made[:n], made[n:]
        dense_parts = []
        if last:
            dense_parts = [dense_halves[0], swap(dense_halves[1], "dp", 1)]
        grad_w = call(
            functools.partial(qkv_grad_kernel, n, heads, own_rows, first, last),
            [((width, lanes), bf16) if last else ((width, 3 * wide), bf16)],
            "qkv_grad",
            smem=[idx],
            arrays=[gain_a, *xs[m], *([*attn_grad, *dense_grad] if last else [])],
            hbm=[dqkv, *grad_w, *dense_parts],
            flops=2 * length * width * 3 * wide,
            scratch=[pltpu.VMEM((length, width), bf16)]
            + [pltpu.VMEM(x.shape, bf16) for x in (dqkv, *grad_w, *dense_parts)]
            + [pltpu.SemaphoreType.DMA] * (1 + len(grad_w) + len(dense_parts)),
        )
        summed, sent_last = halving_terms(parts, "dp", lambda: [grad_w[0]] if last else [])
        if first:
            first_came, first_sent = summed[-1], sent_last
        (token_grad,) = call(
            functools.partial(token_grad_kernel, len(summed)),
            [((micros, tok, width), bf16)],
            "token_grad",
            arrays=[(tokens, m), mixed_grad, gain_a, *summed],
            out_micro=[(0, m, token_grad)],
        )

    message = gate(grad_w[0], sent_last, ends[3][1], first_came)
    message = exchange(message.reshape(whole_count, own_rows, lanes), both)
    grad_qkv, grad_bias, grad_router, grad_gain_a, grad_gain_f, dense_sum = call(
        functools.partial(finish_kernel, n, across),
        [
            ((own_rows, 3 * width), f32),
            ((H, WINDOW), f32),
            ((experts, own_rows), f32),
            ((1, own_rows), f32),
            ((1, own_rows), f32),
            ((own_rows, width), f32),
        ],
        "finish",
        arrays=[message],
    )
    return (
        out[:, None],
        token_grad[:, None],
        grad_qkv,
        dense_sum,
        grad_bias.T,
        grad_gain_a[0],
        grad_gain_f[0],
        grad_router.T,
        jnp.concatenate([ends[0][0], ends[1][0]])[None],
        jnp.concatenate([ends[2][0], ends[3][0]])[None],
    )


def solution(mesh):
    return jax.shard_map(
        shards,
        mesh=mesh,
        in_specs=(
            P(None, "expert", "dp", None),
            P(None, "expert", None),
            P(None, "expert", "dp", None),
            P(None, "expert", "dp", None),
            P(("dp", "expert"), None),
            P(("dp", "expert"), None),
            P(),
            P(("dp", "expert")),
            P(("dp", "expert")),
            P(("dp", "expert"), None),
            P("expert", None, None),
            P("expert", None, None),
            P(None, "expert", "dp", None),
        ),
        out_specs=(
            P(None, "expert", "dp", None),
            P(None, "expert", "dp", None),
            P(("dp", "expert"), None),
            P(("dp", "expert"), None),
            P(),
            P(("dp", "expert")),
            P(("dp", "expert")),
            P(("dp", "expert"), None),
            P("expert", "dp", None),
            P("expert", "dp", None),
        ),
        check_vma=False,
    )
```

```python
import functools

import jax
import jax.numpy as jnp
from jax import lax
from jax.experimental import pallas as pl
from jax.experimental.pallas import tpu as pltpu
from jax.sharding import PartitionSpec as P

H = 12
HD = 64
TOP = 2
WINDOW = 1024
EPSILON = 1e-06
MASKED = -1e30
LANES = 128

bf16 = jnp.bfloat16
f32 = jnp.float32
MIB = 1 << 20

NN = (((1,), (0,)), ((), ()))
NT = (((1,), (1,)), ((), ()))
TN = (((0,), (0,)), ((), ()))


def dot(a, b, dims=NN):
    return lax.dot_general(a, b, dims, preferred_element_type=f32)


def rsq(x):
    return lax.rsqrt(jnp.mean(x * x, axis=-1, keepdims=True) + EPSILON)


def call(kernel, outs, name, smem=(), arrays=(), after=(), flops=0, scratch=(), limit=60, out_micro=(), hbm=(), hbm_out=()):
    def spec(x):
        if isinstance(x, tuple):
            x, i = x
            return pl.BlockSpec((None,) + x.shape[1:], lambda _: (i,) + (0,) * (x.ndim - 1))
        return pl.BlockSpec(x.shape, lambda _: (0,) * x.ndim)

    arrays = list(arrays)
    given = [x[0] if isinstance(x, tuple) else x for x in arrays]
    micro_of = {k: i for k, i, _ in out_micro}
    olds = [(k, old) for k, _, old in out_micro if old is not None]

    def out_spec(k, s):
        if k in hbm_out:
            return pl.BlockSpec(memory_space=pl.ANY)
        if k in micro_of:
            return pl.BlockSpec((None,) + s[1:], lambda _: (micro_of[k],) + (0,) * (len(s) - 1))
        return pl.BlockSpec(s, lambda _: (0,) * len(s))

    after = list(hbm) + list(after) + [old for _, old in olds]
    aliases = {len(smem) + len(arrays) + len(after) - len(olds) + i: k for i, (k, _) in enumerate(olds)}
    size = lambda shape, dtype: int(jnp.dtype(dtype).itemsize * functools.reduce(lambda p, q: p * q, shape, 1))
    moved = sum(size(x.shape, x.dtype) for x in given) + sum(size(*o) for o in outs)
    return pl.pallas_call(
        kernel,
        grid=(1,),
        out_shape=[jax.ShapeDtypeStruct(s, d) for s, d in outs],
        in_specs=[pl.BlockSpec(memory_space=pltpu.SMEM)] * len(smem)
        + [spec(x) for x in arrays]
        + [pl.BlockSpec(memory_space=pl.ANY)] * len(after),
        out_specs=[out_spec(k, s) for k, (s, _) in enumerate(outs)],
        input_output_aliases=aliases,
        scratch_shapes=list(scratch),
        compiler_params=pltpu.CompilerParams(vmem_limit_bytes=limit * MIB),
        cost_estimate=pl.CostEstimate(flops=int(flops), transcendentals=0, bytes_accessed=moved),
        name=name,
    )(*smem, *given, *after)


def gate(x, *after):
    hbm = pl.BlockSpec(memory_space=pl.ANY)
    return pl.pallas_call(
        lambda *refs: None,
        out_shape=jax.ShapeDtypeStruct(x.shape, x.dtype),
        in_specs=[hbm] * (1 + len(after)),
        out_specs=hbm,
        input_output_aliases={0: 0},
        name="gate",
    )(x, *after)


def packed_blocks(heads):
    return 3 * (heads // 2) + (2 if heads % 2 else 1)


def gain_place(heads):
    return packed_blocks(heads) - 1, HD if heads % 2 else 0


def head_place(heads, kind, h):
    if heads % 2 and h == heads - 1:
        return 3 * (heads // 2) + kind // 2, kind % 2
    return 3 * (h // 2) + kind, h % 2


def low_lanes(shape):
    return lax.broadcasted_iota(jnp.int32, shape, 1) < HD


def move_half(block, source, target):
    return block if source == target else pltpu.roll(block, HD, axis=1)


def column_of(row):
    n = row.shape[1]
    same = lax.broadcasted_iota(jnp.int32, (n, n), 0) == lax.broadcasted_iota(jnp.int32, (n, n), 1)
    return jnp.sum(jnp.where(same, row, 0.0), axis=1, keepdims=True)


def dense_share(n, width):
    return -(-(width + LANES) // (n * LANES)) * LANES


def pack_kernel(n, w_ref, gain_ref, w_out_ref, router_ref, gain_ffn_ref, out_ref):
    count, rows, _ = out_ref.shape
    copies = count // n
    heads = -(-H // n)
    width = w_ref.shape[1] // 3
    low = low_lanes((rows, LANES))
    lane = lax.broadcasted_iota(jnp.int32, (rows, LANES), 1)
    gain = column_of(gain_ref[...].astype(f32))
    gain_block, gain_lane = gain_place(heads)
    for d in range(n):
        found = {}
        for kind in range(3):
            for h in range(heads):
                head = d * heads + h
                if head >= H:
                    continue
                block, half = head_place(heads, kind, h)
                column = kind * width + head * HD
                start = column // LANES * LANES
                piece = move_half(
                    w_ref[:, start : start + LANES].astype(f32), (column - start) // HD, half
                )
                found[block, half] = piece
        for block in range(packed_blocks(heads)):
            none = jnp.zeros((rows, LANES), f32)
            value = jnp.where(low, found.get((block, 0), none), found.get((block, 1), none))
            if block == gain_block:
                value = jnp.where(lane == gain_lane, gain, value)
            value = value.astype(bf16)
            for e in range(copies):
                out_ref[d * copies + e, :, block * LANES : (block + 1) * LANES] = value
    share = dense_share(n, width)
    gain = column_of(gain_ffn_ref[...].astype(f32))
    router = jnp.concatenate(
        [router_ref[...].astype(f32), jnp.zeros((LANES - router_ref.shape[0], rows), f32)], axis=0
    ).T
    router = jnp.where(lane == LANES - 1, gain, router).astype(bf16)
    for d in range(n):
        for c in range(0, share, LANES):
            column = d * share + c
            if column < width:
                value = w_out_ref[:, column : column + LANES]
            elif column == width:
                value = router
            else:
                value = jnp.zeros((rows, LANES), bf16)
            at = packed_blocks(heads) * LANES + c
            for e in range(copies):
                out_ref[d * copies + e, :, at : at + LANES] = value


def unpack_qkv(heads, w_ref, w_scr):
    groups = -(-heads // 2)
    rows = w_ref.shape[0]
    low = low_lanes((rows, LANES))
    for kind in range(3):
        for g in range(groups):
            block, half = head_place(heads, kind, 2 * g)
            value = w_ref[:, block * LANES : (block + 1) * LANES]
            if 2 * g + 1 == heads:
                value = jnp.where(low, move_half(value.astype(f32), half, 0), 0.0).astype(bf16)
            at = (kind * groups + g) * LANES
            w_scr[:, at : at + LANES] = value
    block, lane = gain_place(heads)
    turned = w_ref[:, block * LANES : (block + 1) * LANES].astype(f32).T
    return turned[lane : lane + 1]


def pack_grad(heads, grad, gain_row, extra, out_ref):
    groups = -(-heads // 2)
    rows = grad.shape[0]
    low = low_lanes((rows, LANES))
    lane = lax.broadcasted_iota(jnp.int32, (rows, LANES), 1)
    part = lambda kind, g: grad[:, (kind * groups + g) * LANES : (kind * groups + g + 1) * LANES]
    blocks = [part(kind, g) for g in range(heads // 2) for kind in range(3)]
    if heads % 2:
        g = groups - 1
        blocks.append(jnp.where(low, part(0, g), pltpu.roll(part(1, g), HD, axis=1)))
        blocks.append(jnp.where(low, part(2, g), 0.0))
    else:
        blocks.append(jnp.zeros((rows, LANES), f32))
    gain_col = jnp.broadcast_to(gain_row, (LANES, rows)).T
    _, gain_lane = gain_place(heads)
    blocks[-1] = jnp.where(lane == gain_lane, gain_col, blocks[-1])
    blocks[-1] = jnp.where(lane > gain_lane, pltpu.roll(extra, gain_lane + 1, axis=1), blocks[-1])
    for i, block in enumerate(blocks):
        out_ref[:, i * LANES : (i + 1) * LANES] = block.astype(bf16)


def finish_kernel(n, across, message_ref, qkv_ref, bias_ref, router_ref, gain_ref, gain_ffn_ref, dense_ref):
    count, rows, lanes = message_ref.shape
    copies = count // n
    heads = -(-H // n)
    width = qkv_ref.shape[1] // 3
    packed = packed_blocks(heads) * LANES
    low = low_lanes((rows, LANES))
    sums = []
    gain_block, gain_lane = gain_place(heads)
    gain = None
    for d in range(n):
        total = message_ref[d * copies].astype(f32)
        for e in range(1, copies):
            total = total + message_ref[d * copies + e].astype(f32)
        sums.append(total)
        term = total[:, gain_block * LANES : (gain_block + 1) * LANES]
        gain = term if gain is None else gain + term
    count = router_ref.shape[0]
    turned = jnp.concatenate([gain, jnp.zeros((-rows % 8, LANES), f32)], axis=0).T if rows % 8 else gain.T
    router_ref[...] = turned[gain_lane + 1 : gain_lane + 1 + count, :rows]
    gain_ref[...] = turned[gain_lane : gain_lane + 1, :rows]
    gain_ffn_ref[...] = turned[gain_lane + 1 + count : gain_lane + 2 + count, :rows]
    wide = across // LANES
    lines = min(WINDOW, rows * across // heads) // LANES
    for c in range(lines):
        found = []
        for head in range(H):
            row, place = divmod(head % heads * lines + c, wide)
            at = packed + place * LANES
            found.append(sums[head // heads][row : row + 1, at : at + LANES])
        bias_ref[:, c * LANES : (c + 1) * LANES] = jnp.concatenate(found, axis=0)
    if lines * LANES < WINDOW:
        bias_ref[:, lines * LANES :] = jnp.zeros((H, WINDOW - lines * LANES), f32)
    half = dense_ref.shape[1] // 2
    for core in range(2):
        dense_ref[:, core * half : (core + 1) * half] = sum(t[:, lanes - half :] for t in sums[core::2])
    for kind in range(3):
        for pair in range(H // 2):
            halves = []
            for to in range(2):
                head = 2 * pair + to
                block, half = head_place(heads, kind, head % heads)
                value = sums[head // heads][:, block * LANES : (block + 1) * LANES]
                halves.append(move_half(value, half, to))
            at = kind * width + pair * LANES
            qkv_ref[:, at : at + LANES] = jnp.where(low, halves[0], halves[1])


def tiles_kernel(spans, rows, band_ref, *rest):
    out_ref = rest[-1]
    heads = out_ref.shape[0]
    for h in range(heads):
        for s in range(spans):
            ahead = band_ref[h : h + 1, (s + 1) * rows : (s + 2) * rows]
            behind = band_ref[h : h + 1, s * rows : (s + 1) * rows]
            line = jnp.concatenate([ahead, behind], axis=1)
            spread = jnp.broadcast_to(line, (rows, 2 * rows))
            rolled = pltpu.roll(spread, 0, axis=1, stride=1, stride_axis=0)
            out_ref[h, s] = rolled[:, :rows]


def pick_each(places, total):
    slot = lax.broadcasted_iota(jnp.int32, (total, places.shape[1]), 0)
    return [jnp.where(slot == places[k : k + 1], 1.0, 0.0) for k in range(TOP)]


def picks_of(places, total):
    return sum(pick_each(places, total)).astype(bf16)


def dispatch_kernel(capacity, padded, places_row_ref, places_ref, other_ref, cot_ref, after_ref, out_ref):
    tok = places_ref.shape[0]
    total, width = out_ref.shape
    experts = total // padded
    lane = lax.broadcasted_iota(jnp.int32, (tok, LANES), 1)
    lines = []
    for e in range(experts):
        slot = jnp.where(lane < capacity, lane + e * padded, -1)
        found = sum(
            jnp.where(slot == places_ref[:, k : k + 1], other_ref[:, k : k + 1].astype(f32), 0.0)
            for k in range(TOP)
        )
        lines.append(jnp.sum(found, axis=0, keepdims=True))
    spare = -experts % 16
    if spare:
        lines.append(jnp.zeros((spare, LANES), f32))
    lines = jnp.concatenate(lines, axis=0).astype(bf16)
    shape = (total, lines.shape[0])
    row = lax.broadcasted_iota(jnp.int32, shape, 0)
    here = row == lax.broadcasted_iota(jnp.int32, shape, 1) * padded + capacity
    ids = dot(jnp.where(here, 1.0, 0.0).astype(bf16), lines)
    rows = dot(picks_of(places_row_ref[...], total), cot_ref[...])
    out_ref[:, :LANES] = (rows[:, :LANES] + ids).astype(bf16)
    out_ref[:, LANES:] = rows[:, LANES:].astype(bf16)


def attn_fwd_kernel(n, reach, heads, first, idx_ref, w_ref, *rest):
    if not first:
        gain_ref, *rest = rest
    kdoc_ref, qdoc_ref, *rest = rest
    x_refs, rest = rest[:n], rest[n:]
    tiles_hbm, *rest = rest
    att_refs, rest = rest[:n], rest[n:]
    qkv_hbm, lse_ref, *rest = rest
    if first:
        heads_ref, gain_out_ref, *rest = rest
        gain = unpack_qkv(heads, w_ref, heads_ref)
        gain_out_ref[...] = gain
        w_ref = heads_ref
    else:
        gain = gain_ref[...]
    vt_scr, ot_scr, att_scr, tiles_ref, qkv_ref, tiles_sem, qkv_sem = rest
    tiles_copy = pltpu.make_async_copy(tiles_hbm, tiles_ref, tiles_sem)
    tiles_copy.start()
    tok = x_refs[0].shape[0]
    part = heads * HD
    groups = qkv_ref.shape[0] // 3
    me = idx_ref[0]
    for r in range(n):
        start = pl.multiple_of(jnp.bitwise_xor(me, r) * tok, tok)
        x = x_refs[r][...].astype(f32)
        normed = (x * rsq(x) * gain).astype(bf16)
        qkv = dot(normed, w_ref[...]).astype(bf16)
        for c in range(3 * groups):
            qkv_ref[c, pl.ds(start, tok), :] = qkv[:, c * LANES : (c + 1) * LANES]
    for g in range(groups):
        vt_scr[g * LANES : (g + 1) * LANES, :] = qkv_ref[2 * groups + g].astype(f32).T.astype(bf16)
    lse_ref[...] = jnp.zeros_like(lse_ref)
    qkv_copy = pltpu.make_async_copy(qkv_ref, qkv_hbm, qkv_sem)
    qkv_copy.start()
    tiles_copy.wait()

    lane = lax.broadcasted_iota(jnp.int32, (tok, LANES), 1)
    halves = [lane < HD, lane >= HD]

    def scores(h, j):
        lo = max(0, j - reach)
        q = qkv_ref[h // 2, j * tok : (j + 1) * tok, :].astype(f32)
        q = jnp.where(halves[h % 2], q * HD ** (-0.5), 0.0).astype(bf16)
        return dot(qkv_ref[groups + h // 2, lo * tok : (j + 1) * tok, :], q, NT)

    def attend(h, j, s):
        lo = max(0, j - reach)
        rows, cols = slice(lo * tok, (j + 1) * tok), slice(j * tok, (j + 1) * tok)
        bias = jnp.concatenate([tiles_ref[h, j - b] for b in range(lo, j + 1)], axis=0)
        s = jnp.where(kdoc_ref[rows, :] == qdoc_ref[:, cols], s + bias, MASKED)
        peak = jnp.max(s, axis=0, keepdims=True)
        e = jnp.exp(s - peak)
        total = jnp.sum(e, axis=0, keepdims=True)
        p = (e * (1.0 / total)).astype(bf16)
        lse_ref[h : h + 1, cols] = peak + jnp.log(total)
        return p

    def values(h, j, p):
        lo = max(0, j - reach)
        rows, cols = slice(lo * tok, (j + 1) * tok), slice(j * tok, (j + 1) * tok)
        ot_scr[h * HD : (h + 1) * HD, cols] = dot(vt_scr[h * HD : (h + 1) * HD, rows], p)

    work = [(h, j) for h in range(heads) for j in range(n)]
    ahead = scores(*work[0])
    for i, at in enumerate(work):
        s = ahead
        if i + 1 < len(work):
            ahead = scores(*work[i + 1])
        now = (*at, attend(*at, s))
        if i:
            values(*late)
        late = now
    values(*late)
    att_scr[...] = ot_scr[...].T.astype(bf16)
    for r in range(n):
        start = pl.multiple_of(jnp.bitwise_xor(me, r) * tok, tok)
        att_refs[r][...] = att_scr[pl.ds(start, tok), :part]
    qkv_copy.wait()


def unshear(tiles):
    rows = tiles[0].shape[0]
    span = 2 * rows
    wide = [jnp.concatenate([t, jnp.zeros_like(t)], axis=1) for t in tiles]
    count = rows
    while count > 8:
        count //= 2
        wide = [w[:count] + pltpu.roll(w[count:], span - count, axis=1) for w in wide]
    wide = jnp.concatenate(wide, axis=0)
    row = lax.broadcasted_iota(jnp.int32, wide.shape, 0)
    for bit in (4, 2, 1):
        wide = jnp.where(jnp.bitwise_and(row, bit) > 0, pltpu.roll(wide, span - bit, axis=1), wide)
    return [
        jnp.sum(wide[i * count : (i + 1) * count], axis=0, keepdims=True) for i in range(len(tiles))
    ]


def attn_bwd_kernel(
    n, reach, heads, first, after, idx_ref, kdoc_ref, qdoc_ref, qkv_ref, lse_ref, *rest
):
    da_refs, rest = rest[:n], rest[n:]
    if not first:
        old_small_ref, old_band_ref, *rest = rest
    tiles_hbm, w_hbm, *rest = rest
    x_hbms, rest = rest[:n], rest[n + after :]
    part_refs, rest = rest[:n], rest[n:]
    dqkv_ref, new_small_ref, new_band_ref, da_scr, kt_scr, dqt_scr, dkv_scr, acc_scr, *rest = rest
    tiles_ref, w_ref, x_scr, tiles_sem, w_sem, *x_sems = rest
    tiles_copy = pltpu.make_async_copy(tiles_hbm, tiles_ref, tiles_sem)
    tiles_copy.start()
    late_copies = [pltpu.make_async_copy(w_hbm, w_ref, w_sem)]
    late_copies += [
        pltpu.make_async_copy(x_hbms[r], x_scr.at[r], x_sems[r]) for r in range(n)
    ]
    tok = da_refs[0].shape[0]
    groups = qkv_ref.shape[0] // 3
    spans = tiles_ref.shape[1]
    wide = groups * LANES
    me = idx_ref[0]
    if heads * HD < wide:
        da_scr[...] = jnp.zeros_like(da_scr)
    for r in range(n):
        start = pl.multiple_of(jnp.bitwise_xor(me, r) * tok, tok)
        for g in range(groups):
            cols = min(LANES, heads * HD - g * LANES)
            da_scr[g, pl.ds(start, tok), :cols] = da_refs[r][:, g * LANES : g * LANES + cols]
    for g in range(groups):
        kt_scr[g * LANES : (g + 1) * LANES, :] = qkv_ref[groups + g].astype(f32).T.astype(bf16)
    dkv_scr[...] = jnp.zeros_like(dkv_scr)
    dqt_scr[...] = jnp.zeros_like(dqt_scr)
    acc_scr[...] = jnp.zeros_like(acc_scr)
    tiles_copy.wait()
    for copy in late_copies:
        copy.start()

    lane = lax.broadcasted_iota(jnp.int32, (tok, LANES), 1)
    halves = [lane < HD, lane >= HD]

    def places(j):
        lo = max(0, j - reach)
        return lo, slice(lo * tok, (j + 1) * tok), slice(j * tok, (j + 1) * tok)

    def products(h, j):
        _, rows, cols = places(j)
        q = qkv_ref[h // 2, cols, :].astype(f32)
        q = jnp.where(halves[h % 2], q * HD ** (-0.5), 0.0).astype(bf16)
        da = jnp.where(halves[h % 2], da_scr[h // 2, cols, :].astype(f32), 0.0).astype(bf16)
        s = dot(qkv_ref[groups + h // 2, rows, :], q, NT)
        return q, da, s, dot(qkv_ref[2 * groups + h // 2, rows, :], da, NT)

    def score_grads(h, j, s, pg):
        lo, rows, cols = places(j)
        bias = jnp.concatenate([tiles_ref[h, j - b] for b in range(lo, j + 1)], axis=0)
        s = jnp.where(kdoc_ref[rows, :] == qdoc_ref[:, cols], s + bias, MASKED)
        p = jnp.exp(s - lse_ref[h : h + 1, cols])
        centre = jnp.sum(p * pg, axis=0, keepdims=True)
        sg = (p * (pg - centre)).astype(bf16)
        for b in range(lo, j + 1):
            acc_scr[h, j - b] += sg[(b - lo) * tok : (b - lo + 1) * tok].astype(f32)
        return p.astype(bf16), sg

    def gather(h, j, q, da, p, sg):
        _, rows, cols = places(j)
        dkv_scr[h // 2, rows, :] += dot(sg, q)
        dkv_scr[groups + h // 2, rows, :] += dot(p, da)
        at = slice(h * HD, (h + 1) * HD)
        dqt_scr[at, cols] = dot(kt_scr[at, rows], sg) * HD ** (-0.5)

    work = [(h, j) for h in range(heads) for j in range(n)]
    ahead = products(*work[0])
    for i, at in enumerate(work):
        q, da, s, pg = ahead
        if i + 1 < len(work):
            ahead = products(*work[i + 1])
        now = (*at, q, da, *score_grads(*at, s, pg))
        if i:
            gather(*late)
        late = now
    gather(*late)
    for g in range(groups):
        dqkv_ref[:, g * LANES : (g + 1) * LANES] = dqt_scr[g * LANES : (g + 1) * LANES, :].T.astype(bf16)
    for c in range(2 * groups):
        dqkv_ref[:, wide + c * LANES : wide + (c + 1) * LANES] = dkv_scr[c].astype(bf16)
    small = None
    for copy in late_copies:
        copy.wait()
    for r in range(n):
        start = pl.multiple_of(jnp.bitwise_xor(me, r) * tok, tok)
        x = x_scr[r].astype(f32)
        part = dot(dqkv_ref[pl.ds(start, tok), :], w_ref[...], NT)
        part_refs[r][...] = part.astype(bf16)
        term = jnp.sum(part * (x * rsq(x)), axis=0, keepdims=True)
        small = term if small is None else small + term
    if not first:
        small = small + old_small_ref[...]
    new_small_ref[...] = small
    new_band_ref[...] = jnp.zeros_like(new_band_ref)
    lines = unshear([acc_scr[h, s] for h in range(heads) for s in range(spans)])
    for h in range(heads):
        for s in range(spans):
            value = lines[h * spans + s][:, :tok]
            if s + 1 < spans:
                value = value + lines[h * spans + s + 1][:, tok:]
            if not first:
                value = value + old_band_ref[h : h + 1, s * tok : (s + 1) * tok]
            new_band_ref[h : h + 1, s * tok : (s + 1) * tok] = value


def qkv_grad_kernel(n, heads, own_rows, first, last, idx_ref, gain_ref, *rest):
    x_refs, rest = rest[:n], rest[n:]
    if last:
        small_ref, band_ref, extra_ref, *rest = rest
    count = 1 + (not first) + 2 * last
    hbms, (out_ref, mark_ref, normed_scr, *rest) = rest[:count], rest[count:]
    mark_ref[...] = jnp.zeros_like(mark_ref)
    copies = [pltpu.make_async_copy(*c) for c in zip(hbms, rest[:count], rest[count:])]
    for copy in copies:
        copy.start()
    dqkv_ref = rest[0]
    if not first:
        old_w_ref = rest[1]
    if last:
        dense_ref, came_ref = rest[count - 2 : count]
    tok = x_refs[0].shape[0]
    for r in range(n):
        start = pl.multiple_of(jnp.bitwise_xor(idx_ref[0], r) * tok, tok)
        x = x_refs[r][...].astype(f32)
        normed_scr[pl.ds(start, tok), :] = (x * rsq(x) * gain_ref[...]).astype(bf16)
    copies[0].wait()
    new_w = dot(normed_scr[...], dqkv_ref[...], TN)
    for copy in copies[1:]:
        copy.wait()
    if not first:
        new_w = new_w + old_w_ref[...].astype(f32)
    if not last:
        out_ref[...] = new_w.astype(bf16)
        return
    pack_grad(heads, new_w, small_ref[...], extra_ref[...], out_ref)
    packed = packed_blocks(heads) * LANES
    width, lanes = out_ref.shape
    span = min(band_ref.shape[1], WINDOW)
    pieces = [band_ref[h : h + 1, c : c + LANES] for h in range(heads) for c in range(0, span, LANES)]
    dense = dense_ref.shape[1]
    out_ref[:, lanes - dense :] = (dense_ref[...].astype(f32) + came_ref[...].astype(f32)).astype(bf16)
    across = (lanes - packed - dense) // LANES
    pieces += [jnp.zeros((1, LANES), f32)] * (own_rows * across - len(pieces))
    whole = jnp.concatenate(
        [jnp.concatenate(pieces[i * across : (i + 1) * across], axis=1) for i in range(own_rows)]
        + [jnp.zeros((-own_rows % 16, across * LANES), f32)][: 1 if own_rows % 16 else 0],
        axis=0,
    ).astype(bf16)
    shape = (width, whole.shape[0])
    row = lax.rem(lax.broadcasted_iota(jnp.int32, shape, 0), jnp.int32(own_rows))
    pick = jnp.where(row == lax.broadcasted_iota(jnp.int32, shape, 1), 1.0, 0.0).astype(bf16)
    out_ref[:, packed : lanes - dense] = dot(pick, whole).astype(bf16)


def head_rows(me, r, part, width, n):
    at = jnp.bitwise_xor(me, r) * part
    if n * part > width:
        at = jnp.minimum(at, width - part)
    return pl.ds(pl.multiple_of(at, HD), part)


def dense_gain(dense_ref):
    width = dense_ref.shape[1] - LANES
    return dense_ref[:, width:].astype(f32).T[LANES - 1 :]


def gates_of(normed, router, routes):
    logits = dot(normed, router)
    lane = lax.broadcasted_iota(jnp.int32, logits.shape, 1)
    route = [lane == routes[:, k : k + 1] for k in range(TOP)]
    chosen = [jnp.sum(jnp.where(r, logits, 0.0), axis=1, keepdims=True) for r in route]
    peak = jnp.maximum(chosen[0], chosen[1])
    powers = [jnp.exp(c - peak) for c in chosen]
    whole = powers[0] + powers[1]
    return route, [v / whole for v in powers]


def mid_kernel(n, first, idx_ref, x_ref, places_ref, *rest):
    att_refs, rest = rest[:n], rest[n:]
    tok, part = att_refs[0].shape
    width = x_ref.shape[-1]
    me = idx_ref[0]
    if first:
        share_refs = rest[:n]
        mixed_ref, rows_ref, dense_ref, whole_scr = rest[-4:]
        share = share_refs[0].shape[1]
        for r in range(n):
            at = pl.multiple_of(jnp.bitwise_xor(me, r) * share, LANES)
            whole_scr[:, pl.ds(at, share)] = share_refs[r][...]
        dense_ref[...] = whole_scr[:, : dense_ref.shape[1]]
    else:
        dense_ref, routes_ref, cot_ref = rest[:3]
        mixed_ref, rows_ref = rest[-2:]
    mixed = x_ref[...].astype(f32)
    for r in range(n):
        at = head_rows(me, r, part, width, n)
        mixed = mixed + dot(att_refs[r][...], dense_ref[at, :width])
    mixed_ref[...] = mixed
    normed = (mixed * rsq(mixed) * dense_gain(dense_ref)).astype(bf16)
    picks = pick_each(places_ref[...], rows_ref.shape[0])
    rows_ref[:, :width] = dot(sum(picks).astype(bf16), normed).astype(bf16)
    if not first:
        _, gates = gates_of(normed, dense_ref[:, width:], routes_ref[...])
        up = cot_ref[...].astype(f32)
        rows_ref[:, width:] = sum(
            dot(picks[k].astype(bf16), (gates[k] * up).astype(bf16)) for k in range(TOP)
        ).astype(bf16)


def expert_kernel(raw, capacity, padded, src_ref, pos_ref, idx_ref, x_ref, c_ref, dense_ref, win_ref, wback_ref, *rest):
    if raw:
        out_ref, in_ref, back_ref, acc_scr, grad_scr, *rest = rest
    else:
        old_in_ref, old_back_ref, out_ref, in_keep_ref, in_send_ref, back_keep_ref, back_send_ref = rest[:7]
        acc_scr, grad_scr = rest[7:]
    f = pl.program_id(0)
    width = x_ref.shape[-1]

    @pl.when(f == 0)
    def _():
        acc_scr[...] = jnp.zeros_like(acc_scr)
        if not raw:
            grad_scr[...] = c_ref[...]
            return
        c_scr, ids_scr = rest
        up = -(-capacity // 8) * 8
        same = lax.broadcasted_iota(jnp.int32, (up, LANES), 0) == lax.broadcasted_iota(
            jnp.int32, (up, LANES), 1
        )
        for s in range(c_ref.shape[0] // padded):
            block = c_ref[s * padded : (s + 1) * padded, :].astype(f32)
            c_scr[s * capacity : (s + 1) * capacity, :] = block[:capacity]
            line = block[capacity : capacity + 1, :LANES]
            column = jnp.sum(jnp.where(same, line, 0.0), axis=1, keepdims=True)
            ids_scr[s * capacity : (s + 1) * capacity, 0:1] = column[:capacity]
        ids = ids_scr[:, 0:1].astype(jnp.int32)
        logits = dot(x_ref[...], dense_ref[...])
        lane = lax.broadcasted_iota(jnp.int32, logits.shape, 1)
        own = jnp.sum(jnp.where(lane == idx_ref[1], logits, 0.0), axis=1, keepdims=True)
        other = jnp.sum(jnp.where(lane == ids, logits, 0.0), axis=1, keepdims=True)
        peak = jnp.maximum(own, other)
        own = jnp.exp(own - peak)
        gate = own / (own + jnp.exp(other - peak))
        grad_scr[...] = (gate * c_scr[...]).astype(bf16)

    pre = dot(x_ref[...], win_ref[...])
    c0 = 0.7978845608028654
    square = pre * pre
    t = jnp.tanh(pre * (c0 + (c0 * 0.044715) * square))
    hidden = (0.5 * pre * (1.0 + t)).astype(bf16)
    slope = 0.5 * (1.0 + t) + 0.5 * pre * (1.0 - t * t) * (c0 + (3 * c0 * 0.044715) * square)
    acc_scr[:, :width] += dot(hidden, wback_ref[...])
    pre_grad = (dot(grad_scr[...], wback_ref[...], NT) * slope).astype(bf16)
    acc_scr[:, width:] += dot(pre_grad, win_ref[...], NT)
    grad_in = dot(x_ref[...], pre_grad, TN)
    grad_back = dot(hidden, grad_scr[...], TN)
    if raw:
        in_ref[...] = grad_in.astype(bf16)
        back_ref[...] = grad_back.astype(bf16)
    else:
        grad_in = (grad_in + old_in_ref[...].astype(f32)).astype(bf16)
        grad_back = (grad_back + old_back_ref[...].astype(f32)).astype(bf16)
        half, rows, _ = in_keep_ref.shape
        for b in range(2 * half):
            at = pos_ref[b]
            block = grad_in[b * rows : (b + 1) * rows]

            @pl.when(at < half)
            def _():
                in_keep_ref[at] = block

            @pl.when(at >= half)
            def _():
                in_send_ref[at - half] = block

        @pl.when(f < half)
        def _():
            back_send_ref[...] = grad_back

        @pl.when(f >= half)
        def _():
            back_keep_ref[...] = grad_back

    @pl.when(f == pl.num_programs(0) - 1)
    def _():
        out_ref[...] = acc_scr[...].astype(bf16)


def combine_kernel(n, experts, first, after, idx_ref, back_ref, places_ref, routes_ref, mixed_ref, cot_ref, dense_ref, *rest):
    att_refs, rest = rest[:n], rest[n:]
    if not first:
        old_ref, *rest = rest
    rest = rest[after:]
    out_ref, mg_ref, branch_ref, new_ref, *da_refs = rest
    tok, part = att_refs[0].shape
    width = mixed_ref.shape[-1]
    total = back_ref.shape[0]
    gain = dense_gain(dense_ref)
    mixed = mixed_ref[...]
    rr = rsq(mixed)
    normed = (mixed * rr * gain).astype(bf16)
    router = dense_ref[:, width:]
    route, gates = gates_of(normed, router, routes_ref[...])
    slot = lax.broadcasted_iota(jnp.int32, (tok, total), 1)
    hits = [jnp.where(slot == places_ref[:, k : k + 1], 1.0, 0.0) for k in range(TOP)]
    results = back_ref[:, :width]
    returned = [dot(h.astype(bf16), results) for h in hits]
    moe = gates[0] * returned[0] + gates[1] * returned[1]
    out_ref[...] = (mixed + moe).astype(bf16)
    up = cot_ref[...].astype(f32)
    gate_grad = [jnp.sum(up * v, axis=1, keepdims=True) for v in returned]
    centre = gates[0] * gate_grad[0] + gates[1] * gate_grad[1]
    chosen_grad = [gates[k] * (gate_grad[k] - centre) for k in range(TOP)]
    logit_grad = jnp.where(route[0], chosen_grad[0], 0.0) + jnp.where(route[1], chosen_grad[1], 0.0)
    high = logit_grad.astype(bf16)
    low = (logit_grad - high.astype(f32)).astype(bf16)
    normed_grad = dot((hits[0] + hits[1]).astype(bf16), back_ref[:, width:])
    normed_grad = normed_grad + dot(high, router, NT) + dot(low, router, NT)
    router_grad = dot(normed, high, TN) + dot(normed, low, TN)
    scaled = mixed * rr
    gain_part = jnp.sum(normed_grad * scaled, axis=0, keepdims=True)
    ng = gain * normed_grad
    mixed_grad = up + rr * (ng - scaled * jnp.mean(ng * scaled, axis=-1, keepdims=True))
    mg_ref[...] = mixed_grad
    branch = mixed_grad.astype(bf16)
    gain_col = jnp.broadcast_to(gain_part, (LANES, width)).T
    lane = lax.broadcasted_iota(jnp.int32, gain_col.shape, 1)
    extra = jnp.where(lane == experts, gain_col, router_grad)
    if not first:
        extra = extra + old_ref[...]
    new_ref[...] = extra
    branch_ref[...] = branch
    for r in range(n):
        at = head_rows(idx_ref[0], r, part, width, n)
        da_refs[r][...] = dot(branch, dense_ref[at, :width], NT).astype(bf16)


def dense_grad_kernel(n, micros, idx_ref, *rest):
    keep_ref, send_ref, scr = rest[-3:]
    part = rest[1].shape[1]
    width, half = keep_ref.shape[0], keep_ref.shape[1]
    for r in range(n):
        at = head_rows(idx_ref[0], r, part, width, n)

        def add_grad(at=at, r=r):
            scr[at, :] = sum(
                dot(rest[m * (n + 1) + 1 + r][...], rest[m * (n + 1)][...], TN) for m in range(micros)
            )

        if n * part > width:
            pl.when(jnp.bitwise_xor(idx_ref[0], r) * part < width)(add_grad)
        else:
            add_grad()
    upper = jnp.bitwise_and(idx_ref[0], 1) == 1
    low, high = scr[:, :half], scr[:, half:]
    keep_ref[...] = jnp.where(upper, high, low).astype(bf16)
    send_ref[...] = jnp.where(upper, low, high).astype(bf16)


def token_grad_kernel(count, x_ref, mg_ref, gain_ref, *rest):
    parts, out_ref = rest[:count], rest[-1]
    grad = parts[0][...].astype(f32)
    for p in parts[1:]:
        grad = grad + p[...].astype(f32)
    x = x_ref[...].astype(f32)
    r = rsq(x)
    scaled = x * r
    ng = gain_ref[...] * grad
    out_ref[...] = (
        mg_ref[...] + r * (ng - scaled * jnp.mean(ng * scaled, axis=-1, keepdims=True))
    ).astype(bf16)


def swap(x, axis, by):
    return lax.ppermute(x, axis, [(i, i ^ by) for i in range(lax.axis_size(axis))])


def exchange(x, axes):
    return lax.all_to_all(x, axes, split_axis=0, concat_axis=0, tiled=True)


def bit_reversed(n):
    bits = n.bit_length() - 1
    return [int(format(r, "b").zfill(bits)[::-1], 2) if bits else 0 for r in range(n)]


def add_kernel(*refs):
    count = len(refs) // 4
    for i in range(count):
        total = refs[2 * i][...].astype(f32) + refs[2 * i + 1][...].astype(f32)
        rows = total.shape[1] // 2
        refs[2 * count + 2 * i][...] = total[:, :rows].astype(bf16)
        refs[2 * count + 2 * i + 1][...] = total[:, rows:].astype(bf16)


def halving_start(grads, axis):
    cames = [swap(send, axis, 1) for _, send in grads]
    arrays = []
    specs = []
    outs = []
    out_specs = []
    for (keep, _), came in zip(grads, cames):
        half, (rows, cols) = keep.shape[0] // 2, keep.shape[1:]
        arrays += [keep, came]
        specs += [pl.BlockSpec((half, rows, cols), lambda _: (1, 0, 0))] * 2
        outs += [jax.ShapeDtypeStruct((half, rows // 2, cols), bf16)] * 2
        out_specs += [pl.BlockSpec((half, rows // 2, cols), lambda _: (0, 0, 0))] * 2
    fars = pl.pallas_call(
        add_kernel,
        grid=(1,),
        out_shape=outs,
        in_specs=specs,
        out_specs=out_specs,
        compiler_params=pltpu.CompilerParams(vmem_limit_bytes=60 * MIB),
        name="add",
    )(*arrays)
    pieces = []
    for i, ((keep, _), came) in enumerate(zip(grads, cames)):
        half, rows = keep.shape[0] // 2, keep.shape[1] // 2
        for j, piece in enumerate((slice(0, rows), slice(rows, None))):
            pieces.append(([keep[:half, piece], came[:half, piece]], fars[2 * i + j]))
    return pieces


def halving_end(terms, far, axis):
    by = 2
    while True:
        half = terms[0].shape[0] // 2
        came = swap(far, axis, by)
        terms = terms + [came]
        if not half:
            return sum(t[0].astype(f32) for t in terms), came
        far = sum(t[half:].astype(f32) for t in terms).astype(bf16)
        terms = [t[:half] for t in terms]
        by *= 2


def bits_of(axis):
    return [1 << i for i in range(lax.axis_size(axis).bit_length() - 1)][::-1]


def upper_half(axis, by):
    return lax.rem(lax.div(lax.axis_index(axis), by), 2) == 1


def by_distance(x, axis, after=(), came=None):
    blocks = {0: x}
    by = lax.axis_size(axis) // 2
    if came is not None:
        blocks[by] = gate(came, *after)
        after = ()
        by //= 2
    while by:
        for r in list(blocks):
            blocks[r ^ by] = swap(blocks[r], axis, by)
        by //= 2
        if after and by:
            blocks.update({r: gate(b, *after) for r, b in blocks.items() if r})
            after = ()
    return [blocks[r] for r in range(len(blocks))]


def sum_kernel(count, *refs):
    refs[-1][...] = sum(r[...].astype(f32) for r in refs[:count]).astype(bf16)


def halving_terms(parts, axis, after=lambda: ()):
    terms = {r: [p] for r, p in enumerate(parts)}
    total = parts[0]
    by = 1
    while by < len(parts):
        for r in [r for r in terms if r & by]:
            held = terms.pop(r)
            total = held[0]
            if len(held) > 1:
                (total,) = call(
                    functools.partial(sum_kernel, len(held)),
                    [(total.shape, bf16)],
                    "sum",
                    arrays=held,
                    after=after(),
                )
            terms[r ^ by].append(swap(total, axis, by))
        by *= 2
    return terms[0], total


def shards(
    tokens, doc_lengths, routes, slots, w_qkv, w_out, rel_bias, gain_attn, gain_ffn, w_router, w_in, w_back, cotangent
):
    micros, _, tok, width = tokens.shape
    n = lax.axis_size("dp")
    experts = lax.axis_size("expert")
    me = lax.axis_index("dp")
    my_expert = lax.axis_index("expert")
    reach = min((WINDOW - 2) // tok + 1, n - 1)
    spans = reach + 1
    capacity = (9 * tok * TOP + 8 * experts - 1) // (8 * experts)
    total = experts * capacity
    length = n * tok
    heads = -(-H // n)
    groups = -(-heads // 2)
    part = heads * HD
    wide = groups * LANES
    ff = w_in.shape[2]
    own_rows = w_qkv.shape[0]
    whole_count = n * experts
    both = ("dp", "expert")
    tokens, cotangent = tokens[:, 0], cotangent[:, 0]
    routes, slots = routes[:, 0], slots[:, 0]
    idx = jnp.stack([me, my_expert]).astype(jnp.int32)

    packed = packed_blocks(heads) * LANES
    share = dense_share(n, width)
    (columns,) = call(
        functools.partial(pack_kernel, n),
        [((whole_count, own_rows, packed + share), bf16)],
        "pack",
        arrays=[w_qkv, gain_attn[None], w_out, w_router.T, gain_ffn[None]],
    )
    w_mine = exchange(columns, both).reshape(width, packed + share)

    places = jnp.where(slots >= 0, routes * capacity + slots, total)
    places_row = places.transpose(0, 2, 1)
    padded = -(-(capacity + 1) // 8) * 8
    padded_places = jnp.where(slots[0] >= 0, routes[0] * padded + slots[0], experts * padded)
    (cot_rows,) = call(
        functools.partial(dispatch_kernel, capacity, padded),
        [((experts * padded, width), bf16)],
        "dispatch_cotangent",
        arrays=[padded_places.T, padded_places, routes[0, :, ::-1], (cotangent, 0)],
        after=[columns],
        flops=2 * total * tok * width,
    )

    bias = jnp.pad(rel_bias.astype(f32).T, ((0, heads * n - H), (0, 0)))
    bias = lax.dynamic_slice_in_dim(bias, me * heads, heads, 0)[:, : spans * tok]
    band = jnp.concatenate(
        [
            jnp.full((heads, tok), MASKED, f32),
            bias,
            jnp.full((heads, spans * tok - bias.shape[1]), MASKED, f32),
        ],
        axis=1,
    )
    band = jnp.pad(band, ((0, -heads % 8), (0, 0)))
    (tiles,) = call(
        functools.partial(tiles_kernel, spans, tok),
        [((heads, spans, tok, tok), f32)],
        "bias_tiles",
        arrays=[band],
        after=[columns],
    )
    doc_ends = jnp.cumsum(doc_lengths[:, 0], axis=-1)
    positions = jnp.arange(length, dtype=jnp.int32)
    docs = jnp.sum((doc_ends[:, None, :] <= positions[None, :, None]).astype(jnp.int32), axis=2)
    kdocs, qdocs = docs[:, :, None], docs[:, None, :]

    assert micros == 2
    xs = [by_distance(tokens[0], "dp", [cot_rows, tiles, kdocs])]
    second = swap(gate(tokens[1], tiles), "dp", n // 2)

    cot_rows = gate(cot_rows, w_mine, tiles, xs[0][-1], kdocs, second)
    cot_rows = exchange(cot_rows.reshape(experts, padded, width), "expert").reshape(-1, width)

    att = []
    saved = []
    pair_flops = 2 * heads * LANES * tok * tok * sum(min(j, reach) + 1 for j in range(n))
    w_heads = w_mine
    gain_a = None
    for m in range(micros):
        first = m == 0
        if not first:
            xs.append(by_distance(tokens[1], "dp", [saved[0][1]], second))
        made = call(
            functools.partial(attn_fwd_kernel, n, reach, heads, first),
            [((tok, part), bf16)] * n
            + [((3 * groups, length, LANES), bf16), ((8, length), f32)]
            + ([((width, 3 * wide), bf16), ((1, width), f32)] if first else []),
            "attention_forward",
            smem=[idx],
            arrays=[
                w_heads,
                *([] if first else [gain_a]),
                (kdocs, m),
                (qdocs, m),
                *xs[m],
            ],
            hbm=[tiles],
            hbm_out=[n],
            flops=2 * length * width * 3 * wide + 2 * pair_flops,
            scratch=[
                pltpu.VMEM((wide, length), bf16),
                pltpu.VMEM((wide, length), f32),
                pltpu.VMEM((length, wide), bf16),
                pltpu.VMEM(tiles.shape, f32),
                pltpu.VMEM((3 * groups, length, LANES), bf16),
                pltpu.SemaphoreType.DMA,
                pltpu.SemaphoreType.DMA,
            ],
        )
        att_m, (qkv, lse, *more) = made[:n], made[n:]
        if first:
            w_heads, gain_a = more
        att.append([att_m[0]] + [swap(att_m[r], "dp", r) for r in range(1, n)])
        saved.append((qkv, lse))

    shares = by_distance(w_mine[:, packed:], "dp", [saved[0][1]])
    mixed = []
    arrived = []
    dense = None
    for m in range(micros):
        first = m == 0
        mixed_m, rows, *more = call(
            functools.partial(mid_kernel, n, first),
            [((tok, width), f32), ((total, width if first else 2 * width), bf16)]
            + ([((width, width + LANES), bf16)] if first else []),
            "mix_and_dispatch",
            smem=[idx],
            arrays=[(tokens, m), (places_row, m), *att[m], *(shares if first else [dense, (routes, m), (cotangent, m)])],
            after=[xs[1][-1]] if first else [],
            scratch=[pltpu.VMEM((width, n * share), bf16)] if first else [],
            flops=2 * tok * width * width + 2 * total * tok * width,
        )
        if first:
            (dense,) = more
            rows = gate(rows, cot_rows)
        mixed.append(mixed_m)
        arrived.append(exchange(rows.reshape(experts, capacity, -1), "expert").reshape(total, -1))

    cols = ff // n
    reverse = jnp.asarray(bit_reversed(n), jnp.int32)
    pos = reverse[jnp.bitwise_xor(jnp.arange(n, dtype=jnp.int32), me)]
    src = jnp.bitwise_xor(jnp.roll(reverse, -(n // 2)), me)
    whole = lambda shape, c=0: pl.BlockSpec(shape, lambda f, *_, c=c: (0, c))
    in_block = pl.BlockSpec((width, cols), lambda f, src, pos: (0, src[f]))
    back_block = pl.BlockSpec((cols, width), lambda f, src, pos: (src[f], 0))
    half_block = pl.BlockSpec((n // 2, width // n, cols), lambda f, src, pos: (0, 0, src[f]))
    results = []
    grads = []
    for m in range(micros):
        raw = m == 0
        result, *grads = pl.pallas_call(
            functools.partial(expert_kernel, raw, capacity, padded),
            out_shape=[jax.ShapeDtypeStruct((total, 2 * width), bf16)]
            + (
                [jax.ShapeDtypeStruct((width, ff), bf16), jax.ShapeDtypeStruct((ff, width), bf16)]
                if raw
                else [jax.ShapeDtypeStruct((n // 2, width // n, ff), bf16)] * 2
                + [jax.ShapeDtypeStruct((n // 2, cols, width), bf16)] * 2
            ),
            grid_spec=pltpu.PrefetchScalarGridSpec(
                num_scalar_prefetch=2,
                grid=(n,),
                in_specs=[
                    pl.BlockSpec(memory_space=pltpu.SMEM),
                    whole((total, width)),
                    whole(cot_rows.shape) if raw else whole((total, width), 1),
                    whole((width, LANES), width // LANES),
                    pl.BlockSpec((None, width, cols), lambda f, src, pos: (0, 0, src[f])),
                    pl.BlockSpec((None, cols, width), lambda f, src, pos: (0, src[f], 0)),
                ]
                + ([] if raw else [in_block, back_block]),
                out_specs=[whole((total, 2 * width))]
                + (
                    [in_block, back_block]
                    if raw
                    else [
                        half_block,
                        half_block,
                        pl.BlockSpec(
                            (None, cols, width), lambda f, src, pos: (jnp.maximum(f - n // 2, 0), 0, 0)
                        ),
                        pl.BlockSpec(
                            (None, cols, width), lambda f, src, pos: (jnp.minimum(f, n // 2 - 1), 0, 0)
                        ),
                    ]
                ),
                scratch_shapes=[
                    pltpu.VMEM((total, 2 * width), f32),
                    pltpu.VMEM((total, width), bf16),
                ]
                + ([pltpu.VMEM((total, width), f32), pltpu.VMEM((total, LANES), f32)] if raw else []),
            ),
            compiler_params=pltpu.CompilerParams(vmem_limit_bytes=60 * MIB),
            cost_estimate=pl.CostEstimate(
                flops=12 * total * width * ff, transcendentals=total * ff, bytes_accessed=24 * MIB
            ),
            name="expert",
        )(src, pos, idx, arrived[m], cot_rows if raw else arrived[m], dense, w_in, w_back, *grads)
        results.append(result)
    in_keep, in_send, back_keep, back_send = grads
    pieces = halving_start([(in_keep, in_send), (back_keep, back_send)], "dp")
    results[1] = gate(results[1], *[far for _, far in pieces])
    back = [
        exchange(r.reshape(experts, capacity, 2 * width), "expert").reshape(total, 2 * width) for r in results
    ]

    out = token_grad = None
    dense_grad = []
    branches = []
    attn_grad = []
    grad_w = []
    ends = [halving_end(*pieces[0], "dp")]
    across = -(-heads * min(spans * tok, WINDOW) // (own_rows * LANES)) * LANES
    lanes = packed + across + width // 2
    for m in range(micros):
        first, last = m == 0, m == micros - 1
        after = [] if first else [grad_w[0], ends[0][1], ends[1][1], first_sent]
        out, mixed_grad, branch, new_grad, *da = call(
            functools.partial(combine_kernel, n, experts, first, len(after) + (out is not None)),
            [
                ((micros, tok, width), bf16),
                ((tok, width), f32),
                ((tok, width), bf16),
                ((width, LANES), f32),
            ]
            + [((tok, part), bf16)] * n,
            "combine",
            smem=[idx],
            arrays=[
                back[m],
                (places, m),
                (routes, m),
                mixed[m],
                (cotangent, m),
                dense,
                *att[m],
                *dense_grad,
            ],
            after=after,
            flops=6 * total * tok * width + 4 * tok * width * width,
            out_micro=[(0, m, out)],
        )
        dense_grad = [new_grad]
        branches += [branch, *att[m]]
        da = [da[0]] + [swap(da[r], "dp", r) for r in range(1, n)]
        qkv, lse = saved[m]
        after = []
        for terms, far in pieces[1:3] if first else pieces[3:]:
            far = gate(far, *da[1:])
            after.append(far)
            ends.append(halving_end(terms, far, "dp"))
        if not first:
            dense_halves = call(
                functools.partial(dense_grad_kernel, n, micros),
                [((width, width // 2), bf16)] * 2,
                "dense_grad",
                smem=[idx],
                arrays=branches,
                flops=2 * micros * tok * width * width,
                scratch=[pltpu.VMEM((width, width), f32)],
            )
            after += [ends[2][1], dense_halves[1]]
        made = call(
            functools.partial(attn_bwd_kernel, n, reach, heads, first, len(after)),
            [((tok, width), bf16)] * n
            + [((length, 3 * wide), bf16), ((1, width), f32), ((8, spans * tok), f32)],
            "attention_backward",
            smem=[idx],
            arrays=[(kdocs, m), (qdocs, m), qkv, lse, *da, *attn_grad],
            hbm=[tiles, w_heads, *xs[m]],
            after=after,
            flops=2 * length * width * 3 * wide + 5 * pair_flops,
            scratch=[
                pltpu.VMEM((groups, length, LANES), bf16),
                pltpu.VMEM((wide, length), bf16),
                pltpu.VMEM((wide, length), f32),
                pltpu.VMEM((2 * groups, length, LANES), f32),
                pltpu.VMEM((heads, spans, tok, tok), f32),
                pltpu.VMEM(tiles.shape, f32),
                pltpu.VMEM((width, 3 * wide), bf16),
                pltpu.VMEM((n, tok, width), bf16),
            ]
            + [pltpu.SemaphoreType.DMA] * (2 + n),
        )
        parts, (dqkv, *attn_grad) = made[:n], made[n:]
        dense_parts = []
        if last:
            dense_parts = [dense_halves[0], swap(dense_halves[1], "dp", 1)]
        *grad_w, mark = call(
            functools.partial(qkv_grad_kernel, n, heads, own_rows, first, last),
            [((width, lanes), bf16) if last else ((width, 3 * wide), bf16), ((8, LANES), f32)],
            "qkv_grad",
            smem=[idx],
            arrays=[gain_a, *xs[m], *([*attn_grad, *dense_grad] if last else [])],
            hbm=[dqkv, *grad_w, *dense_parts],
            flops=2 * length * width * 3 * wide,
            scratch=[pltpu.VMEM((length, width), bf16)]
            + [pltpu.VMEM(x.shape, bf16) for x in (dqkv, *grad_w, *dense_parts)]
            + [pltpu.SemaphoreType.DMA] * (1 + len(grad_w) + len(dense_parts)),
        )
        summed, sent_last = halving_terms(parts, "dp", lambda: [mark] if last else [])
        if first:
            first_came, first_sent = summed[-1], sent_last
        (token_grad,) = call(
            functools.partial(token_grad_kernel, len(summed)),
            [((micros, tok, width), bf16)],
            "token_grad",
            arrays=[(tokens, m), mixed_grad, gain_a, *summed],
            out_micro=[(0, m, token_grad)],
        )

    message = gate(grad_w[0], ends[3][1], first_came)
    message = exchange(message.reshape(whole_count, own_rows, lanes), both)
    grad_qkv, grad_bias, grad_router, grad_gain_a, grad_gain_f, dense_sum = call(
        functools.partial(finish_kernel, n, across),
        [
            ((own_rows, 3 * width), f32),
            ((H, WINDOW), f32),
            ((experts, own_rows), f32),
            ((1, own_rows), f32),
            ((1, own_rows), f32),
            ((own_rows, width), f32),
        ],
        "finish",
        arrays=[message],
    )
    return (
        out[:, None],
        token_grad[:, None],
        grad_qkv,
        dense_sum,
        grad_bias.T,
        grad_gain_a[0],
        grad_gain_f[0],
        grad_router.T,
        jnp.concatenate([ends[0][0], ends[1][0]])[None],
        jnp.concatenate([ends[2][0], ends[3][0]])[None],
    )


def solution(mesh):
    return jax.shard_map(
        shards,
        mesh=mesh,
        in_specs=(
            P(None, "expert", "dp", None),
            P(None, "expert", None),
            P(None, "expert", "dp", None),
            P(None, "expert", "dp", None),
            P(("dp", "expert"), None),
            P(("dp", "expert"), None),
            P(),
            P(("dp", "expert")),
            P(("dp", "expert")),
            P(("dp", "expert"), None),
            P("expert", None, None),
            P("expert", None, None),
            P(None, "expert", "dp", None),
        ),
        out_specs=(
            P(None, "expert", "dp", None),
            P(None, "expert", "dp", None),
            P(("dp", "expert"), None),
            P(("dp", "expert"), None),
            P(),
            P(("dp", "expert")),
            P(("dp", "expert")),
            P(("dp", "expert"), None),
            P("expert", "dp", None),
            P("expert", "dp", None),
        ),
        check_vma=False,
    )
```

```python
import functools

import jax
import jax.numpy as jnp
from jax import lax
from jax.experimental import pallas as pl
from jax.experimental.pallas import tpu as pltpu
from jax.sharding import PartitionSpec as P

H = 12
HD = 64
TOP = 2
WINDOW = 1024
EPSILON = 1e-06
MASKED = -1e30
LANES = 128

bf16 = jnp.bfloat16
f32 = jnp.float32
MIB = 1 << 20

NN = (((1,), (0,)), ((), ()))
NT = (((1,), (1,)), ((), ()))
TN = (((0,), (0,)), ((), ()))


def dot(a, b, dims=NN):
    return lax.dot_general(a, b, dims, preferred_element_type=f32)


def rsq(x):
    return lax.rsqrt(jnp.mean(x * x, axis=-1, keepdims=True) + EPSILON)


def call(kernel, outs, name, smem=(), arrays=(), after=(), flops=0, scratch=(), limit=60, out_micro=(), hbm=(), hbm_out=()):
    def spec(x):
        if isinstance(x, tuple):
            x, i = x
            return pl.BlockSpec((None,) + x.shape[1:], lambda _: (i,) + (0,) * (x.ndim - 1))
        return pl.BlockSpec(x.shape, lambda _: (0,) * x.ndim)

    arrays = list(arrays)
    given = [x[0] if isinstance(x, tuple) else x for x in arrays]
    micro_of = {k: i for k, i, _ in out_micro}
    olds = [(k, old) for k, _, old in out_micro if old is not None]

    def out_spec(k, s):
        if k in hbm_out:
            return pl.BlockSpec(memory_space=pl.ANY)
        if k in micro_of:
            return pl.BlockSpec((None,) + s[1:], lambda _: (micro_of[k],) + (0,) * (len(s) - 1))
        return pl.BlockSpec(s, lambda _: (0,) * len(s))

    after = list(hbm) + list(after) + [old for _, old in olds]
    aliases = {len(smem) + len(arrays) + len(after) - len(olds) + i: k for i, (k, _) in enumerate(olds)}
    size = lambda shape, dtype: int(jnp.dtype(dtype).itemsize * functools.reduce(lambda p, q: p * q, shape, 1))
    moved = sum(size(x.shape, x.dtype) for x in given) + sum(size(*o) for o in outs)
    return pl.pallas_call(
        kernel,
        grid=(1,),
        out_shape=[jax.ShapeDtypeStruct(s, d) for s, d in outs],
        in_specs=[pl.BlockSpec(memory_space=pltpu.SMEM)] * len(smem)
        + [spec(x) for x in arrays]
        + [pl.BlockSpec(memory_space=pl.ANY)] * len(after),
        out_specs=[out_spec(k, s) for k, (s, _) in enumerate(outs)],
        input_output_aliases=aliases,
        scratch_shapes=list(scratch),
        compiler_params=pltpu.CompilerParams(vmem_limit_bytes=limit * MIB),
        cost_estimate=pl.CostEstimate(flops=int(flops), transcendentals=0, bytes_accessed=moved),
        name=name,
    )(*smem, *given, *after)


def gate(x, *after):
    hbm = pl.BlockSpec(memory_space=pl.ANY)
    return pl.pallas_call(
        lambda *refs: None,
        out_shape=jax.ShapeDtypeStruct(x.shape, x.dtype),
        in_specs=[hbm] * (1 + len(after)),
        out_specs=hbm,
        input_output_aliases={0: 0},
        name="gate",
    )(x, *after)


def packed_blocks(heads):
    return 3 * (heads // 2) + (2 if heads % 2 else 1)


def gain_place(heads):
    return packed_blocks(heads) - 1, HD if heads % 2 else 0


def head_place(heads, kind, h):
    if heads % 2 and h == heads - 1:
        return 3 * (heads // 2) + kind // 2, kind % 2
    return 3 * (h // 2) + kind, h % 2


def low_lanes(shape):
    return lax.broadcasted_iota(jnp.int32, shape, 1) < HD


def move_half(block, source, target):
    return block if source == target else pltpu.roll(block, HD, axis=1)


def column_of(row):
    n = row.shape[1]
    same = lax.broadcasted_iota(jnp.int32, (n, n), 0) == lax.broadcasted_iota(jnp.int32, (n, n), 1)
    return jnp.sum(jnp.where(same, row, 0.0), axis=1, keepdims=True)


def dense_share(n, width):
    return -(-(width + LANES) // (n * LANES)) * LANES


def pack_kernel(n, w_ref, gain_ref, w_out_ref, router_ref, gain_ffn_ref, out_ref):
    count, rows, _ = out_ref.shape
    copies = count // n
    heads = -(-H // n)
    width = w_ref.shape[1] // 3
    low = low_lanes((rows, LANES))
    lane = lax.broadcasted_iota(jnp.int32, (rows, LANES), 1)
    gain = column_of(gain_ref[...].astype(f32))
    gain_block, gain_lane = gain_place(heads)
    for d in range(n):
        found = {}
        for kind in range(3):
            for h in range(heads):
                head = d * heads + h
                if head >= H:
                    continue
                block, half = head_place(heads, kind, h)
                column = kind * width + head * HD
                start = column // LANES * LANES
                piece = move_half(
                    w_ref[:, start : start + LANES].astype(f32), (column - start) // HD, half
                )
                found[block, half] = piece
        for block in range(packed_blocks(heads)):
            none = jnp.zeros((rows, LANES), f32)
            value = jnp.where(low, found.get((block, 0), none), found.get((block, 1), none))
            if block == gain_block:
                value = jnp.where(lane == gain_lane, gain, value)
            value = value.astype(bf16)
            for e in range(copies):
                out_ref[d * copies + e, :, block * LANES : (block + 1) * LANES] = value
    share = dense_share(n, width)
    gain = column_of(gain_ffn_ref[...].astype(f32))
    router = jnp.concatenate(
        [router_ref[...].astype(f32), jnp.zeros((LANES - router_ref.shape[0], rows), f32)], axis=0
    ).T
    router = jnp.where(lane == LANES - 1, gain, router).astype(bf16)
    for d in range(n):
        for c in range(0, share, LANES):
            column = d * share + c
            if column < width:
                value = w_out_ref[:, column : column + LANES]
            elif column == width:
                value = router
            else:
                value = jnp.zeros((rows, LANES), bf16)
            at = packed_blocks(heads) * LANES + c
            for e in range(copies):
                out_ref[d * copies + e, :, at : at + LANES] = value


def unpack_qkv(heads, w_ref, w_scr):
    groups = -(-heads // 2)
    rows = w_ref.shape[0]
    low = low_lanes((rows, LANES))
    for kind in range(3):
        for g in range(groups):
            block, half = head_place(heads, kind, 2 * g)
            value = w_ref[:, block * LANES : (block + 1) * LANES]
            if 2 * g + 1 == heads:
                value = jnp.where(low, move_half(value.astype(f32), half, 0), 0.0).astype(bf16)
            at = (kind * groups + g) * LANES
            w_scr[:, at : at + LANES] = value
    block, lane = gain_place(heads)
    turned = w_ref[:, block * LANES : (block + 1) * LANES].astype(f32).T
    return turned[lane : lane + 1]


def pack_grad(heads, grad, gain_row, extra, out_ref):
    groups = -(-heads // 2)
    rows = grad.shape[0]
    low = low_lanes((rows, LANES))
    lane = lax.broadcasted_iota(jnp.int32, (rows, LANES), 1)
    part = lambda kind, g: grad[:, (kind * groups + g) * LANES : (kind * groups + g + 1) * LANES]
    blocks = [part(kind, g) for g in range(heads // 2) for kind in range(3)]
    if heads % 2:
        g = groups - 1
        blocks.append(jnp.where(low, part(0, g), pltpu.roll(part(1, g), HD, axis=1)))
        blocks.append(jnp.where(low, part(2, g), 0.0))
    else:
        blocks.append(jnp.zeros((rows, LANES), f32))
    gain_col = jnp.broadcast_to(gain_row, (LANES, rows)).T
    _, gain_lane = gain_place(heads)
    blocks[-1] = jnp.where(lane == gain_lane, gain_col, blocks[-1])
    blocks[-1] = jnp.where(lane > gain_lane, pltpu.roll(extra, gain_lane + 1, axis=1), blocks[-1])
    for i, block in enumerate(blocks):
        out_ref[:, i * LANES : (i + 1) * LANES] = block.astype(bf16)


def finish_kernel(n, across, message_ref, qkv_ref, bias_ref, router_ref, gain_ref, gain_ffn_ref, dense_ref):
    count, rows, lanes = message_ref.shape
    copies = count // n
    heads = -(-H // n)
    width = qkv_ref.shape[1] // 3
    packed = packed_blocks(heads) * LANES
    low = low_lanes((rows, LANES))
    sums = []
    gain_block, gain_lane = gain_place(heads)
    gain = None
    for d in range(n):
        total = message_ref[d * copies].astype(f32)
        for e in range(1, copies):
            total = total + message_ref[d * copies + e].astype(f32)
        sums.append(total)
        term = total[:, gain_block * LANES : (gain_block + 1) * LANES]
        gain = term if gain is None else gain + term
    count = router_ref.shape[0]
    turned = jnp.concatenate([gain, jnp.zeros((-rows % 8, LANES), f32)], axis=0).T if rows % 8 else gain.T
    router_ref[...] = turned[gain_lane + 1 : gain_lane + 1 + count, :rows]
    gain_ref[...] = turned[gain_lane : gain_lane + 1, :rows]
    gain_ffn_ref[...] = turned[gain_lane + 1 + count : gain_lane + 2 + count, :rows]
    wide = across // LANES
    lines = min(WINDOW, rows * across // heads) // LANES
    for c in range(lines):
        found = []
        for head in range(H):
            row, place = divmod(head % heads * lines + c, wide)
            at = packed + place * LANES
            found.append(sums[head // heads][row : row + 1, at : at + LANES])
        bias_ref[:, c * LANES : (c + 1) * LANES] = jnp.concatenate(found, axis=0)
    if lines * LANES < WINDOW:
        bias_ref[:, lines * LANES :] = jnp.zeros((H, WINDOW - lines * LANES), f32)
    half = dense_ref.shape[1] // 2
    for core in range(2):
        dense_ref[:, core * half : (core + 1) * half] = sum(t[:, lanes - half :] for t in sums[core::2])
    for kind in range(3):
        for pair in range(H // 2):
            halves = []
            for to in range(2):
                head = 2 * pair + to
                block, half = head_place(heads, kind, head % heads)
                value = sums[head // heads][:, block * LANES : (block + 1) * LANES]
                halves.append(move_half(value, half, to))
            at = kind * width + pair * LANES
            qkv_ref[:, at : at + LANES] = jnp.where(low, halves[0], halves[1])


def tiles_kernel(spans, rows, band_ref, *rest):
    out_ref = rest[-1]
    heads = out_ref.shape[0]
    for h in range(heads):
        for s in range(spans):
            ahead = band_ref[h : h + 1, (s + 1) * rows : (s + 2) * rows]
            behind = band_ref[h : h + 1, s * rows : (s + 1) * rows]
            line = jnp.concatenate([ahead, behind], axis=1)
            spread = jnp.broadcast_to(line, (rows, 2 * rows))
            rolled = pltpu.roll(spread, 0, axis=1, stride=1, stride_axis=0)
            out_ref[h, s] = rolled[:, :rows]


def pick_each(places, total):
    slot = lax.broadcasted_iota(jnp.int32, (total, places.shape[1]), 0)
    return [jnp.where(slot == places[k : k + 1], 1.0, 0.0) for k in range(TOP)]


def picks_of(places, total):
    return sum(pick_each(places, total)).astype(bf16)


def dispatch_kernel(capacity, padded, places_row_ref, places_ref, other_ref, cot_ref, after_ref, out_ref):
    tok = places_ref.shape[0]
    total, width = out_ref.shape
    experts = total // padded
    lane = lax.broadcasted_iota(jnp.int32, (tok, LANES), 1)
    lines = []
    for e in range(experts):
        slot = jnp.where(lane < capacity, lane + e * padded, -1)
        found = sum(
            jnp.where(slot == places_ref[:, k : k + 1], other_ref[:, k : k + 1].astype(f32), 0.0)
            for k in range(TOP)
        )
        lines.append(jnp.sum(found, axis=0, keepdims=True))
    spare = -experts % 16
    if spare:
        lines.append(jnp.zeros((spare, LANES), f32))
    lines = jnp.concatenate(lines, axis=0).astype(bf16)
    shape = (total, lines.shape[0])
    row = lax.broadcasted_iota(jnp.int32, shape, 0)
    here = row == lax.broadcasted_iota(jnp.int32, shape, 1) * padded + capacity
    ids = dot(jnp.where(here, 1.0, 0.0).astype(bf16), lines)
    rows = dot(picks_of(places_row_ref[...], total), cot_ref[...])
    out_ref[:, :LANES] = (rows[:, :LANES] + ids).astype(bf16)
    out_ref[:, LANES:] = rows[:, LANES:].astype(bf16)


def attn_fwd_kernel(n, reach, heads, first, idx_ref, w_ref, *rest):
    if not first:
        gain_ref, *rest = rest
    kdoc_ref, qdoc_ref, *rest = rest
    x_refs, rest = rest[:n], rest[n:]
    tiles_hbm, *rest = rest
    att_refs, rest = rest[:n], rest[n:]
    qkv_hbm, lse_ref, *rest = rest
    if first:
        heads_ref, gain_out_ref, *rest = rest
        gain = unpack_qkv(heads, w_ref, heads_ref)
        gain_out_ref[...] = gain
        w_ref = heads_ref
    else:
        gain = gain_ref[...]
    vt_scr, ot_scr, att_scr, tiles_ref, qkv_ref, tiles_sem, qkv_sem = rest
    tiles_copy = pltpu.make_async_copy(tiles_hbm, tiles_ref, tiles_sem)
    tiles_copy.start()
    tok = x_refs[0].shape[0]
    part = heads * HD
    groups = qkv_ref.shape[0] // 3
    me = idx_ref[0]
    for r in range(n):
        start = pl.multiple_of(jnp.bitwise_xor(me, r) * tok, tok)
        x = x_refs[r][...].astype(f32)
        normed = (x * rsq(x) * gain).astype(bf16)
        qkv = dot(normed, w_ref[...]).astype(bf16)
        for c in range(3 * groups):
            qkv_ref[c, pl.ds(start, tok), :] = qkv[:, c * LANES : (c + 1) * LANES]
    for g in range(groups):
        vt_scr[g * LANES : (g + 1) * LANES, :] = qkv_ref[2 * groups + g].astype(f32).T.astype(bf16)
    lse_ref[...] = jnp.zeros_like(lse_ref)
    qkv_copy = pltpu.make_async_copy(qkv_ref, qkv_hbm, qkv_sem)
    qkv_copy.start()
    tiles_copy.wait()

    lane = lax.broadcasted_iota(jnp.int32, (tok, LANES), 1)
    halves = [lane < HD, lane >= HD]

    def scores(h, j):
        lo = max(0, j - reach)
        q = qkv_ref[h // 2, j * tok : (j + 1) * tok, :].astype(f32)
        q = jnp.where(halves[h % 2], q * HD ** (-0.5), 0.0).astype(bf16)
        return dot(qkv_ref[groups + h // 2, lo * tok : (j + 1) * tok, :], q, NT)

    def attend(h, j, s):
        lo = max(0, j - reach)
        rows, cols = slice(lo * tok, (j + 1) * tok), slice(j * tok, (j + 1) * tok)
        bias = jnp.concatenate([tiles_ref[h, j - b] for b in range(lo, j + 1)], axis=0)
        s = jnp.where(kdoc_ref[rows, :] == qdoc_ref[:, cols], s + bias, MASKED)
        peak = jnp.max(s, axis=0, keepdims=True)
        e = jnp.exp(s - peak)
        total = jnp.sum(e, axis=0, keepdims=True)
        p = (e * (1.0 / total)).astype(bf16)
        lse_ref[h : h + 1, cols] = peak + jnp.log(total)
        return p

    def values(h, j, p):
        lo = max(0, j - reach)
        rows, cols = slice(lo * tok, (j + 1) * tok), slice(j * tok, (j + 1) * tok)
        ot_scr[h * HD : (h + 1) * HD, cols] = dot(vt_scr[h * HD : (h + 1) * HD, rows], p)

    work = [(h, j) for h in range(heads) for j in range(n)]
    ahead = scores(*work[0])
    for i, at in enumerate(work):
        s = ahead
        if i + 1 < len(work):
            ahead = scores(*work[i + 1])
        now = (*at, attend(*at, s))
        if i:
            values(*late)
        late = now
    values(*late)
    att_scr[...] = ot_scr[...].T.astype(bf16)
    for r in range(n):
        start = pl.multiple_of(jnp.bitwise_xor(me, r) * tok, tok)
        att_refs[r][...] = att_scr[pl.ds(start, tok), :part]
    qkv_copy.wait()


def unshear(tiles):
    rows = tiles[0].shape[0]
    span = 2 * rows
    wide = [jnp.concatenate([t, jnp.zeros_like(t)], axis=1) for t in tiles]
    count = rows
    while count > 8:
        count //= 2
        wide = [w[:count] + pltpu.roll(w[count:], span - count, axis=1) for w in wide]
    wide = jnp.concatenate(wide, axis=0)
    row = lax.broadcasted_iota(jnp.int32, wide.shape, 0)
    for bit in (4, 2, 1):
        wide = jnp.where(jnp.bitwise_and(row, bit) > 0, pltpu.roll(wide, span - bit, axis=1), wide)
    return [
        jnp.sum(wide[i * count : (i + 1) * count], axis=0, keepdims=True) for i in range(len(tiles))
    ]


def attn_bwd_kernel(
    n, reach, heads, first, after, idx_ref, kdoc_ref, qdoc_ref, qkv_ref, lse_ref, *rest
):
    da_refs, rest = rest[:n], rest[n:]
    if not first:
        old_small_ref, old_band_ref, *rest = rest
    tiles_hbm, w_hbm, *rest = rest
    x_hbms, rest = rest[:n], rest[n + after :]
    part_refs, rest = rest[:n], rest[n:]
    dqkv_ref, new_small_ref, new_band_ref, da_scr, kt_scr, dqt_scr, dkv_scr, acc_scr, *rest = rest
    tiles_ref, w_ref, x_scr, tiles_sem, w_sem, *x_sems = rest
    tiles_copy = pltpu.make_async_copy(tiles_hbm, tiles_ref, tiles_sem)
    tiles_copy.start()
    late_copies = [pltpu.make_async_copy(w_hbm, w_ref, w_sem)]
    late_copies += [
        pltpu.make_async_copy(x_hbms[r], x_scr.at[r], x_sems[r]) for r in range(n)
    ]
    tok = da_refs[0].shape[0]
    groups = qkv_ref.shape[0] // 3
    spans = tiles_ref.shape[1]
    wide = groups * LANES
    me = idx_ref[0]
    if heads * HD < wide:
        da_scr[...] = jnp.zeros_like(da_scr)
    for r in range(n):
        start = pl.multiple_of(jnp.bitwise_xor(me, r) * tok, tok)
        for g in range(groups):
            cols = min(LANES, heads * HD - g * LANES)
            da_scr[g, pl.ds(start, tok), :cols] = da_refs[r][:, g * LANES : g * LANES + cols]
    for g in range(groups):
        kt_scr[g * LANES : (g + 1) * LANES, :] = qkv_ref[groups + g].astype(f32).T.astype(bf16)
    dkv_scr[...] = jnp.zeros_like(dkv_scr)
    dqt_scr[...] = jnp.zeros_like(dqt_scr)
    acc_scr[...] = jnp.zeros_like(acc_scr)
    tiles_copy.wait()
    for copy in late_copies:
        copy.start()

    lane = lax.broadcasted_iota(jnp.int32, (tok, LANES), 1)
    halves = [lane < HD, lane >= HD]

    def places(j):
        lo = max(0, j - reach)
        return lo, slice(lo * tok, (j + 1) * tok), slice(j * tok, (j + 1) * tok)

    def products(h, j):
        _, rows, cols = places(j)
        q = qkv_ref[h // 2, cols, :].astype(f32)
        q = jnp.where(halves[h % 2], q * HD ** (-0.5), 0.0).astype(bf16)
        da = jnp.where(halves[h % 2], da_scr[h // 2, cols, :].astype(f32), 0.0).astype(bf16)
        s = dot(qkv_ref[groups + h // 2, rows, :], q, NT)
        return q, da, s, dot(qkv_ref[2 * groups + h // 2, rows, :], da, NT)

    def score_grads(h, j, s, pg):
        lo, rows, cols = places(j)
        bias = jnp.concatenate([tiles_ref[h, j - b] for b in range(lo, j + 1)], axis=0)
        s = jnp.where(kdoc_ref[rows, :] == qdoc_ref[:, cols], s + bias, MASKED)
        p = jnp.exp(s - lse_ref[h : h + 1, cols])
        centre = jnp.sum(p * pg, axis=0, keepdims=True)
        sg = (p * (pg - centre)).astype(bf16)
        for b in range(lo, j + 1):
            acc_scr[h, j - b] += sg[(b - lo) * tok : (b - lo + 1) * tok].astype(f32)
        return p.astype(bf16), sg

    def gather(h, j, q, da, p, sg):
        _, rows, cols = places(j)
        dkv_scr[h // 2, rows, :] += dot(sg, q)
        dkv_scr[groups + h // 2, rows, :] += dot(p, da)
        at = slice(h * HD, (h + 1) * HD)
        dqt_scr[at, cols] = dot(kt_scr[at, rows], sg) * HD ** (-0.5)

    work = [(h, j) for h in range(heads) for j in range(n)]
    ahead = products(*work[0])
    for i, at in enumerate(work):
        q, da, s, pg = ahead
        if i + 1 < len(work):
            ahead = products(*work[i + 1])
        now = (*at, q, da, *score_grads(*at, s, pg))
        if i:
            gather(*late)
        late = now
    gather(*late)
    for g in range(groups):
        dqkv_ref[:, g * LANES : (g + 1) * LANES] = dqt_scr[g * LANES : (g + 1) * LANES, :].T.astype(bf16)
    for c in range(2 * groups):
        dqkv_ref[:, wide + c * LANES : wide + (c + 1) * LANES] = dkv_scr[c].astype(bf16)
    small = None
    for copy in late_copies:
        copy.wait()
    for r in range(n):
        start = pl.multiple_of(jnp.bitwise_xor(me, r) * tok, tok)
        x = x_scr[r].astype(f32)
        part = dot(dqkv_ref[pl.ds(start, tok), :], w_ref[...], NT)
        part_refs[r][...] = part.astype(bf16)
        term = jnp.sum(part * (x * rsq(x)), axis=0, keepdims=True)
        small = term if small is None else small + term
    if not first:
        small = small + old_small_ref[...]
    new_small_ref[...] = small
    new_band_ref[...] = jnp.zeros_like(new_band_ref)
    lines = unshear([acc_scr[h, s] for h in range(heads) for s in range(spans)])
    for h in range(heads):
        for s in range(spans):
            value = lines[h * spans + s][:, :tok]
            if s + 1 < spans:
                value = value + lines[h * spans + s + 1][:, tok:]
            if not first:
                value = value + old_band_ref[h : h + 1, s * tok : (s + 1) * tok]
            new_band_ref[h : h + 1, s * tok : (s + 1) * tok] = value


def qkv_grad_kernel(n, heads, own_rows, first, last, idx_ref, gain_ref, *rest):
    x_refs, rest = rest[:n], rest[n:]
    if last:
        small_ref, band_ref, extra_ref, *rest = rest
    count = 1 + (not first) + 2 * last
    hbms, (out_ref, mark_ref, normed_scr, *rest) = rest[:count], rest[count:]
    mark_ref[...] = jnp.zeros_like(mark_ref)
    copies = [pltpu.make_async_copy(*c) for c in zip(hbms, rest[:count], rest[count:])]
    for copy in copies:
        copy.start()
    dqkv_ref = rest[0]
    if not first:
        old_w_ref = rest[1]
    if last:
        dense_ref, came_ref = rest[count - 2 : count]
    tok = x_refs[0].shape[0]
    for r in range(n):
        start = pl.multiple_of(jnp.bitwise_xor(idx_ref[0], r) * tok, tok)
        x = x_refs[r][...].astype(f32)
        normed_scr[pl.ds(start, tok), :] = (x * rsq(x) * gain_ref[...]).astype(bf16)
    copies[0].wait()
    new_w = dot(normed_scr[...], dqkv_ref[...], TN)
    for copy in copies[1:]:
        copy.wait()
    if not first:
        new_w = new_w + old_w_ref[...].astype(f32)
    if not last:
        out_ref[...] = new_w.astype(bf16)
        return
    pack_grad(heads, new_w, small_ref[...], extra_ref[...], out_ref)
    packed = packed_blocks(heads) * LANES
    width, lanes = out_ref.shape
    span = min(band_ref.shape[1], WINDOW)
    pieces = [band_ref[h : h + 1, c : c + LANES] for h in range(heads) for c in range(0, span, LANES)]
    dense = dense_ref.shape[1]
    out_ref[:, lanes - dense :] = (dense_ref[...].astype(f32) + came_ref[...].astype(f32)).astype(bf16)
    across = (lanes - packed - dense) // LANES
    pieces += [jnp.zeros((1, LANES), f32)] * (own_rows * across - len(pieces))
    whole = jnp.concatenate(
        [jnp.concatenate(pieces[i * across : (i + 1) * across], axis=1) for i in range(own_rows)]
        + [jnp.zeros((-own_rows % 16, across * LANES), f32)][: 1 if own_rows % 16 else 0],
        axis=0,
    ).astype(bf16)
    shape = (width, whole.shape[0])
    row = lax.rem(lax.broadcasted_iota(jnp.int32, shape, 0), jnp.int32(own_rows))
    pick = jnp.where(row == lax.broadcasted_iota(jnp.int32, shape, 1), 1.0, 0.0).astype(bf16)
    out_ref[:, packed : lanes - dense] = dot(pick, whole).astype(bf16)


def head_rows(me, r, part, width, n):
    at = jnp.bitwise_xor(me, r) * part
    if n * part > width:
        at = jnp.minimum(at, width - part)
    return pl.ds(pl.multiple_of(at, HD), part)


def dense_gain(dense_ref):
    width = dense_ref.shape[1] - LANES
    return dense_ref[:, width:].astype(f32).T[LANES - 1 :]


def gates_of(normed, router, routes):
    logits = dot(normed, router)
    lane = lax.broadcasted_iota(jnp.int32, logits.shape, 1)
    route = [lane == routes[:, k : k + 1] for k in range(TOP)]
    chosen = [jnp.sum(jnp.where(r, logits, 0.0), axis=1, keepdims=True) for r in route]
    peak = jnp.maximum(chosen[0], chosen[1])
    powers = [jnp.exp(c - peak) for c in chosen]
    whole = powers[0] + powers[1]
    return route, [v / whole for v in powers]


def mid_kernel(n, first, idx_ref, x_ref, places_ref, *rest):
    att_refs, rest = rest[:n], rest[n:]
    tok, part = att_refs[0].shape
    width = x_ref.shape[-1]
    me = idx_ref[0]
    if first:
        share_refs = rest[:n]
        mixed_ref, rows_ref, dense_hbm, whole_scr, dense_sem = rest[-5:]
        share = share_refs[0].shape[1]
        for r in range(n):
            at = pl.multiple_of(jnp.bitwise_xor(me, r) * share, LANES)
            whole_scr[:, pl.ds(at, share)] = share_refs[r][...]
        dense_ref = whole_scr.at[:, pl.ds(0, dense_hbm.shape[1])]
        dense_copy = pltpu.make_async_copy(dense_ref, dense_hbm, dense_sem)
        dense_copy.start()
    else:
        dense_ref, routes_ref, cot_ref = rest[:3]
        mixed_ref, rows_ref = rest[-2:]
    mixed = x_ref[...].astype(f32)
    for r in range(n):
        at = head_rows(me, r, part, width, n)
        mixed = mixed + dot(att_refs[r][...], dense_ref[at, :width])
    mixed_ref[...] = mixed
    normed = (mixed * rsq(mixed) * dense_gain(dense_ref)).astype(bf16)
    picks = pick_each(places_ref[...], rows_ref.shape[0])
    rows_ref[:, :width] = dot(sum(picks).astype(bf16), normed).astype(bf16)
    if first:
        dense_copy.wait()
    else:
        _, gates = gates_of(normed, dense_ref[:, width:], routes_ref[...])
        up = cot_ref[...].astype(f32)
        rows_ref[:, width:] = sum(
            dot(picks[k].astype(bf16), (gates[k] * up).astype(bf16)) for k in range(TOP)
        ).astype(bf16)


def expert_kernel(raw, capacity, padded, src_ref, pos_ref, idx_ref, x_ref, c_ref, dense_ref, win_ref, wback_ref, *rest):
    if raw:
        out_ref, in_ref, back_ref, acc_scr, grad_scr, *rest = rest
    else:
        old_in_ref, old_back_ref, out_ref, in_keep_ref, in_send_ref, back_keep_ref, back_send_ref = rest[:7]
        acc_scr, grad_scr = rest[7:]
    f = pl.program_id(0)
    width = x_ref.shape[-1]

    @pl.when(f == 0)
    def _():
        acc_scr[...] = jnp.zeros_like(acc_scr)
        if not raw:
            grad_scr[...] = c_ref[...]
            return
        c_scr, ids_scr = rest
        up = -(-capacity // 8) * 8
        same = lax.broadcasted_iota(jnp.int32, (up, LANES), 0) == lax.broadcasted_iota(
            jnp.int32, (up, LANES), 1
        )
        for s in range(c_ref.shape[0] // padded):
            block = c_ref[s * padded : (s + 1) * padded, :].astype(f32)
            c_scr[s * capacity : (s + 1) * capacity, :] = block[:capacity]
            line = block[capacity : capacity + 1, :LANES]
            column = jnp.sum(jnp.where(same, line, 0.0), axis=1, keepdims=True)
            ids_scr[s * capacity : (s + 1) * capacity, 0:1] = column[:capacity]
        ids = ids_scr[:, 0:1].astype(jnp.int32)
        logits = dot(x_ref[...], dense_ref[...])
        lane = lax.broadcasted_iota(jnp.int32, logits.shape, 1)
        own = jnp.sum(jnp.where(lane == idx_ref[1], logits, 0.0), axis=1, keepdims=True)
        other = jnp.sum(jnp.where(lane == ids, logits, 0.0), axis=1, keepdims=True)
        peak = jnp.maximum(own, other)
        own = jnp.exp(own - peak)
        gate = own / (own + jnp.exp(other - peak))
        grad_scr[...] = (gate * c_scr[...]).astype(bf16)

    pre = dot(x_ref[...], win_ref[...])
    c0 = 0.7978845608028654
    square = pre * pre
    t = jnp.tanh(pre * (c0 + (c0 * 0.044715) * square))
    hidden = (0.5 * pre * (1.0 + t)).astype(bf16)
    slope = 0.5 * (1.0 + t) + 0.5 * pre * (1.0 - t * t) * (c0 + (3 * c0 * 0.044715) * square)
    acc_scr[:, :width] += dot(hidden, wback_ref[...])
    pre_grad = (dot(grad_scr[...], wback_ref[...], NT) * slope).astype(bf16)
    acc_scr[:, width:] += dot(pre_grad, win_ref[...], NT)
    grad_in = dot(x_ref[...], pre_grad, TN)
    grad_back = dot(hidden, grad_scr[...], TN)
    if raw:
        in_ref[...] = grad_in.astype(bf16)
        back_ref[...] = grad_back.astype(bf16)
    else:
        grad_in = (grad_in + old_in_ref[...].astype(f32)).astype(bf16)
        grad_back = (grad_back + old_back_ref[...].astype(f32)).astype(bf16)
        half, rows, _ = in_keep_ref.shape
        for b in range(2 * half):
            at = pos_ref[b]
            block = grad_in[b * rows : (b + 1) * rows]

            @pl.when(at < half)
            def _():
                in_keep_ref[at] = block

            @pl.when(at >= half)
            def _():
                in_send_ref[at - half] = block

        @pl.when(f < half)
        def _():
            back_send_ref[...] = grad_back

        @pl.when(f >= half)
        def _():
            back_keep_ref[...] = grad_back

    @pl.when(f == pl.num_programs(0) - 1)
    def _():
        out_ref[...] = acc_scr[...].astype(bf16)


def combine_kernel(n, experts, first, after, idx_ref, back_ref, places_ref, routes_ref, mixed_ref, cot_ref, dense_ref, *rest):
    att_refs, rest = rest[:n], rest[n:]
    if not first:
        old_ref, *rest = rest
    rest = rest[after:]
    out_ref, mg_ref, branch_ref, new_ref, *da_refs = rest
    tok, part = att_refs[0].shape
    width = mixed_ref.shape[-1]
    total = back_ref.shape[0]
    gain = dense_gain(dense_ref)
    mixed = mixed_ref[...]
    rr = rsq(mixed)
    normed = (mixed * rr * gain).astype(bf16)
    router = dense_ref[:, width:]
    route, gates = gates_of(normed, router, routes_ref[...])
    slot = lax.broadcasted_iota(jnp.int32, (tok, total), 1)
    hits = [jnp.where(slot == places_ref[:, k : k + 1], 1.0, 0.0) for k in range(TOP)]
    results = back_ref[:, :width]
    returned = [dot(h.astype(bf16), results) for h in hits]
    moe = gates[0] * returned[0] + gates[1] * returned[1]
    out_ref[...] = (mixed + moe).astype(bf16)
    up = cot_ref[...].astype(f32)
    gate_grad = [jnp.sum(up * v, axis=1, keepdims=True) for v in returned]
    centre = gates[0] * gate_grad[0] + gates[1] * gate_grad[1]
    chosen_grad = [gates[k] * (gate_grad[k] - centre) for k in range(TOP)]
    logit_grad = jnp.where(route[0], chosen_grad[0], 0.0) + jnp.where(route[1], chosen_grad[1], 0.0)
    high = logit_grad.astype(bf16)
    low = (logit_grad - high.astype(f32)).astype(bf16)
    normed_grad = dot((hits[0] + hits[1]).astype(bf16), back_ref[:, width:])
    normed_grad = normed_grad + dot(high, router, NT) + dot(low, router, NT)
    router_grad = dot(normed, high, TN) + dot(normed, low, TN)
    scaled = mixed * rr
    gain_part = jnp.sum(normed_grad * scaled, axis=0, keepdims=True)
    ng = gain * normed_grad
    mixed_grad = up + rr * (ng - scaled * jnp.mean(ng * scaled, axis=-1, keepdims=True))
    mg_ref[...] = mixed_grad
    branch = mixed_grad.astype(bf16)
    gain_col = jnp.broadcast_to(gain_part, (LANES, width)).T
    lane = lax.broadcasted_iota(jnp.int32, gain_col.shape, 1)
    extra = jnp.where(lane == experts, gain_col, router_grad)
    if not first:
        extra = extra + old_ref[...]
    new_ref[...] = extra
    branch_ref[...] = branch
    for r in range(n):
        at = head_rows(idx_ref[0], r, part, width, n)
        da_refs[r][...] = dot(branch, dense_ref[at, :width], NT).astype(bf16)


def dense_grad_kernel(n, micros, idx_ref, *rest):
    keep_ref, send_ref, scr = rest[-3:]
    part = rest[1].shape[1]
    width, half = keep_ref.shape[0], keep_ref.shape[1]
    for r in range(n):
        at = head_rows(idx_ref[0], r, part, width, n)

        def add_grad(at=at, r=r):
            scr[at, :] = sum(
                dot(rest[m * (n + 1) + 1 + r][...], rest[m * (n + 1)][...], TN) for m in range(micros)
            )

        if n * part > width:
            pl.when(jnp.bitwise_xor(idx_ref[0], r) * part < width)(add_grad)
        else:
            add_grad()
    upper = jnp.bitwise_and(idx_ref[0], 1) == 1
    low, high = scr[:, :half], scr[:, half:]
    keep_ref[...] = jnp.where(upper, high, low).astype(bf16)
    send_ref[...] = jnp.where(upper, low, high).astype(bf16)


def token_grad_kernel(count, x_ref, mg_ref, gain_ref, *rest):
    parts, out_ref = rest[:count], rest[-1]
    grad = parts[0][...].astype(f32)
    for p in parts[1:]:
        grad = grad + p[...].astype(f32)
    x = x_ref[...].astype(f32)
    r = rsq(x)
    scaled = x * r
    ng = gain_ref[...] * grad
    out_ref[...] = (
        mg_ref[...] + r * (ng - scaled * jnp.mean(ng * scaled, axis=-1, keepdims=True))
    ).astype(bf16)


def swap(x, axis, by):
    return lax.ppermute(x, axis, [(i, i ^ by) for i in range(lax.axis_size(axis))])


def exchange(x, axes):
    return lax.all_to_all(x, axes, split_axis=0, concat_axis=0, tiled=True)


def bit_reversed(n):
    bits = n.bit_length() - 1
    return [int(format(r, "b").zfill(bits)[::-1], 2) if bits else 0 for r in range(n)]


def add_kernel(*refs):
    count = len(refs) // 4
    for i in range(count):
        total = refs[2 * i][...].astype(f32) + refs[2 * i + 1][...].astype(f32)
        rows = total.shape[1] // 2
        refs[2 * count + 2 * i][...] = total[:, :rows].astype(bf16)
        refs[2 * count + 2 * i + 1][...] = total[:, rows:].astype(bf16)


def halving_start(grads, axis):
    cames = [swap(send, axis, 1) for _, send in grads]
    arrays = []
    specs = []
    outs = []
    out_specs = []
    for (keep, _), came in zip(grads, cames):
        half, (rows, cols) = keep.shape[0] // 2, keep.shape[1:]
        arrays += [keep, came]
        specs += [pl.BlockSpec((half, rows, cols), lambda _: (1, 0, 0))] * 2
        outs += [jax.ShapeDtypeStruct((half, rows // 2, cols), bf16)] * 2
        out_specs += [pl.BlockSpec((half, rows // 2, cols), lambda _: (0, 0, 0))] * 2
    fars = pl.pallas_call(
        add_kernel,
        grid=(1,),
        out_shape=outs,
        in_specs=specs,
        out_specs=out_specs,
        compiler_params=pltpu.CompilerParams(vmem_limit_bytes=60 * MIB),
        name="add",
    )(*arrays)
    pieces = []
    for i, ((keep, _), came) in enumerate(zip(grads, cames)):
        half, rows = keep.shape[0] // 2, keep.shape[1] // 2
        for j, piece in enumerate((slice(0, rows), slice(rows, None))):
            pieces.append(([keep[:half, piece], came[:half, piece]], fars[2 * i + j]))
    return pieces


def halving_end(terms, far, axis):
    by = 2
    while True:
        half = terms[0].shape[0] // 2
        came = swap(far, axis, by)
        terms = terms + [came]
        if not half:
            return sum(t[0].astype(f32) for t in terms), came
        far = sum(t[half:].astype(f32) for t in terms).astype(bf16)
        terms = [t[:half] for t in terms]
        by *= 2


def bits_of(axis):
    return [1 << i for i in range(lax.axis_size(axis).bit_length() - 1)][::-1]


def upper_half(axis, by):
    return lax.rem(lax.div(lax.axis_index(axis), by), 2) == 1


def by_distance(x, axis, after=(), came=None):
    blocks = {0: x}
    by = lax.axis_size(axis) // 2
    if came is not None:
        blocks[by] = gate(came, *after)
        after = ()
        by //= 2
    while by:
        for r in list(blocks):
            blocks[r ^ by] = swap(blocks[r], axis, by)
        by //= 2
        if after and by:
            blocks.update({r: gate(b, *after) for r, b in blocks.items() if r})
            after = ()
    return [blocks[r] for r in range(len(blocks))]


def sum_kernel(count, *refs):
    refs[-1][...] = sum(r[...].astype(f32) for r in refs[:count]).astype(bf16)


def halving_terms(parts, axis, after=lambda: ()):
    terms = {r: [p] for r, p in enumerate(parts)}
    total = parts[0]
    by = 1
    while by < len(parts):
        for r in [r for r in terms if r & by]:
            held = terms.pop(r)
            total = held[0]
            if len(held) > 1:
                (total,) = call(
                    functools.partial(sum_kernel, len(held)),
                    [(total.shape, bf16)],
                    "sum",
                    arrays=held,
                    after=after(),
                )
            terms[r ^ by].append(swap(total, axis, by))
        by *= 2
    return terms[0], total


def shards(
    tokens, doc_lengths, routes, slots, w_qkv, w_out, rel_bias, gain_attn, gain_ffn, w_router, w_in, w_back, cotangent
):
    micros, _, tok, width = tokens.shape
    n = lax.axis_size("dp")
    experts = lax.axis_size("expert")
    me = lax.axis_index("dp")
    my_expert = lax.axis_index("expert")
    reach = min((WINDOW - 2) // tok + 1, n - 1)
    spans = reach + 1
    capacity = (9 * tok * TOP + 8 * experts - 1) // (8 * experts)
    total = experts * capacity
    length = n * tok
    heads = -(-H // n)
    groups = -(-heads // 2)
    part = heads * HD
    wide = groups * LANES
    ff = w_in.shape[2]
    own_rows = w_qkv.shape[0]
    whole_count = n * experts
    both = ("dp", "expert")
    tokens, cotangent = tokens[:, 0], cotangent[:, 0]
    routes, slots = routes[:, 0], slots[:, 0]
    idx = jnp.stack([me, my_expert]).astype(jnp.int32)

    packed = packed_blocks(heads) * LANES
    share = dense_share(n, width)
    (columns,) = call(
        functools.partial(pack_kernel, n),
        [((whole_count, own_rows, packed + share), bf16)],
        "pack",
        arrays=[w_qkv, gain_attn[None], w_out, w_router.T, gain_ffn[None]],
    )
    w_mine = exchange(columns, both).reshape(width, packed + share)

    places = jnp.where(slots >= 0, routes * capacity + slots, total)
    places_row = places.transpose(0, 2, 1)
    padded = -(-(capacity + 1) // 8) * 8
    padded_places = jnp.where(slots[0] >= 0, routes[0] * padded + slots[0], experts * padded)
    (cot_rows,) = call(
        functools.partial(dispatch_kernel, capacity, padded),
        [((experts * padded, width), bf16)],
        "dispatch_cotangent",
        arrays=[padded_places.T, padded_places, routes[0, :, ::-1], (cotangent, 0)],
        after=[columns],
        flops=2 * total * tok * width,
    )

    bias = jnp.pad(rel_bias.astype(f32).T, ((0, heads * n - H), (0, 0)))
    bias = lax.dynamic_slice_in_dim(bias, me * heads, heads, 0)[:, : spans * tok]
    band = jnp.concatenate(
        [
            jnp.full((heads, tok), MASKED, f32),
            bias,
            jnp.full((heads, spans * tok - bias.shape[1]), MASKED, f32),
        ],
        axis=1,
    )
    band = jnp.pad(band, ((0, -heads % 8), (0, 0)))
    (tiles,) = call(
        functools.partial(tiles_kernel, spans, tok),
        [((heads, spans, tok, tok), f32)],
        "bias_tiles",
        arrays=[band],
        after=[columns],
    )
    doc_ends = jnp.cumsum(doc_lengths[:, 0], axis=-1)
    positions = jnp.arange(length, dtype=jnp.int32)
    docs = jnp.sum((doc_ends[:, None, :] <= positions[None, :, None]).astype(jnp.int32), axis=2)
    kdocs, qdocs = docs[:, :, None], docs[:, None, :]

    assert micros == 2
    xs = [by_distance(tokens[0], "dp", [cot_rows, tiles, kdocs])]
    second = swap(gate(tokens[1], tiles), "dp", n // 2)

    cot_rows = gate(cot_rows, w_mine, tiles, xs[0][-1], kdocs, second)
    cot_rows = exchange(cot_rows.reshape(experts, padded, width), "expert").reshape(-1, width)

    att = []
    saved = []
    pair_flops = 2 * heads * LANES * tok * tok * sum(min(j, reach) + 1 for j in range(n))
    w_heads = w_mine
    gain_a = None
    for m in range(micros):
        first = m == 0
        if not first:
            xs.append(by_distance(tokens[1], "dp", [saved[0][1]], second))
        made = call(
            functools.partial(attn_fwd_kernel, n, reach, heads, first),
            [((tok, part), bf16)] * n
            + [((3 * groups, length, LANES), bf16), ((8, length), f32)]
            + ([((width, 3 * wide), bf16), ((1, width), f32)] if first else []),
            "attention_forward",
            smem=[idx],
            arrays=[
                w_heads,
                *([] if first else [gain_a]),
                (kdocs, m),
                (qdocs, m),
                *xs[m],
            ],
            hbm=[tiles],
            hbm_out=[n],
            flops=2 * length * width * 3 * wide + 2 * pair_flops,
            scratch=[
                pltpu.VMEM((wide, length), bf16),
                pltpu.VMEM((wide, length), f32),
                pltpu.VMEM((length, wide), bf16),
                pltpu.VMEM(tiles.shape, f32),
                pltpu.VMEM((3 * groups, length, LANES), bf16),
                pltpu.SemaphoreType.DMA,
                pltpu.SemaphoreType.DMA,
            ],
        )
        att_m, (qkv, lse, *more) = made[:n], made[n:]
        if first:
            w_heads, gain_a = more
        att.append([att_m[0]] + [swap(att_m[r], "dp", r) for r in range(1, n)])
        saved.append((qkv, lse))

    shares = by_distance(w_mine[:, packed:], "dp", [saved[0][1]])
    mixed = []
    arrived = []
    dense = None
    for m in range(micros):
        first = m == 0
        mixed_m, rows, *more = call(
            functools.partial(mid_kernel, n, first),
            [((tok, width), f32), ((total, width if first else 2 * width), bf16)]
            + ([((width, width + LANES), bf16)] if first else []),
            "mix_and_dispatch",
            smem=[idx],
            arrays=[(tokens, m), (places_row, m), *att[m], *(shares if first else [dense, (routes, m), (cotangent, m)])],
            after=[xs[1][-1]] if first else [],
            scratch=[pltpu.VMEM((width, n * share), bf16), pltpu.SemaphoreType.DMA] if first else [],
            hbm_out=[2] if first else [],
            flops=2 * tok * width * width + 2 * total * tok * width,
        )
        if first:
            (dense,) = more
            rows = gate(rows, cot_rows)
        mixed.append(mixed_m)
        arrived.append(exchange(rows.reshape(experts, capacity, -1), "expert").reshape(total, -1))

    cols = ff // n
    reverse = jnp.asarray(bit_reversed(n), jnp.int32)
    pos = reverse[jnp.bitwise_xor(jnp.arange(n, dtype=jnp.int32), me)]
    src = jnp.bitwise_xor(jnp.roll(reverse, -(n // 2)), me)
    whole = lambda shape, c=0: pl.BlockSpec(shape, lambda f, *_, c=c: (0, c))
    in_block = pl.BlockSpec((width, cols), lambda f, src, pos: (0, src[f]))
    back_block = pl.BlockSpec((cols, width), lambda f, src, pos: (src[f], 0))
    half_block = pl.BlockSpec((n // 2, width // n, cols), lambda f, src, pos: (0, 0, src[f]))
    results = []
    grads = []
    for m in range(micros):
        raw = m == 0
        result, *grads = pl.pallas_call(
            functools.partial(expert_kernel, raw, capacity, padded),
            out_shape=[jax.ShapeDtypeStruct((total, 2 * width), bf16)]
            + (
                [jax.ShapeDtypeStruct((width, ff), bf16), jax.ShapeDtypeStruct((ff, width), bf16)]
                if raw
                else [jax.ShapeDtypeStruct((n // 2, width // n, ff), bf16)] * 2
                + [jax.ShapeDtypeStruct((n // 2, cols, width), bf16)] * 2
            ),
            grid_spec=pltpu.PrefetchScalarGridSpec(
                num_scalar_prefetch=2,
                grid=(n,),
                in_specs=[
                    pl.BlockSpec(memory_space=pltpu.SMEM),
                    whole((total, width)),
                    whole(cot_rows.shape) if raw else whole((total, width), 1),
                    whole((width, LANES), width // LANES),
                    pl.BlockSpec((None, width, cols), lambda f, src, pos: (0, 0, src[f])),
                    pl.BlockSpec((None, cols, width), lambda f, src, pos: (0, src[f], 0)),
                ]
                + ([] if raw else [in_block, back_block]),
                out_specs=[whole((total, 2 * width))]
                + (
                    [in_block, back_block]
                    if raw
                    else [
                        half_block,
                        half_block,
                        pl.BlockSpec(
                            (None, cols, width), lambda f, src, pos: (jnp.maximum(f - n // 2, 0), 0, 0)
                        ),
                        pl.BlockSpec(
                            (None, cols, width), lambda f, src, pos: (jnp.minimum(f, n // 2 - 1), 0, 0)
                        ),
                    ]
                ),
                scratch_shapes=[
                    pltpu.VMEM((total, 2 * width), f32),
                    pltpu.VMEM((total, width), bf16),
                ]
                + ([pltpu.VMEM((total, width), f32), pltpu.VMEM((total, LANES), f32)] if raw else []),
            ),
            compiler_params=pltpu.CompilerParams(vmem_limit_bytes=60 * MIB),
            cost_estimate=pl.CostEstimate(
                flops=12 * total * width * ff, transcendentals=total * ff, bytes_accessed=24 * MIB
            ),
            name="expert",
        )(src, pos, idx, arrived[m], cot_rows if raw else arrived[m], dense, w_in, w_back, *grads)
        results.append(result)
    in_keep, in_send, back_keep, back_send = grads
    pieces = halving_start([(in_keep, in_send), (back_keep, back_send)], "dp")
    results[1] = gate(results[1], *[far for _, far in pieces])
    back = [
        exchange(r.reshape(experts, capacity, 2 * width), "expert").reshape(total, 2 * width) for r in results
    ]

    out = token_grad = None
    dense_grad = []
    branches = []
    attn_grad = []
    grad_w = []
    ends = [halving_end(*pieces[0], "dp")]
    across = -(-heads * min(spans * tok, WINDOW) // (own_rows * LANES)) * LANES
    lanes = packed + across + width // 2
    for m in range(micros):
        first, last = m == 0, m == micros - 1
        after = [] if first else [grad_w[0], ends[0][1], ends[1][1], first_sent]
        out, mixed_grad, branch, new_grad, *da = call(
            functools.partial(combine_kernel, n, experts, first, len(after) + (out is not None)),
            [
                ((micros, tok, width), bf16),
                ((tok, width), f32),
                ((tok, width), bf16),
                ((width, LANES), f32),
            ]
            + [((tok, part), bf16)] * n,
            "combine",
            smem=[idx],
            arrays=[
                back[m],
                (places, m),
                (routes, m),
                mixed[m],
                (cotangent, m),
                dense,
                *att[m],
                *dense_grad,
            ],
            after=after,
            flops=6 * total * tok * width + 4 * tok * width * width,
            out_micro=[(0, m, out)],
        )
        dense_grad = [new_grad]
        branches += [branch, *att[m]]
        da = [da[0]] + [swap(da[r], "dp", r) for r in range(1, n)]
        qkv, lse = saved[m]
        after = []
        for terms, far in pieces[1:3] if first else pieces[3:]:
            far = gate(far, *da[1:])
            after.append(far)
            ends.append(halving_end(terms, far, "dp"))
        if not first:
            dense_halves = call(
                functools.partial(dense_grad_kernel, n, micros),
                [((width, width // 2), bf16)] * 2,
                "dense_grad",
                smem=[idx],
                arrays=branches,
                flops=2 * micros * tok * width * width,
                scratch=[pltpu.VMEM((width, width), f32)],
            )
            after += [ends[2][1], dense_halves[1]]
        made = call(
            functools.partial(attn_bwd_kernel, n, reach, heads, first, len(after)),
            [((tok, width), bf16)] * n
            + [((length, 3 * wide), bf16), ((1, width), f32), ((8, spans * tok), f32)],
            "attention_backward",
            smem=[idx],
            arrays=[(kdocs, m), (qdocs, m), qkv, lse, *da, *attn_grad],
            hbm=[tiles, w_heads, *xs[m]],
            after=after,
            flops=2 * length * width * 3 * wide + 5 * pair_flops,
            scratch=[
                pltpu.VMEM((groups, length, LANES), bf16),
                pltpu.VMEM((wide, length), bf16),
                pltpu.VMEM((wide, length), f32),
                pltpu.VMEM((2 * groups, length, LANES), f32),
                pltpu.VMEM((heads, spans, tok, tok), f32),
                pltpu.VMEM(tiles.shape, f32),
                pltpu.VMEM((width, 3 * wide), bf16),
                pltpu.VMEM((n, tok, width), bf16),
            ]
            + [pltpu.SemaphoreType.DMA] * (2 + n),
        )
        parts, (dqkv, *attn_grad) = made[:n], made[n:]
        dense_parts = []
        if last:
            dense_parts = [dense_halves[0], swap(dense_halves[1], "dp", 1)]
        *grad_w, mark = call(
            functools.partial(qkv_grad_kernel, n, heads, own_rows, first, last),
            [((width, lanes), bf16) if last else ((width, 3 * wide), bf16), ((8, LANES), f32)],
            "qkv_grad",
            smem=[idx],
            arrays=[gain_a, *xs[m], *([*attn_grad, *dense_grad] if last else [])],
            hbm=[dqkv, *grad_w, *dense_parts],
            flops=2 * length * width * 3 * wide,
            scratch=[pltpu.VMEM((length, width), bf16)]
            + [pltpu.VMEM(x.shape, bf16) for x in (dqkv, *grad_w, *dense_parts)]
            + [pltpu.SemaphoreType.DMA] * (1 + len(grad_w) + len(dense_parts)),
        )
        summed, sent_last = halving_terms(parts, "dp", lambda: [mark] if last else [])
        if first:
            first_came, first_sent = summed[-1], sent_last
        (token_grad,) = call(
            functools.partial(token_grad_kernel, len(summed)),
            [((micros, tok, width), bf16)],
            "token_grad",
            arrays=[(tokens, m), mixed_grad, gain_a, *summed],
            out_micro=[(0, m, token_grad)],
        )

    message = gate(grad_w[0], ends[3][1], first_came)
    message = exchange(message.reshape(whole_count, own_rows, lanes), both)
    grad_qkv, grad_bias, grad_router, grad_gain_a, grad_gain_f, dense_sum = call(
        functools.partial(finish_kernel, n, across),
        [
            ((own_rows, 3 * width), f32),
            ((H, WINDOW), f32),
            ((experts, own_rows), f32),
            ((1, own_rows), f32),
            ((1, own_rows), f32),
            ((own_rows, width), f32),
        ],
        "finish",
        arrays=[message],
    )
    return (
        out[:, None],
        token_grad[:, None],
        grad_qkv,
        dense_sum,
        grad_bias.T,
        grad_gain_a[0],
        grad_gain_f[0],
        grad_router.T,
        jnp.concatenate([ends[0][0], ends[1][0]])[None],
        jnp.concatenate([ends[2][0], ends[3][0]])[None],
    )


def solution(mesh):
    return jax.shard_map(
        shards,
        mesh=mesh,
        in_specs=(
            P(None, "expert", "dp", None),
            P(None, "expert", None),
            P(None, "expert", "dp", None),
            P(None, "expert", "dp", None),
            P(("dp", "expert"), None),
            P(("dp", "expert"), None),
            P(),
            P(("dp", "expert")),
            P(("dp", "expert")),
            P(("dp", "expert"), None),
            P("expert", None, None),
            P("expert", None, None),
            P(None, "expert", "dp", None),
        ),
        out_specs=(
            P(None, "expert", "dp", None),
            P(None, "expert", "dp", None),
            P(("dp", "expert"), None),
            P(("dp", "expert"), None),
            P(),
            P(("dp", "expert")),
            P(("dp", "expert")),
            P(("dp", "expert"), None),
            P("expert", "dp", None),
            P("expert", "dp", None),
        ),
        check_vma=False,
    )
```
